32 devices in a mesh: gx: 4 (over y, x), gy: 8 (over z, core).
Axes of the slice: x: 2, y: 2, z: 4, core: 2. Of those that a mesh axis runs over, the one named last changes fastest.
Arguments:
- coarse: bfloat16 [12, 64, 256], P(None, ('gx', 'gy')), may hold values from -6 to 6
- weight_one: bfloat16 [3, 3, 12, 64], replicated, may hold values from -0.625 to 0.625
- weight_two: bfloat16 [3, 3, 64, 64], replicated, may hold values from -0.25 to 0.25
- weight_three: bfloat16 [3, 3, 64, 256], replicated, may hold values from -0.25 to 0.25
- weight_four: bfloat16 [3, 3, 64, 256], replicated, may hold values from -0.25 to 0.25
- weight_five: bfloat16 [3, 3, 64, 12], replicated, may hold values from -0.25 to 0.25
- bias_one: float32 [64], replicated, may hold values from -3 to 3
- bias_two: float32 [64], replicated, may hold values from -3 to 3
- bias_three: float32 [256], replicated, may hold values from -3 to 3
- bias_four: float32 [256], replicated, may hold values from -3 to 3
- bias_five: float32 [12], replicated, may hold values from -3 to 3
- cotangent: bfloat16 [12, 256, 1024], P(None, 'gx', 'gy'), may hold values from -6 to 6
Outputs:
- fine: float32 [12, 256, 1024], P(None, 'gx', 'gy')
- grad_w1: float32 [3, 3, 12, 64], replicated
- grad_w2: float32 [3, 3, 64, 64], replicated
- grad_w3: float32 [3, 3, 64, 256], replicated
- grad_w4: float32 [3, 3, 64, 256], replicated
- grad_w5: float32 [3, 3, 64, 12], replicated
- grad_b1: float32 [64], replicated
- grad_b2: float32 [64], replicated
- grad_b3: float32 [256], replicated
- grad_b4: float32 [256], replicated
- grad_b5: float32 [12], replicated
The draws below stay inside these ranges and needn't reach their ends.
All inputs are finite; a program needn't handle non-finite values.
Results may differ from the reference program's by a relative error of at most 0.013.
Values may be sent and summed in bfloat16 or wider, within the bound.
No kernel may reach another device: no remote copies, remote signals or barrier semaphores. Data moves between devices by JAX's collectives and lax.ppermute only.
A program may use at most 128 MiB of HBM per device.

```python
import jax
import jax.numpy as jnp
from jax import lax

CH = 12
C = 64
NX = 64
NY = 256


def level_of(stream_key, extent, cuts, smallest, top_value):
    def one(position, blocks):
        draws = jax.random.uniform(jax.random.fold_in(jax.random.fold_in(stream_key, 6), position), (blocks,), jnp.float32, smallest / len(cuts), top_value / len(cuts))
        return jnp.repeat(jnp.exp(draws), extent[position] // blocks).reshape((-1,) + (1,) * (len(extent) - position - 1))

    factor_of = one(*cuts[0])
    for cut in cuts[1:]:
        factor_of = factor_of * one(*cut)
    return factor_of


def gaussian(stream_key, extent, spread, limit, shards=(), kind=jnp.bfloat16):
    array = jax.random.normal(stream_key, extent, jnp.float32) * spread
    if len(shards) > 0:
        array = level_of(stream_key, extent, shards, -0.22, 0.18) * array
    return jnp.clip(array, min=-limit, max=limit).astype(kind)


def setup_inputs(seed: int = 0) -> dict:
    arg_keys = jax.random.split(jax.random.key(seed), 13)
    return {
        "coarse": gaussian(arg_keys[0], (CH, NX, NY), 1.0, 6.0, ((1, 32),)),
        "weight_one": gaussian(arg_keys[1], (3, 3, CH, C), (9 * CH) ** -0.5, 0.625),
        "weight_two": gaussian(arg_keys[2], (3, 3, C, C), (9 * C) ** -0.5, 0.25),
        "weight_three": gaussian(arg_keys[3], (3, 3, C, 4 * C), (9 * C) ** -0.5, 0.25),
        "weight_four": gaussian(arg_keys[4], (3, 3, C, 4 * C), (9 * C) ** -0.5, 0.25),
        "weight_five": gaussian(arg_keys[5], (3, 3, C, CH), (9 * C) ** -0.5, 0.25),
        "bias_one": gaussian(arg_keys[6], (C,), 0.3, 3.0, (), jnp.float32),
        "bias_two": gaussian(arg_keys[7], (C,), 0.3, 3.0, (), jnp.float32),
        "bias_three": gaussian(arg_keys[8], (4 * C,), 0.3, 3.0, (), jnp.float32),
        "bias_four": gaussian(arg_keys[9], (4 * C,), 0.3, 3.0, (), jnp.float32),
        "bias_five": gaussian(arg_keys[10], (CH,), 0.3, 3.0, (), jnp.float32),
        "cotangent": gaussian(arg_keys[11], (CH, 4 * NX, 4 * NY), 1.0, 6.0, ((1, 4), (2, 8))),
    }


def conv_valid(padded, weight, bias):
    rows = padded.shape[1] - 2
    cols = padded.shape[2] - 2
    values = padded.astype(jnp.float32)
    kernel = weight.astype(jnp.float32)
    total = jnp.zeros((weight.shape[3], rows, cols), jnp.float32) + bias[:, None, None]
    for row_off in range(3):
        for col_off in range(3):
            total = total + jnp.einsum('chw,co->ohw', values[:, row_off:row_off + rows, col_off:col_off + cols], kernel[row_off, col_off])
    return total

def conv_back(padded, weight):
    rows = padded.shape[1] - 2
    cols = padded.shape[2] - 2
    values = padded.astype(jnp.float32)
    kernel = weight.astype(jnp.float32)
    total = jnp.zeros((weight.shape[2], rows, cols), jnp.float32)
    for row_off in range(3):
        for col_off in range(3):
            total = total + jnp.einsum('ohw,co->chw', values[:, 2 - row_off:2 - row_off + rows, 2 - col_off:2 - col_off + cols], kernel[row_off, col_off])
    return total

def weight_grad(padded, grad):
    rows = grad.shape[1]
    cols = grad.shape[2]
    values = padded.astype(jnp.float32)
    grad_f = grad.astype(jnp.float32)
    pieces = []
    for row_off in range(3):
        for col_off in range(3):
            pieces.append(jnp.einsum('chw,ohw->co', values[:, row_off:row_off + rows, col_off:col_off + cols], grad_f))
    stacked = jnp.stack(pieces)
    return stacked.reshape(3, 3, stacked.shape[1], stacked.shape[2])

def squash(value):
    return jnp.tanh(value)

def slopes(act):
    act_f = act.astype(jnp.float32)
    return 1.0 - act_f * act_f

def shuffle(value):
    chans, rows, cols = value.shape
    return value.reshape(chans // 4, 2, 2, rows, cols).transpose(0, 3, 1, 4, 2).reshape(chans // 4, 2 * rows, 2 * cols)

def unshuffle(value):
    chans, rows, cols = value.shape
    return value.reshape(chans, rows // 2, 2, cols // 2, 2).transpose(0, 2, 4, 1, 3).reshape(4 * chans, rows // 2, cols // 2)

def padded_one(value):
    return jnp.pad(value, ((0, 0), (1, 1), (1, 1)))

def reference(coarse, weight_one, weight_two, weight_three, weight_four, weight_five, bias_one, bias_two, bias_three, bias_four, bias_five, cotangent):
    pad_zero = padded_one(coarse)
    act_one = squash(conv_valid(pad_zero, weight_one, bias_one)).astype(jnp.bfloat16)
    pad_one = padded_one(act_one)
    act_two = squash(conv_valid(pad_one, weight_two, bias_two)).astype(jnp.bfloat16)
    pad_two = padded_one(act_two)
    act_three = shuffle(squash(conv_valid(pad_two, weight_three, bias_three))).astype(jnp.bfloat16)
    pad_three = padded_one(act_three)
    act_four = shuffle(squash(conv_valid(pad_three, weight_four, bias_four))).astype(jnp.bfloat16)
    pad_four = padded_one(act_four)
    fine = conv_valid(pad_four, weight_five, bias_five)
    scale = jnp.float32(16 * NX * NY) ** (-0.5)
    grad_w5 = scale * weight_grad(pad_four, cotangent)
    grad_b5 = scale * lax.optimization_barrier(jnp.sum(cotangent.astype(jnp.float32), axis=(1, 2)))
    back_four = unshuffle(conv_back(padded_one(cotangent), weight_five) * slopes(act_four)).astype(jnp.bfloat16)
    grad_w4 = scale * weight_grad(pad_three, back_four)
    grad_b4 = scale * lax.optimization_barrier(jnp.sum(back_four.astype(jnp.float32), axis=(1, 2)))
    back_three = unshuffle(conv_back(padded_one(back_four), weight_four) * slopes(act_three)).astype(jnp.bfloat16)
    grad_w3 = scale * weight_grad(pad_two, back_three)
    grad_b3 = scale * lax.optimization_barrier(jnp.sum(back_three.astype(jnp.float32), axis=(1, 2)))
    back_two = (conv_back(padded_one(back_three), weight_three) * slopes(act_two)).astype(jnp.bfloat16)
    grad_w2 = scale * weight_grad(pad_one, back_two)
    grad_b2 = scale * lax.optimization_barrier(jnp.sum(back_two.astype(jnp.float32), axis=(1, 2)))
    back_one = (conv_back(padded_one(back_two), weight_two) * slopes(act_one)).astype(jnp.bfloat16)
    grad_w1 = scale * weight_grad(pad_zero, back_one)
    grad_b1 = scale * lax.optimization_barrier(jnp.sum(back_one.astype(jnp.float32), axis=(1, 2)))
    return (fine, grad_w1, grad_w2, grad_w3, grad_w4, grad_w5, grad_b1, grad_b2, grad_b3, grad_b4, grad_b5)
```

```python
import jax
import jax.numpy as jnp
import numpy as np
from jax import lax
from jax.experimental import pallas as pl
from jax.experimental.pallas import tpu as pltpu
from jax.sharding import PartitionSpec as P

BF = jnp.bfloat16
F32 = jnp.float32

ROWS, COLS, PITCH, CHUNKS = 16, 32, 48, 32
CELLS = PITCH * CHUNKS
OWN = PITCH * 8
HALO = 6
FINE_HALO = 12
PACKED = 1408


def dotn(left, right):
    return lax.dot_general(left, right, (((1,), (0,)), ((), ())), preferred_element_type=F32)


def dott(left, right):
    return lax.dot_general(left, right, (((1,), (1,)), ((), ())), preferred_element_type=F32)


def take(ref, start, count, low=0, high=None):
    high = ref.shape[1] if high is None else high
    return ref[pl.ds(pl.multiple_of(start, 16), count), low:high]


def taps(ref, start, count):
    return jnp.concatenate([take(ref, start + d, count) for d in (-PITCH, 0, PITCH)], axis=1)


def own(ref, low, high, row=0):
    block = ref[OWN + PITCH * row : OWN + PITCH * (row + ROWS), low:high]
    return block.reshape(ROWS, PITCH, high - low)[:, 16:48, :].reshape(ROWS * COLS, high - low)


def roll(value, by):
    return pltpu.roll(value, by % value.shape[0], 0)


def lane_roll(value, by):
    return pltpu.roll(value, by % value.shape[1], 1)


def slope(act):
    act = act.astype(F32)
    return 1.0 - act * act


def split_dot(value, perm):
    high = value.astype(BF)
    rest = value - high.astype(F32)
    middle = rest.astype(BF)
    low = (rest - middle.astype(F32)).astype(BF)
    return (dotn(low, perm) + dotn(middle, perm)) + dotn(high, perm)


def body(
    extent,
    scale,
    pos_ref,
    dx_ref,
    dc_ref,
    s0_ref,
    s5_ref,
    e_ref,
    perm3_ref,
    perm4_ref,
    w1_ref,
    w2_ref,
    w3_ref,
    w4_ref,
    w5_ref,
    bias_ref,
    fine_ref,
    g_ref,
    mask,
    x0,
    x1,
    x2,
    x3,
    a1,
    a2,
    a3,
    a4,
    c5,
    b4,
    b3,
    b2,
    b1,
    k2,
    k3,
    k4,
    k5,
    k5s,
    r5,
    r4,
    r3,
    r2,
):
    low_half = lax.broadcasted_iota(jnp.int32, (1, 128), 1) < 64

    w3p = dotn(w3_ref[...], perm3_ref[...]).astype(BF)
    w4p = dotn(w4_ref[...], perm4_ref[...]).astype(BF)
    for ref in (k2, k3, k4, k5, k5s, r4, r3, r2):
        ref[...] = jnp.zeros(ref.shape, BF)
    for r in range(3):
        part = w2_ref[r * 192 : (r + 1) * 192, :]
        k2[r * 256 : r * 256 + 192, :] = jnp.concatenate([part, part], axis=1)
        k3[r * 256 : r * 256 + 192, :] = w3p[r * 192 : (r + 1) * 192, :]
        for q in range(2):
            k4[r * 256 + q * 64 : r * 256 + q * 64 + 192, q * 256 : (q + 1) * 256] = w4p[
                r * 192 : (r + 1) * 192, :
            ]
        for s in range(3):
            t = 2 - r
            tap = (3 * r + s) * 64
            r3[s * 64 : (s + 1) * 64, t * 256 : (t + 1) * 256] = w3p[tap : tap + 64, :]
            r2[s * 64 : (s + 1) * 64, t * 128 : t * 128 + 64] = w2_ref[tap : tap + 64, :]
            if s == 2:
                r3[192:256, t * 256 : (t + 1) * 256] = w3p[tap : tap + 64, :]
                r2[192:256, t * 128 : t * 128 + 64] = w2_ref[tap : tap + 64, :]
            block = w4p[tap : tap + 64, :]
            for q in range(2):
                for q_src in range(2):
                    at = t * 512 + q_src * 256
                    if q - q_src + 1 == s:
                        r4[(1 - q) * 64 : (2 - q) * 64, at : at + 256] = block
                    if q_src == 1 - q and s == 2 - 2 * q:
                        r4[128 + (1 - q) * 64 : 128 + (2 - q) * 64, at : at + 256] = block
    w5 = [w5_ref[s].astype(F32) for s in range(3)]
    empty = jnp.zeros((64, 64), BF)
    for t in range(6):
        rows = [lane_roll(w5[s], 16 * (t - 2)).astype(BF)[:, :64] for s in range(3)]
        at = 64 if t == 0 else (1536 if t == 5 else 512 + ((t - 1) // 2) * 512 + ((t - 1) % 2) * 64)
        side = 64 if t == 0 else (384 if t == 5 else 128 + ((t - 1) // 2) * 128 + ((t - 1) % 2) * 64)
        for src in range(4):
            k5[at + src * 128 : at + src * 128 + 64, :] = jnp.concatenate(
                [rows[src - q + 1] if 0 <= src - q + 1 <= 2 else empty for q in range(4)], axis=1
            )
        k5s[side : side + 64, :] = jnp.concatenate([rows[0], empty], axis=1)
        k5s[512 + side : 512 + side + 64, :] = jnp.concatenate([empty, rows[2]], axis=1)
    for p in range(4):
        for v in range(3):
            r5[p * 64 : (p + 1) * 64, v * 128 : (v + 1) * 128] = lane_roll(w5[2 - v], 16 * p).astype(BF)

    row0 = pos_ref[0]
    col0 = pos_ref[1]
    m = lax.broadcasted_iota(jnp.int32, (PITCH, 128), 0)
    col = col0 + jnp.where(m < 8, m + 32, m - 16)
    col_ok = jnp.logical_and(col >= 0, col < extent[1])

    def mask_chunk(k, _):
        row = row0 + jnp.where(m < 8, k - 9, k - 8)
        ok = jnp.logical_and(col_ok, jnp.logical_and(row >= 0, row < extent[0]))
        mask[pl.ds(pl.multiple_of(k * PITCH, 16), PITCH), :] = jnp.where(ok, 1.0, 0.0)
        return 0

    lax.fori_loop(0, CHUNKS, mask_chunk, 0)

    for ref, first, last in (
        (x0, 2, 32),
        (x1, 3, 30),
        (x2, 4, 29),
        (x3, 5, 29),
        (a4, 5, 29),
        (c5, 5, 29),
        (b4, 5, 29),
        (b3, 6, 27),
        (b2, 7, 27),
    ):
        ref[0 : first * PITCH, :] = jnp.zeros((first * PITCH, ref.shape[1]), BF)
        if last < CHUNKS:
            count = CELLS - last * PITCH
            ref[last * PITCH :, :] = jnp.zeros((count, ref.shape[1]), BF)

    def coarse_chunk(k, _):
        lines = dx_ref[pl.ds(k - 2, 3)].reshape(48, 64)
        lines = jnp.concatenate([lines, jnp.zeros((80, 64), BF)], axis=0)
        moved = dott(s0_ref[...], lines).astype(BF)
        for s in range(3):
            x0[pl.ds(pl.multiple_of(k * PITCH, 16), PITCH), s * 128 : (s + 1) * 128] = moved[
                s * PITCH : (s + 1) * PITCH, :
            ]
        return 0

    lax.fori_loop(2, 32, coarse_chunk, 0)

    def cot_chunk(k, _):
        lines = dc_ref[pl.ds(4 * (k - 5), 6)].reshape(96, 160)
        lines = jnp.concatenate([lines, jnp.zeros((32, 160), BF)], axis=0)
        moved = dott(s5_ref[...], lines).astype(BF)
        for u in range(6):
            c5[pl.ds(pl.multiple_of(k * PITCH, 16), PITCH), u * 128 : (u + 1) * 128] = moved[
                u * PITCH : (u + 1) * PITCH, :
            ]
        return 0

    lax.fori_loop(5, 29, cot_chunk, 0)

    def blocks(first, chunks_each, count, work):
        size = chunks_each * PITCH

        def step(n, _):
            start = pl.multiple_of(first * PITCH + n * size, 16)
            work(start, size)
            return 0

        lax.fori_loop(0, count, step, 0)

    def put(ref, start, size, value, low, high):
        ref[pl.ds(start, size), low:high] = value.astype(BF)

    def narrow(src, weight, bias_at, variants, act):
        def work(start, size):
            wide = size + 32
            z = dotn(taps(src, start - 16, wide), weight[...])
            z = jnp.tanh(z + bias_ref[bias_at : bias_at + 1, 0:128])
            z = z * take(mask, start - 16, wide)
            inner = slice(16, 16 + size)
            left = jnp.where(low_half, roll(z, 1), z)
            put(variants, start, size, left[inner], 0, 128)
            put(variants, start, size, roll(z, -1)[inner], 128, 256)
            put(act, start, size, z[inner], 0, 128)

        return work

    def conv_one(start, size):
        wide = size + 32
        z = dotn(take(x0, start - 16, wide), w1_ref[...])
        z = jnp.tanh(z + bias_ref[0:1, 0:128]) * take(mask, start - 16, wide)
        inner = slice(16, 16 + size)
        left = jnp.where(low_half, roll(z, 1), z)
        put(x1, start, size, left[inner], 0, 128)
        put(x1, start, size, roll(z, -1)[inner], 128, 256)
        put(a1, start, size, z[inner], 0, 128)

    blocks(3, 9, 3, conv_one)
    blocks(4, 5, 5, narrow(x1, k2, 1, x2, a2))

    def conv_three(start, size):
        wide = size + 32
        z = dotn(taps(x2, start - 16, wide), k3[...])
        z = jnp.tanh(z + bias_ref[2:3, 0:256])
        ok = take(mask, start - 16, wide)
        inner = slice(16, 16 + size)
        for p in range(2):
            half = z[:, p * 128 : (p + 1) * 128] * ok
            left = jnp.where(low_half, roll(half, 1), half)
            right = jnp.where(low_half, half, roll(half, -1))
            put(x3, start, size, left[inner], p * 256, p * 256 + 128)
            put(x3, start, size, right[inner], p * 256 + 128, p * 256 + 256)
            put(a3, start, size, half[inner], p * 128, p * 128 + 128)

    blocks(5, 8, 3, conv_three)

    def row_of(t):
        return t % 2, PITCH * (t // 2)

    def conv_four(start, size):
        ok = take(mask, start, size)
        for p in range(2):
            lines = []
            for r in range(3):
                phase, by = row_of(p + r - 1)
                lines.append(take(x3, start + by, size, phase * 256, phase * 256 + 256))
            z = dotn(jnp.concatenate(lines, axis=1), k4[...])
            z = jnp.tanh(z + bias_ref[3:4, 0:512])
            for q in range(4):
                put(a4, start, size, z[:, q * 128 : (q + 1) * 128] * ok, p * 512 + q * 128, p * 512 + q * 128 + 128)

    blocks(5, 6, 4, conv_four)

    def conv_five(start, size):
        wide = size + 32
        at = start - 16
        above = take(a4, at - PITCH, wide, 512, 1024)
        here = take(a4, at, wide)
        below = take(a4, at + PITCH, wide, 0, 512)
        z = dotn(jnp.concatenate([above, here, below], axis=1), k5[...])
        side = jnp.concatenate(
            [
                above[:, 384:512],
                here[:, 384:512],
                here[:, 896:1024],
                below[:, 384:512],
                above[:, 0:128],
                here[:, 0:128],
                here[:, 512:640],
                below[:, 0:128],
            ],
            axis=1,
        )
        side = dotn(side, k5s[...])
        left = z[:, 0:128] + jnp.where(low_half, roll(side, 1), 0.0)
        right = z[:, 128:256] + jnp.where(low_half, 0.0, roll(side, -1))
        z = jnp.concatenate([left, right], axis=1) + bias_ref[4:5, 0:256]
        line = lax.div(start - OWN, PITCH)
        for n in range(size // PITCH):
            cells = z[16 + n * PITCH + 16 : 16 + n * PITCH + 48, :]
            stack = jnp.concatenate([cells[:, q * 64 : (q + 1) * 64] for q in range(4)], axis=0)
            stack = stack.T
            high = stack.astype(BF)
            low = (stack - high.astype(F32)).astype(BF)
            done = dotn(low, e_ref[...]) + dotn(high, e_ref[...])
            fine_ref[pl.ds(4 * (line + n), 4)] = done.reshape(4, 16, 128)

    blocks(8, 8, 2, conv_five)

    def back_four(start, size):
        ok = take(mask, start, size)
        for q in range(4):
            z = dott(take(c5, start, size, q * 128, q * 128 + 384), r5[...])
            for p in range(2):
                at = p * 512 + q * 128
                z_p = z[:, p * 128 : (p + 1) * 128] * ok
                put(b4, start, size, z_p * slope(take(a4, start, size, at, at + 128)), at, at + 128)

    blocks(5, 6, 4, back_four)

    def back_three(start, size):
        wide = size + 32
        ok = take(mask, start, size)
        inner = slice(16, 16 + size)
        for p in range(2):
            lines = []
            for t in range(3):
                phase, by = row_of(p + t - 1)
                lines.append(take(b4, start - 16 + by, wide, phase * 512, phase * 512 + 512))
            z = dott(jnp.concatenate(lines, axis=1), r4[...])
            moved = jnp.where(low_half, roll(z[:, 128:256], -1), roll(z[:, 128:256], 1))
            z = (z[:, 0:128] + moved)[inner] * ok
            at = p * 128
            put(b3, start, size, z * slope(take(a3, start, size, at, at + 128)), at, at + 128)

    blocks(6, 7, 3, back_three)

    def back_narrow(src, weight, act, out):
        def work(start, size):
            wide = size + 32
            z = dott(taps(src, start - 16, wide), weight[...])
            pair = jnp.where(low_half, roll(z[:, 0:128], -1), z[:, 0:128])
            z = pair + lane_roll(pair, 64) + roll(z[:, 128:256], 1)
            z = z[16 : 16 + size] * take(mask, start, size)
            put(out, start, size, z * slope(take(act, start, size)), 0, 128)

        return work

    blocks(7, 5, 4, back_narrow(b3, r3, a2, b2))
    blocks(8, 6, 3, back_narrow(b2, r2, a1, b1))

    g_ref[...] = jnp.zeros(g_ref.shape, F32)

    back = own(b4, 0, 1024)
    sums4 = jnp.sum(back.astype(F32), axis=0, keepdims=True)
    back = back.T
    for r in range(3):
        total = None
        for p in range(2):
            phase, by = row_of(p + r - 1)
            field = own(x3, phase * 256, phase * 256 + 256, by // PITCH)
            term = dotn(back[p * 512 : (p + 1) * 512, :], field)
            total = term if total is None else total + term
        total = total[0:256, 0:192] + total[256:512, 64:256]
        g_ref[r * 192 : (r + 1) * 192, :] = split_dot(total.T * scale, perm4_ref[...].T)
    sums4 = sums4[:, 0:512] + sums4[:, 512:1024]
    sums4 = sums4[:, 0:256] + sums4[:, 256:512]

    back = own(b3, 0, 256)
    sums3 = jnp.sum(back.astype(F32), axis=0, keepdims=True)
    back = back.T
    for r in range(3):
        total = dotn(back, own(x2, 0, 256, r - 1))[:, 0:192]
        g_ref[576 + r * 192 : 576 + (r + 1) * 192, :] = split_dot(total.T * scale, perm3_ref[...].T)

    back = own(b2, 0, 128)
    sums2 = jnp.sum(back.astype(F32), axis=0, keepdims=True)
    back = back.T
    for r in range(3):
        total = dotn(back[0:64, :], own(x1, 0, 256, r - 1))
        g_ref[1152:1344, r * 64 : (r + 1) * 64] = total[:, 0:192].T * scale

    back = own(b1, 0, 128)
    sums1 = jnp.sum(back.astype(F32), axis=0, keepdims=True)
    back = back.T
    total = dotn(back[0:64, :], own(x0, 0, 384)).T * scale
    for s in range(3):
        g_ref[1152 + s * 48 : 1152 + (s + 1) * 48, 192:256] = total[s * 128 : s * 128 + 48, :]

    cot = own(c5, 0, 768)
    sums5 = jnp.sum(cot.astype(F32), axis=0, keepdims=True)
    cot = cot.T
    total = None
    for q in range(4):
        field = jnp.concatenate(
            [own(a4, q * 128, q * 128 + 128), own(a4, 512 + q * 128, 640 + q * 128)], axis=1
        )
        term = dotn(cot[q * 128 : q * 128 + 384, :], field)
        total = term if total is None else total + term
    total = total * scale
    for r in range(3):
        for s in range(3):
            sum_p = None
            for p in range(4):
                at = (2 - s) * 128 + (p + 2 - r) * 16
                term = total[at : at + 16, p * 64 : (p + 1) * 64]
                sum_p = term if sum_p is None else sum_p + term
            g_ref[1344 + s * 16 : 1344 + (s + 1) * 16, r * 64 : (r + 1) * 64] = sum_p

    sums5 = sums5[:, 128:256] + sums5[:, 256:384] + sums5[:, 384:512] + sums5[:, 512:640]
    five = sums5
    for t in range(1, 4):
        five = five + lane_roll(sums5, -16 * t)
    pad = jnp.zeros((1, 128), F32)
    biases = [
        sums4,
        sums3,
        jnp.concatenate([sums2, sums1], axis=1),
        jnp.concatenate([five, pad], axis=1),
    ]
    biases = [value * scale for value in biases]
    biases[0] = split_dot(jnp.broadcast_to(biases[0], (8, 256)), perm4_ref[...].T)[0:1]
    biases[1] = split_dot(jnp.broadcast_to(biases[1], (8, 256)), perm3_ref[...].T)[0:1]
    for n, value in enumerate(biases):
        high = value.astype(BF).astype(F32)
        g_ref[1392 + 2 * n : 1393 + 2 * n, :] = high
        g_ref[1393 + 2 * n : 1394 + 2 * n, :] = value - high


def selections():
    s0 = np.zeros((3, PITCH, 64), np.float32)
    s5 = np.zeros((6, PITCH, 160), np.float32)
    for m in range(PITCH):
        for s in range(3):
            s0[s, m, m + s + (1 if m < 8 else 9)] = 1
        for u in range(6):
            if m < 3:
                s5[u, m, 4 * m + u + 1] = 1
            elif m >= 13:
                s5[u, m, 4 * m + u - 35] = 1
    spread = np.zeros((4, COLS, 128), np.float32)
    for q in range(4):
        for j in range(COLS):
            spread[q, j, 4 * j + q] = 1
    perm3 = np.zeros((256, 256), np.float32)
    perm4 = np.zeros((256, 256), np.float32)
    for p in range(2):
        for q in range(2):
            for c in range(64):
                perm3[4 * c + 2 * p + q, p * 128 + (1 - q) * 64 + c] = 1
                perm4[4 * c + 2 * p + q, q * 128 + p * 64 + c] = 1
    arrays = (s0.reshape(144, 64), s5.reshape(288, 160), spread.reshape(128, 128), perm3, perm4)
    return tuple(jnp.asarray(a, BF) for a in arrays)


def pairs(count, by):
    return [(i, i + by) for i in range(count) if 0 <= i + by < count]


def with_halos(coarse, cotangent):
    gx, gy = lax.axis_size("gx"), lax.axis_size("gy")
    each = coarse.shape[1]
    cols = coarse.shape[2] // gy
    wide = cols + 2 * HALO
    padded = jnp.pad(coarse, ((0, 0), (0, 0), (HALO, HALO)))
    pieces = jnp.stack([padded[:, :, g * cols : g * cols + wide] for g in range(gy)])
    got = lax.all_to_all(pieces.transpose(0, 2, 1, 3), "gy", 0, 0, tiled=True)
    got = got.reshape(gy * each, coarse.shape[0], wide)
    cot = cotangent.transpose(1, 0, 2)
    n = FINE_HALO
    left = lax.ppermute(cot[:, :, -n:], "gy", pairs(gy, 1))
    right = lax.ppermute(cot[:, :, :n], "gy", pairs(gy, -1))
    cot = jnp.concatenate([left, cot, right], axis=2)
    full = jnp.pad(got, ((0, 0), (0, 0), (0, cot.shape[2] - wide)))
    above = lax.ppermute(jnp.concatenate([full[-HALO:], cot[-n:]]), "gx", pairs(gx, 1))
    below = lax.ppermute(jnp.concatenate([full[:HALO], cot[:n]]), "gx", pairs(gx, -1))
    coarse_all = jnp.concatenate([above[:HALO, :, :wide], got, below[:HALO, :, :wide]])
    cot_all = jnp.concatenate([above[HALO:], cot, below[HALO:]])

    def rows(value, low, high):
        return jnp.pad(value, ((low, high), (0, 4), (0, 0)))

    def gap(value, count):
        return jnp.zeros(value.shape[:2] + (count,), BF)

    here, before = rows(coarse_all, 1, 3), rows(coarse_all, 2, 2)
    lines0 = jnp.concatenate([before[:, :, 36:44], gap(before, 12), here], axis=2)
    here, before = rows(cot_all, 1, 9), rows(cot_all, 5, 5)
    lines5 = jnp.concatenate([before[:, :, 138:152], gap(before, 4), here[:, :, :142]], axis=2)
    return lines0, lines5


def part(value, at, count):
    return lax.dynamic_slice_in_dim(value, at * count, count, 0)


def joined(bit, mine, other):
    return jnp.where(
        bit == 0, jnp.concatenate([mine, other]), jnp.concatenate([other, mine])
    )


def total_over_all(value):
    gx, gy = lax.axis_size("gx"), lax.axis_size("gy")
    at_x, at_y = lax.axis_index("gx"), lax.axis_index("gy")

    def swap(block, axis, flip):
        count = lax.axis_size(axis)
        return lax.ppermute(block, axis, [(i, i ^ flip) for i in range(count)])

    core = at_y % 2
    half = value.shape[0] // 2
    other = swap(part(value, 1 - core, half).astype(BF), "gy", 1)
    value = part(value, core, half) + other.astype(F32)
    bits = list(range(gx.bit_length() - 1))
    orders = [bits, bits[::-1]]
    halves = [value[: half // 2], value[half // 2 :]]
    for step in range(len(bits)):
        sent = []
        for order, block in zip(orders, halves):
            bit = (at_x >> order[step]) & 1
            size = block.shape[0] // 2
            sent.append(swap(part(block, 1 - bit, size).astype(BF), "gx", 1 << order[step]))
        for n, order in enumerate(orders):
            bit = (at_x >> order[step]) & 1
            size = halves[n].shape[0] // 2
            halves[n] = part(halves[n], bit, size) + sent[n].astype(F32)
    size = halves[0].shape[0]
    block = jnp.concatenate(halves).astype(BF)
    terms = [block] + [swap(block, "gy", 2 * d) for d in range(1, gy // 2)]
    terms = [term.astype(F32) for term in terms]
    while len(terms) > 1:
        terms = [terms[n] + terms[n + 1] for n in range(0, len(terms), 2)]
    block = terms[0].astype(BF)
    halves = [block[:size], block[size:]]
    for step in reversed(range(len(bits))):
        sent = [swap(b, "gx", 1 << order[step]) for order, b in zip(orders, halves)]
        halves = [
            joined((at_x >> order[step]) & 1, b, other)
            for order, b, other in zip(orders, halves, sent)
        ]
    value = jnp.concatenate(halves)
    return joined(core, value, swap(value, "gy", 1)).astype(F32)


def local(
    coarse,
    weight_one,
    weight_two,
    weight_three,
    weight_four,
    weight_five,
    bias_one,
    bias_two,
    bias_three,
    bias_four,
    bias_five,
    cotangent,
):
    gx, gy = lax.axis_size("gx"), lax.axis_size("gy")
    rows = coarse.shape[1] * gy
    cols = coarse.shape[2] // gy
    assert (rows, cols) == (ROWS, COLS)
    lines0, lines5 = with_halos(coarse, cotangent)
    one = jnp.pad(weight_one.transpose(1, 0, 2, 3), ((0, 0), (0, 0), (0, 4), (0, 0)))
    one = jnp.pad(one.reshape(3, 48, 64), ((0, 0), (0, 80), (0, 0))).reshape(384, 64)
    one = jnp.concatenate([one, one], axis=1)
    five = jnp.pad(weight_five[::-1], ((0, 0), (0, 0), (0, 0), (0, 4)))
    five = five.transpose(1, 2, 0, 3).reshape(3, 64, 48)
    five = jnp.pad(five, ((0, 0), (0, 0), (0, 80)))
    three = bias_three.reshape(64, 2, 2)[:, :, ::-1].transpose(1, 2, 0).reshape(256)
    four = bias_four.reshape(64, 2, 2).transpose(2, 1, 0).reshape(256)
    biases = jnp.stack(
        [
            jnp.tile(bias_one, 8),
            jnp.tile(bias_two, 8),
            jnp.tile(three, 2),
            jnp.tile(four, 2),
            jnp.tile(jnp.pad(bias_five, (0, 4)), 32),
        ]
    )
    pos = jnp.stack([lax.axis_index("gx") * rows, lax.axis_index("gy") * cols]).astype(jnp.int32)
    extent = (rows * gx, cols * gy)
    scale = float((16 * extent[0] * extent[1]) ** -0.5)
    s0, s5, spread, perm3, perm4 = selections()

    def buf(width, kind=BF):
        return pltpu.VMEM((CELLS, width), kind)

    vmem = pl.BlockSpec(memory_space=pltpu.VMEM)
    fine, grads = pl.pallas_call(
        lambda *refs: body(extent, scale, *refs),
        out_shape=(
            jax.ShapeDtypeStruct((4 * rows, 16, 4 * cols), F32),
            jax.ShapeDtypeStruct((PACKED, 256), F32),
        ),
        in_specs=[pl.BlockSpec(memory_space=pltpu.SMEM)] + [vmem] * 13,
        out_specs=(vmem, vmem),
        scratch_shapes=[
            buf(128, F32),
            buf(384),
            buf(256),
            buf(256),
            buf(512),
            buf(128),
            buf(128),
            buf(256),
            buf(1024),
            buf(768),
            buf(1024),
            buf(256),
            buf(128),
            buf(128),
            pltpu.VMEM((768, 128), BF),
            pltpu.VMEM((768, 256), BF),
            pltpu.VMEM((768, 512), BF),
            pltpu.VMEM((2048, 256), BF),
            pltpu.VMEM((1024, 128), BF),
            pltpu.VMEM((256, 384), BF),
            pltpu.VMEM((256, 1536), BF),
            pltpu.VMEM((256, 768), BF),
            pltpu.VMEM((256, 384), BF),
        ],
        compiler_params=pltpu.CompilerParams(vmem_limit_bytes=56 * 1024 * 1024),
    )(
        pos,
        lines0,
        lines5,
        s0,
        s5,
        spread,
        perm3,
        perm4,
        one,
        weight_two.reshape(576, 64),
        weight_three.reshape(576, 256),
        weight_four.reshape(576, 256),
        five,
        biases,
    )
    fine = fine.transpose(1, 0, 2)[: cotangent.shape[0]]
    grads = total_over_all(grads)
    chans = coarse.shape[0]
    g4 = grads[0:576].reshape(3, 3, 64, 256)
    g3 = grads[576:1152].reshape(3, 3, 64, 256)
    g2 = grads[1152:1344, 0:192].reshape(192, 3, 64).transpose(1, 0, 2).reshape(3, 3, 64, 64)
    g1 = grads[1152:1296, 192:256].reshape(3, 3, 16, 64).transpose(1, 0, 2, 3)[:, :, :chans]
    g5 = grads[1344:1392, 0:192].reshape(3, 16, 3, 64).transpose(2, 0, 3, 1)[:, :, :, :chans]
    sums = grads[1392:1400].reshape(4, 2, 256).sum(axis=1)
    return (
        fine,
        g1,
        g2,
        g3,
        g4,
        g5,
        sums[2, 128:192],
        sums[2, 0:64],
        sums[1],
        sums[0],
        sums[3, 16 : 16 + chans],
    )


def solution(mesh):
    in_specs = (
        P(None, ("gx", "gy"), None),
        P(),
        P(),
        P(),
        P(),
        P(),
        P(),
        P(),
        P(),
        P(),
        P(),
        P(None, "gx", "gy"),
    )
    out_specs = (P(None, "gx", "gy"), P(), P(), P(), P(), P(), P(), P(), P(), P(), P())
    return jax.shard_map(local, mesh=mesh, in_specs=in_specs, out_specs=out_specs, check_vma=False)
```

```python
import jax
import jax.numpy as jnp
from jax import lax
from jax.experimental import pallas as pl
from jax.experimental.pallas import tpu as pltpu
from jax.sharding import PartitionSpec as P

BF = jnp.bfloat16
F32 = jnp.float32

ROWS, COLS, PITCH, CHUNKS = 16, 32, 48, 32
CELLS = PITCH * CHUNKS
OWN = PITCH * 8
HALO = 6
FINE_HALO = 12
PACKED = 1408
GROUP0, GROUP5 = 6, 6
N1, N2, N3, N4 = 3, 5, 3, 4
M4, M3, M2, M1 = 4, 3, 4, 3
LIMIT = 12


def dotn(left, right):
    return lax.dot_general(left, right, (((1,), (0,)), ((), ())), preferred_element_type=F32)


def dott(left, right):
    return lax.dot_general(left, right, (((1,), (1,)), ((), ())), preferred_element_type=F32)


def take(ref, start, count, low=0, high=None):
    high = ref.shape[1] if high is None else high
    if not isinstance(start, int):
        start = pl.multiple_of(start, 16)
    return ref[pl.ds(start, count), low:high]


def taps(ref, start, count):
    return jnp.concatenate([take(ref, start + d, count) for d in (-PITCH, 0, PITCH)], axis=1)


def own(ref, low, high, row=0):
    block = ref[OWN + PITCH * row : OWN + PITCH * (row + ROWS), low:high]
    return block.reshape(ROWS, PITCH, high - low)[:, 16:48, :].reshape(ROWS * COLS, high - low)


def roll(value, by):
    return pltpu.roll(value, by % value.shape[0], 0)


def lane_roll(value, by):
    return pltpu.roll(value, by % value.shape[1], 1)


def grouped(first, last, group, work):
    def step(n, _):
        for k in range(group):
            work(first + n * group + k)
        return 0

    lax.fori_loop(0, (last - first) // group, step, 0)


def blocks(first, chunks_each, count, work):
    size = chunks_each * PITCH
    if count == 1:
        work(first * PITCH, size)
        return

    def step(n, _):
        work(pl.multiple_of(first * PITCH + n * size, 16), size)
        return 0

    lax.fori_loop(0, count, step, 0)


def clear_margins(fields):
    for ref, first, last in fields:
        ref[0 : first * PITCH, :] = jnp.zeros((first * PITCH, ref.shape[1]), BF)
        if last < CHUNKS:
            ref[last * PITCH :, :] = jnp.zeros((CELLS - last * PITCH, ref.shape[1]), BF)


def put(ref, start, size, value, low, high):
    ref[pl.ds(start, size), low:high] = value.astype(BF)


def row_of(t):
    return t % 2, PITCH * (t // 2)


def low_half():
    return lax.broadcasted_iota(jnp.int32, (1, 128), 1) < 64


def slope(act):
    act = act.astype(F32)
    return 1.0 - act * act


def split_dot(value, perm):
    high = value.astype(BF)
    rest = value - high.astype(F32)
    middle = rest.astype(BF)
    low = (rest - middle.astype(F32)).astype(BF)
    return (dotn(low, perm) + dotn(middle, perm)) + dotn(high, perm)


def grid(rows, cols):
    return tuple(lax.broadcasted_iota(jnp.int32, (rows, cols), n) for n in (0, 1))


def one_hot(chosen):
    return jnp.where(chosen, 1.0, 0.0).astype(BF)


def select(s0_ref, s5_ref, e_ref, turn3_ref, turn4_ref):
    m, lane = grid(PITCH, 64)
    for s in range(3):
        s0_ref[s * PITCH : (s + 1) * PITCH, :] = one_hot(lane == m + s + jnp.where(m < 8, 1, 9))
    m, lane = grid(PITCH, 160)
    wanted = jnp.where(m < 3, 4 * m + 1, jnp.where(m >= 13, 4 * m - 35, 1000))
    for u in range(6):
        s5_ref[u * PITCH : (u + 1) * PITCH, :] = one_hot(lane == wanted + u)
    cell, lane = grid(512, 512)
    e_ref[...] = one_hot(lane == ((cell >> 5) & 3) * 128 + (cell & 31) * 4 + (cell >> 7))
    new, old = grid(256, 256)
    turn3_ref[...] = one_hot(old == 4 * (new & 63) + 2 * (new >> 7) + 1 - ((new >> 6) & 1))
    turn4_ref[...] = one_hot(old == 4 * (new & 63) + 2 * ((new >> 6) & 1) + (new >> 7))


def small_terms(perms, small, bias_ref, bias5_ref):
    b1_ref, b2_ref, b3_ref, b4_ref, b5_ref = small
    perm3, perm4 = perms

    def wide(value):
        return jnp.broadcast_to(value, (8, value.shape[1]))

    bias_ref[0:8, 0:128] = wide(jnp.concatenate([b1_ref[...]] * 2, axis=1))
    bias_ref[8:16, 0:128] = wide(jnp.concatenate([b2_ref[...]] * 2, axis=1))
    bias_ref[16:24, 0:256] = split_dot(wide(b3_ref[...]), perm3)
    four = split_dot(wide(b4_ref[...]), perm4)
    bias_ref[24:32, :] = jnp.concatenate([four, four], axis=1)
    chans = b5_ref.shape[1]
    five = jnp.concatenate([b5_ref[...], jnp.zeros((1, 128 - chans), F32)], axis=1)
    five = sum(lane_roll(five, 16 * n) for n in range(8))
    bias5_ref[...] = jnp.concatenate([jnp.broadcast_to(five, (128, 128)).T] * 2, axis=0)


def arrange(perms, weights, there, back):
    w1_ref, w2_ref, w3_ref, w4_ref, w5_ref = weights
    k1, k2, k3, k4, k5, k5s = there
    r5, r4, r3, r2 = back
    perm3, perm4 = perms
    chans = w1_ref.shape[2]
    w3p = dotn(w3_ref[...], perm3).astype(BF)
    w4p = dotn(w4_ref[...], perm4).astype(BF)
    for ref in (k1, k2, k3, k4, k5, k5s, r4, r3, r2):
        ref[...] = jnp.zeros(ref.shape, BF)
    for r in range(3):
        for s in range(3):
            at = s * 128 + r * 16
            k1[at : at + chans, :] = jnp.concatenate([w1_ref[r, s]] * 2, axis=1)
        part = w2_ref[r * 192 : (r + 1) * 192, :]
        k2[r * 256 : r * 256 + 192, :] = jnp.concatenate([part, part], axis=1)
        k3[r * 256 : r * 256 + 192, :] = w3p[r * 192 : (r + 1) * 192, :]
        for q in range(2):
            k4[r * 256 + q * 64 : r * 256 + q * 64 + 192, q * 256 : (q + 1) * 256] = w4p[
                r * 192 : (r + 1) * 192, :
            ]
        for s in range(3):
            t = 2 - r
            tap = (3 * r + s) * 64
            block = w3p[tap : tap + 64, :]
            r3[s * 64 : (s + 1) * 64, t * 256 : (t + 1) * 256] = block
            small = w2_ref[tap : tap + 64, :]
            r2[s * 64 : (s + 1) * 64, t * 128 + 64 : t * 128 + 128] = small
            if s == 2:
                r3[192:256, t * 256 : (t + 1) * 256] = block
                r2[192:256, t * 128 + 64 : t * 128 + 128] = small
            block = w4p[tap : tap + 64, :]
            for q in range(2):
                for q_src in range(2):
                    at = t * 512 + q_src * 256
                    if q - q_src + 1 == s:
                        r4[(1 - q) * 64 : (2 - q) * 64, at : at + 256] = block
                    if q_src == 1 - q and s == 2 - 2 * q:
                        r4[128 + (1 - q) * 64 : 128 + (2 - q) * 64, at : at + 256] = block
    gap_rows = jnp.zeros((16 - chans, 64), F32)
    turned = []
    for s in range(3):
        column = []
        for r in (2, 1, 0):
            column += [w5_ref[r, s].astype(F32), gap_rows]
        turned.append(jnp.concatenate(column + [jnp.zeros((80, 64), F32)], axis=0))
    w5 = [value.T for value in turned]
    turned = [value.astype(BF) for value in turned]
    empty = jnp.zeros((64, 64), BF)
    for t in range(6):
        at = 64 if t == 0 else (1536 if t == 5 else 512 + ((t - 1) // 2) * 512 + ((t - 1) % 2) * 64)
        side = 64 if t == 0 else (384 if t == 5 else 128 + ((t - 1) // 2) * 128 + ((t - 1) % 2) * 64)
        for b in range(3):
            p = t - 2 + b
            if not 0 <= p < 4:
                continue
            for src in range(4):
                for q in range(max(src - 1, 0), min(src + 1, 3) + 1):
                    k5[q * 64 + p * 16 : q * 64 + p * 16 + 16, at + src * 128 : at + src * 128 + 64] = (
                        turned[src - q + 1][b * 16 : b * 16 + 16, :]
                    )
        rows = [lane_roll(w5[s], 16 * (t - 2)).astype(BF)[:, :64] for s in (0, 2)]
        k5s[side : side + 64, :] = jnp.concatenate([rows[0], empty], axis=1)
        k5s[512 + side : 512 + side + 64, :] = jnp.concatenate([empty, rows[1]], axis=1)
    for p in range(4):
        for v in range(3):
            r5[p * 64 : (p + 1) * 64, v * 128 : (v + 1) * 128] = lane_roll(w5[2 - v], 16 * p).astype(BF)


def in_plane(extent, pos_ref, mask):
    row0 = pos_ref[0]
    col0 = pos_ref[1]
    m = lax.broadcasted_iota(jnp.int32, (PITCH, 128), 0)
    col = col0 + jnp.where(m < 8, m + 32, m - 16)
    col_ok = jnp.logical_and(col >= 0, col < extent[1])
    for k in range(CHUNKS):
        row = row0 + jnp.where(m < 8, k - 9, k - 8)
        ok = jnp.logical_and(col_ok, jnp.logical_and(row >= 0, row < extent[0]))
        mask[k * PITCH : (k + 1) * PITCH, :] = jnp.where(ok, 1.0, 0.0)


def forward(
    extent,
    pos_ref,
    dx_ref,
    w1_hbm,
    w2_hbm,
    w3_hbm,
    w4_hbm,
    w5_hbm,
    b1_ref,
    b2_ref,
    b3_ref,
    b4_ref,
    b5_ref,
    mask,
    s5_ref,
    turn3_ref,
    turn4_ref,
    r5,
    r4,
    r3,
    r2,
    x0,
    x1,
    x2,
    x3,
    a3,
    a4,
    fine_ref,
    bias_ref,
    bias5_ref,
    s0_ref,
    e_ref,
    k1,
    k2,
    k3,
    k4,
    k5,
    k5s,
    w1_ref,
    w2_ref,
    w3_ref,
    w4_ref,
    w5_ref,
    sems,
):
    copies = [
        pltpu.make_async_copy(src, dst, sems.at[n])
        for n, (src, dst) in enumerate(
            (
                (w1_hbm, w1_ref),
                (w2_hbm, w2_ref),
                (w3_hbm, w3_ref),
                (w4_hbm, w4_ref),
                (w5_hbm, w5_ref),
            )
        )
    ]
    for copy in copies:
        copy.start()
    small = (b1_ref, b2_ref, b3_ref, b4_ref, b5_ref)
    select(s0_ref, s5_ref, e_ref, turn3_ref, turn4_ref)
    in_plane(extent, pos_ref, mask)
    low = low_half()
    clear_margins(((x0, 2, 32), (x1, 3, 30), (x2, 4, 29), (x3, 5, 29), (a4, 5, 29)))

    def coarse_chunk(k):
        lines = dx_ref[pl.ds(k - 2, 3)].reshape(48, 64)
        lines = jnp.concatenate([lines, jnp.zeros((80, 64), BF)], axis=0)
        moved = dott(s0_ref[...], lines).astype(BF)
        for s in range(3):
            x0[pl.ds(pl.multiple_of(k * PITCH, 16), PITCH), s * 128 : (s + 1) * 128] = moved[
                s * PITCH : (s + 1) * PITCH, :
            ]

    grouped(2, 32, GROUP0, coarse_chunk)
    for copy in copies:
        copy.wait()
    perms = (turn3_ref[...].T, turn4_ref[...].T)
    small_terms(perms, small, bias_ref, bias5_ref)
    arrange(
        perms,
        (w1_ref, w2_ref, w3_ref, w4_ref, w5_ref),
        (k1, k2, k3, k4, k5, k5s),
        (r5, r4, r3, r2),
    )

    def narrow(read, weight, bias_at, variants):
        def work(start, size):
            wide = size + 32
            z = dotn(read(start - 16, wide), weight[...])
            z = jnp.tanh(z + bias_ref[8 * bias_at : 8 * bias_at + 1, 0:128])
            z = z * take(mask, start - 16, wide)
            inner = slice(16, 16 + size)
            left = jnp.where(low, roll(z, 1), z)
            put(variants, start, size, left[inner], 0, 128)
            put(variants, start, size, roll(z, -1)[inner], 128, 256)

        return work

    blocks(3, 27 // N1, N1, narrow(lambda at, n: take(x0, at, n), k1, 0, x1))
    blocks(4, 25 // N2, N2, narrow(lambda at, n: taps(x1, at, n), k2, 1, x2))

    def conv_three(start, size):
        wide = size + 32
        z = dotn(taps(x2, start - 16, wide), k3[...])
        z = jnp.tanh(z + bias_ref[16:17, 0:256])
        ok = take(mask, start - 16, wide)
        inner = slice(16, 16 + size)
        for p in range(2):
            half = z[:, p * 128 : (p + 1) * 128] * ok
            left = jnp.where(low, roll(half, 1), half)
            right = jnp.where(low, half, roll(half, -1))
            put(x3, start, size, left[inner], p * 256, p * 256 + 128)
            put(x3, start, size, right[inner], p * 256 + 128, p * 256 + 256)
            put(a3, start, size, half[inner], p * 128, p * 128 + 128)

    blocks(5, 24 // N3, N3, conv_three)

    def conv_four(start, size):
        ok = take(mask, start, size)
        for p in range(2):
            lines = []
            for r in range(3):
                phase, by = row_of(p + r - 1)
                lines.append(take(x3, start + by, size, phase * 256, phase * 256 + 256))
            z = dotn(jnp.concatenate(lines, axis=1), k4[...])
            z = jnp.tanh(z + bias_ref[24:25, 0:512])
            for q in range(4):
                at = p * 512 + q * 128
                put(a4, start, size, z[:, q * 128 : (q + 1) * 128] * ok, at, at + 128)

    blocks(5, 24 // N4, N4, conv_four)

    size = ROWS * PITCH
    wide = size + 32
    at = OWN - 16
    side = []
    for low_lane in (384, 0):
        side.append(take(a4, at - PITCH, wide, 512 + low_lane, 640 + low_lane))
        side.append(take(a4, at, wide, low_lane, low_lane + 128))
        side.append(take(a4, at, wide, 512 + low_lane, 640 + low_lane))
        side.append(take(a4, at + PITCH, wide, low_lane, low_lane + 128))
    side = dotn(jnp.concatenate(side, axis=1), k5s[...])
    side = jnp.where(low, roll(side, 1), roll(side, -1))[16 : 16 + size]
    side = side.reshape(ROWS, PITCH, 128)[:, 16:48, :].reshape(ROWS * COLS, 128).T
    field = jnp.concatenate(
        [own(a4, 512, 1024, -1), own(a4, 0, 1024), own(a4, 0, 512, 1)], axis=1
    )
    z = dott(k5[...], field) + bias5_ref[:, 0:1]
    z = [z[0:64] + side[0:64], z[64:128], z[128:192], z[192:256] + side[64:128]]
    z = jnp.concatenate(
        [jnp.concatenate([z[q][:, g * 128 : (g + 1) * 128] for q in range(4)], axis=1) for g in range(4)],
        axis=0,
    )
    high = z.astype(BF)
    rest = (z - high.astype(F32)).astype(BF)
    z = dotn(rest, e_ref[...]) + dotn(high, e_ref[...])
    for g in range(4):
        for n in range(4):
            for p in range(4):
                fine_ref[16 * g + 4 * n + p] = z[
                    g * 64 + p * 16 : g * 64 + p * 16 + 16, n * 128 : (n + 1) * 128
                ]


def backward(
    scale,
    pos_ref,
    dc_ref,
    mask,
    s5_ref,
    turn3_ref,
    turn4_ref,
    r5,
    r4,
    r3,
    r2,
    x0,
    x1,
    x2,
    x3,
    a3,
    a4,
    keep_ref,
    send_ref,
    c5,
    b4,
    b3,
    b2,
    b1,
    g_ref,
):
    low = low_half()
    clear_margins(((c5, 5, 29), (b4, 5, 29), (b3, 6, 27), (b2, 7, 27)))

    def cot_chunk(k):
        lines = dc_ref[pl.ds(4 * (k - 5), 6)].reshape(96, 160)
        lines = jnp.concatenate([lines, jnp.zeros((32, 160), BF)], axis=0)
        moved = dott(s5_ref[...], lines).astype(BF)
        for u in range(6):
            c5[pl.ds(pl.multiple_of(k * PITCH, 16), PITCH), u * 128 : (u + 1) * 128] = moved[
                u * PITCH : (u + 1) * PITCH, :
            ]

    grouped(5, 29, GROUP5, cot_chunk)

    def back_four(start, size):
        ok = take(mask, start, size)
        for q in range(4):
            z = dott(take(c5, start, size, q * 128, q * 128 + 384), r5[...])
            for p in range(2):
                at = p * 512 + q * 128
                z_p = z[:, p * 128 : (p + 1) * 128] * ok
                put(b4, start, size, z_p * slope(take(a4, start, size, at, at + 128)), at, at + 128)

    blocks(5, 24 // M4, M4, back_four)

    def back_three(start, size):
        wide = size + 32
        ok = take(mask, start, size)
        inner = slice(16, 16 + size)
        for p in range(2):
            lines = []
            for t in range(3):
                phase, by = row_of(p + t - 1)
                lines.append(take(b4, start - 16 + by, wide, phase * 512, phase * 512 + 512))
            z = dott(jnp.concatenate(lines, axis=1), r4[...])
            moved = jnp.where(low, roll(z[:, 128:256], -1), roll(z[:, 128:256], 1))
            z = (z[:, 0:128] + moved)[inner] * ok
            at = p * 128
            put(b3, start, size, z * slope(take(a3, start, size, at, at + 128)), at, at + 128)

    blocks(6, 21 // M3, M3, back_three)

    def back_narrow(src, weight, act, out):
        def work(start, size):
            wide = size + 32
            z = dott(taps(src, start - 16, wide), weight[...])
            pair = jnp.where(low, roll(z[:, 0:128], -1), z[:, 0:128])
            z = pair + lane_roll(pair, 64) + roll(z[:, 128:256], 1)
            z = z[16 : 16 + size] * take(mask, start, size)
            z = jnp.where(low, 0.0, z * slope(take(act, start, size, 0, 128)))
            put(out, start, size, z, 0, 128)

        return work

    blocks(7, 20 // M2, M2, back_narrow(b3, r3, x2, b2))
    blocks(8, 18 // M1, M1, back_narrow(b2, r2, x1, b1))

    g_ref[PACKED - 64 :, :] = jnp.zeros((64, 256), F32)
    g_ref[1152:1344, 192:256] = jnp.zeros((192, 64), F32)

    back = own(b4, 0, 1024)
    sums4 = jnp.sum(back.astype(F32), axis=0, keepdims=True)
    back = back.T
    for r in range(3):
        total = None
        for p in range(2):
            phase, by = row_of(p + r - 1)
            field = own(x3, phase * 256, phase * 256 + 256, by // PITCH)
            term = dotn(back[p * 512 : (p + 1) * 512, :], field)
            total = term if total is None else total + term
        total = total[0:256, 0:192] + total[256:512, 64:256]
        g_ref[r * 192 : (r + 1) * 192, :] = split_dot(total.T * scale, turn4_ref[...])
    sums4 = sums4[:, 0:512] + sums4[:, 512:1024]
    sums4 = sums4[:, 0:256] + sums4[:, 256:512]

    back = own(b3, 0, 256)
    sums3 = jnp.sum(back.astype(F32), axis=0, keepdims=True)
    back = back.T
    for r in range(3):
        total = dotn(back, own(x2, 0, 256, r - 1))[:, 0:192]
        g_ref[576 + r * 192 : 576 + (r + 1) * 192, :] = split_dot(total.T * scale, turn3_ref[...])

    back = own(b2, 0, 128)
    sums2 = jnp.sum(back.astype(F32), axis=0, keepdims=True)
    back = back.T
    for r in range(3):
        total = dotn(back[64:128, :], own(x1, 0, 256, r - 1))
        g_ref[1152:1344, r * 64 : (r + 1) * 64] = total[:, 0:192].T * scale

    back = own(b1, 0, 128)
    sums1 = jnp.sum(back.astype(F32), axis=0, keepdims=True)
    back = back.T
    total = dotn(back[64:128, :], own(x0, 0, 384)).T * scale
    for s in range(3):
        g_ref[1152 + s * 48 : 1152 + (s + 1) * 48, 192:256] = total[s * 128 : s * 128 + 48, :]

    cot = own(c5, 0, 768)
    sums5 = jnp.sum(cot.astype(F32), axis=0, keepdims=True)
    cot = cot.T
    total = None
    for q in range(4):
        field = jnp.concatenate(
            [own(a4, q * 128, q * 128 + 128), own(a4, 512 + q * 128, 640 + q * 128)], axis=1
        )
        term = dotn(cot[q * 128 : q * 128 + 384, :], field)
        total = term if total is None else total + term
    total = total * scale
    for r in range(3):
        for s in range(3):
            sum_p = None
            for p in range(4):
                at = (2 - s) * 128 + (p + 2 - r) * 16
                term = total[at : at + 16, p * 64 : (p + 1) * 64]
                sum_p = term if sum_p is None else sum_p + term
            g_ref[1344 + s * 16 : 1344 + (s + 1) * 16, r * 64 : (r + 1) * 64] = sum_p

    sums5 = sums5[:, 128:256] + sums5[:, 256:384] + sums5[:, 384:512] + sums5[:, 512:640]
    five = sums5
    for t in range(1, 4):
        five = five + lane_roll(sums5, -16 * t)
    biases = [
        split_dot(jnp.broadcast_to(sums4 * scale, (8, 256)), turn4_ref[...])[0:1],
        split_dot(jnp.broadcast_to(sums3 * scale, (8, 256)), turn3_ref[...])[0:1],
        jnp.concatenate([sums2, sums1], axis=1) * scale,
        jnp.concatenate([five, jnp.zeros((1, 128), F32)], axis=1) * scale,
    ]
    for n, value in enumerate(biases):
        high = value.astype(BF).astype(F32)
        g_ref[1392 + 2 * n : 1393 + 2 * n, :] = high
        g_ref[1393 + 2 * n : 1394 + 2 * n, :] = value - high

    half = PACKED // 2
    core = pos_ref[2]
    keep_ref[...] = g_ref[pl.ds(pl.multiple_of(core * half, 16), half), :]
    send_ref[...] = g_ref[pl.ds(pl.multiple_of((1 - core) * half, 16), half), :].astype(BF)


def finish(chans, places, pos_ref, mine_ref, other_ref, g1, g2, g3, g4, g5, c1, c2, c3, c4, c5, full):
    half = PACKED // 2
    size = half // places
    core = pos_ref[2]
    for b in range(places):
        at = pl.multiple_of(lax.bitwise_xor(pos_ref[3], b) * size, 8)
        here = pl.multiple_of(core * half + b * size, 8)
        there = pl.multiple_of((1 - core) * half + b * size, 8)
        full[pl.ds(here, size), :] = mine_ref[pl.ds(at, size), :].astype(F32)
        full[pl.ds(there, size), :] = other_ref[pl.ds(at, size), :].astype(F32)
    g4[...] = full[0:576, :]
    g3[...] = full[576:1152, :]
    for r in range(3):
        g2[r * 192 : (r + 1) * 192, :] = full[1152:1344, r * 64 : (r + 1) * 64]
        for s in range(3):
            at = 1152 + s * 48 + r * 16
            g1[r, s] = full[at : at + chans, 192:256]
            at = 1344 + s * 16
            g5[r, s] = full[at : at + chans, r * 64 : (r + 1) * 64]
    sums = [full[1392 + 2 * n : 1393 + 2 * n, :] + full[1393 + 2 * n : 1394 + 2 * n, :] for n in range(4)]
    c4[...] = sums[0]
    c3[...] = sums[1]
    c2[...] = sums[2][:, 64:128]
    c1[...] = sums[2][:, 192:256]
    c5[...] = sums[3][:, 16 : 16 + chans]


def pairs(count, by):
    return [(i, i + by) for i in range(count) if 0 <= i + by < count]


def coarse_lines(coarse):
    gx, gy = lax.axis_size("gx"), lax.axis_size("gy")
    chans, each = coarse.shape[:2]
    cols = coarse.shape[2] // gy
    wide = cols + 2 * HALO
    tiles = coarse.reshape(chans, each, gy, cols).transpose(2, 1, 0, 3)
    before = jnp.pad(tiles[:-1, :, :, cols - HALO :], ((1, 0), (0, 0), (0, 0), (0, 0)))
    after = jnp.pad(tiles[1:, :, :, :HALO], ((0, 1), (0, 0), (0, 0), (0, 0)))
    pieces = jnp.concatenate([before, tiles, after], axis=3)
    got = lax.all_to_all(pieces, "gy", 0, 0, tiled=True).reshape(gy * each, chans, wide)
    above = lax.ppermute(got[-HALO:], "gx", pairs(gx, 1))
    below = lax.ppermute(got[:HALO], "gx", pairs(gx, -1))
    whole = jnp.concatenate([above, got, below])
    here, before = rows(whole, 1, 3), rows(whole, 2, 2)
    return jnp.concatenate([before[:, :, 36:44], gap(before, 12), here], axis=2)


def cotangent_lines(cotangent):
    gx, gy = lax.axis_size("gx"), lax.axis_size("gy")
    n = FINE_HALO
    left = lax.ppermute(cotangent[:, :, -n:].transpose(2, 0, 1), "gy", pairs(gy, 1))
    right = lax.ppermute(cotangent[:, :, :n].transpose(2, 0, 1), "gy", pairs(gy, -1))
    cot = jnp.concatenate(
        [left.transpose(2, 1, 0), cotangent.transpose(1, 0, 2), right.transpose(2, 1, 0)], axis=2
    )
    above = lax.ppermute(cot[-n:], "gx", pairs(gx, 1))
    below = lax.ppermute(cot[:n], "gx", pairs(gx, -1))
    whole = jnp.concatenate([above, cot, below])
    here, before = rows(whole, 1, 9), rows(whole, 5, 5)
    return jnp.concatenate([before[:, :, 138:152], gap(before, 4), here[:, :, :142]], axis=2)


def rows(value, low, high):
    return jnp.pad(value, ((low, high), (0, 4), (0, 0)))


def gap(value, count):
    return jnp.zeros(value.shape[:2] + (count,), BF)


def total_over_all(keep, send):
    gx, gy = lax.axis_size("gx"), lax.axis_size("gy")
    at_x = lax.axis_index("gx")

    def swap(block, axis, flip):
        count = lax.axis_size(axis)
        return lax.ppermute(block, axis, [(i, i ^ flip) for i in range(count)])

    def tree(terms):
        while len(terms) > 1:
            terms = [terms[n] + terms[n + 1] for n in range(0, len(terms), 2)]
        return terms[0]

    value = keep + swap(send, "gy", 1).astype(F32)
    size = value.shape[0] // gx

    def part(place):
        return lax.dynamic_slice_in_dim(value, place * size, size, 0)

    terms = [part(at_x)]
    for d in range(1, gx):
        terms.append(swap(part(at_x ^ d).astype(BF), "gx", d).astype(F32))
    block = tree(terms).astype(BF)
    terms = [block] + [swap(block, "gy", 2 * d) for d in range(1, gy // 2)]
    block = tree([term.astype(F32) for term in terms]).astype(BF)
    mine = jnp.concatenate([block] + [swap(block, "gx", d) for d in range(1, gx)])
    return mine, swap(mine, "gy", 1)


def local(
    coarse,
    weight_one,
    weight_two,
    weight_three,
    weight_four,
    weight_five,
    bias_one,
    bias_two,
    bias_three,
    bias_four,
    bias_five,
    cotangent,
):
    gx, gy = lax.axis_size("gx"), lax.axis_size("gy")
    chans = coarse.shape[0]
    tile_rows = coarse.shape[1] * gy
    tile_cols = coarse.shape[2] // gy
    assert (tile_rows, tile_cols) == (ROWS, COLS)
    at_x, at_y = lax.axis_index("gx"), lax.axis_index("gy")
    pos = jnp.stack([at_x * ROWS, at_y * COLS, at_y % 2, at_x]).astype(jnp.int32)
    extent = (ROWS * gx, COLS * gy)
    scale = float((16 * extent[0] * extent[1]) ** -0.5)

    smem = pl.BlockSpec(memory_space=pltpu.SMEM)
    vmem = pl.BlockSpec(memory_space=pltpu.VMEM)
    params = pltpu.CompilerParams(vmem_limit_bytes=LIMIT * 1024 * 1024)

    def near(value):
        return pltpu.with_memory_space_constraint(value, pltpu.VMEM)

    def buf(width, kind=BF):
        return pltpu.VMEM((CELLS, width), kind)

    shared = (
        buf(128, F32),
        pltpu.VMEM((6 * PITCH, 160), BF),
        pltpu.VMEM((256, 256), BF),
        pltpu.VMEM((256, 256), BF),
        pltpu.VMEM((256, 384), BF),
        pltpu.VMEM((256, 1536), BF),
        pltpu.VMEM((256, 768), BF),
        pltpu.VMEM((256, 384), BF),
        buf(384),
        buf(256),
        buf(256),
        buf(512),
        buf(256),
        buf(1024),
    )
    hbm = pl.BlockSpec(memory_space=pltpu.HBM)
    weights = (
        weight_one,
        weight_two.reshape(576, 64),
        weight_three.reshape(576, 256),
        weight_four.reshape(576, 256),
        weight_five.transpose(0, 1, 3, 2),
    )
    *fields, fine = pl.pallas_call(
        lambda *refs: forward(extent, *refs),
        out_shape=shared + (jax.ShapeDtypeStruct((4 * ROWS, 16, 4 * COLS), F32),),
        in_specs=[smem, vmem] + [hbm] * 5 + [vmem] * 5,
        out_specs=(vmem,) * 15,
        scratch_shapes=[
            pltpu.VMEM((32, 512), F32),
            pltpu.VMEM((256, 128), F32),
            pltpu.VMEM((3 * PITCH, 64), BF),
            pltpu.VMEM((512, 512), BF),
            pltpu.VMEM((384, 128), BF),
            pltpu.VMEM((768, 128), BF),
            pltpu.VMEM((768, 256), BF),
            pltpu.VMEM((768, 512), BF),
            pltpu.VMEM((256, 2048), BF),
            pltpu.VMEM((1024, 128), BF),
        ]
        + [pltpu.VMEM(w.shape, BF) for w in weights]
        + [pltpu.SemaphoreType.DMA((5,))],
        compiler_params=params,
        name="forward",
    )(
        pos,
        coarse_lines(coarse),
        *[pltpu.with_memory_space_constraint(w, pltpu.HBM) for w in weights],
        bias_one.reshape(1, -1),
        bias_two.reshape(1, -1),
        bias_three.reshape(1, -1),
        bias_four.reshape(1, -1),
        bias_five.reshape(1, -1),
    )
    fields = [near(f) for f in fields]
    half = PACKED // 2
    keep, send = pl.pallas_call(
        lambda *refs: backward(scale, *refs),
        out_shape=(pltpu.VMEM((half, 256), F32), pltpu.VMEM((half, 256), BF)),
        in_specs=[smem] + [vmem] * 15,
        out_specs=(vmem,) * 2,
        scratch_shapes=[
            buf(768),
            buf(1024),
            buf(256),
            buf(128),
            buf(128),
            pltpu.VMEM((PACKED, 256), F32),
        ],
        compiler_params=params,
        name="backward",
    )(pos, cotangent_lines(cotangent), *fields)
    mine, other = total_over_all(keep, send)

    def out(*shape):
        return jax.ShapeDtypeStruct(shape, F32)

    g1, g2, g3, g4, g5, c1, c2, c3, c4, c5 = pl.pallas_call(
        lambda *refs: finish(chans, gx, *refs),
        out_shape=(
            out(3, 3, chans, 64),
            out(576, 64),
            out(576, 256),
            out(576, 256),
            out(3, 3, chans, 64),
            out(1, 64),
            out(1, 64),
            out(1, 256),
            out(1, 256),
            out(1, chans),
        ),
        in_specs=[smem, vmem, vmem],
        out_specs=(vmem,) * 10,
        scratch_shapes=[pltpu.VMEM((PACKED, 256), F32)],
        compiler_params=params,
        name="finish",
    )(pos, mine, other)
    return (
        fine.transpose(1, 0, 2)[:chans],
        g1,
        g2.reshape(3, 3, 64, 64),
        g3.reshape(3, 3, 64, 256),
        g4.reshape(3, 3, 64, 256),
        g5.transpose(0, 1, 3, 2),
        c1.reshape(64),
        c2.reshape(64),
        c3.reshape(256),
        c4.reshape(256),
        c5.reshape(chans),
    )


def solution(mesh):
    in_specs = (
        P(None, ("gx", "gy"), None),
        P(),
        P(),
        P(),
        P(),
        P(),
        P(),
        P(),
        P(),
        P(),
        P(),
        P(None, "gx", "gy"),
    )
    out_specs = (P(None, "gx", "gy"), P(), P(), P(), P(), P(), P(), P(), P(), P(), P())
    return jax.shard_map(local, mesh=mesh, in_specs=in_specs, out_specs=out_specs, check_vma=False)
```

```python
import jax
import jax.numpy as jnp
from jax import lax
from jax.experimental import pallas as pl
from jax.experimental.pallas import tpu as pltpu
from jax.sharding import PartitionSpec as P

BF = jnp.bfloat16
F32 = jnp.float32

ROWS, COLS, PITCH, CHUNKS = 16, 32, 48, 32
CELLS = PITCH * CHUNKS
OWN = PITCH * 8
HALO = 6
FINE_HALO = 12
TERMS = 1400
GROUP0, GROUP5 = 7, 6
N1, N2, N3, N4 = 3, 5, 3, 4
M4, M3, M2, M1 = 4, 3, 4, 3
LIMIT = 12


def dotn(left, right):
    return lax.dot_general(left, right, (((1,), (0,)), ((), ())), preferred_element_type=F32)


def dott(left, right):
    return lax.dot_general(left, right, (((1,), (1,)), ((), ())), preferred_element_type=F32)


def take(ref, start, count, low=0, high=None):
    high = ref.shape[1] if high is None else high
    if not isinstance(start, int):
        start = pl.multiple_of(start, 16)
    return ref[pl.ds(start, count), low:high]


def taps(ref, start, count):
    return jnp.concatenate([take(ref, start + d, count) for d in (-PITCH, 0, PITCH)], axis=1)


def own(ref, low, high, row=0):
    block = ref[OWN + PITCH * row : OWN + PITCH * (row + ROWS), low:high]
    return block.reshape(ROWS, PITCH, high - low)[:, 16:48, :].reshape(ROWS * COLS, high - low)


def roll(value, by):
    return pltpu.roll(value, by % value.shape[0], 0)


def lane_roll(value, by):
    return pltpu.roll(value, by % value.shape[1], 1)


def grouped(first, last, group, work):
    def step(n, _):
        for k in range(group):
            work(first + n * group + k)
        return 0

    lax.fori_loop(0, (last - first) // group, step, 0)


def blocks(first, chunks_each, count, work):
    size = chunks_each * PITCH
    if count == 1:
        work(first * PITCH, size)
        return

    def step(n, _):
        work(pl.multiple_of(first * PITCH + n * size, 16), size)
        return 0

    lax.fori_loop(0, count, step, 0)


def clear_margins(fields):
    for ref, first, last in fields:
        ref[0 : first * PITCH, :] = jnp.zeros((first * PITCH, ref.shape[1]), BF)
        if last < CHUNKS:
            ref[last * PITCH :, :] = jnp.zeros((CELLS - last * PITCH, ref.shape[1]), BF)


def put(ref, start, size, value, low, high):
    ref[pl.ds(start, size), low:high] = value.astype(BF)


def row_of(t):
    return t % 2, PITCH * (t // 2)


def low_half():
    return lax.broadcasted_iota(jnp.int32, (1, 128), 1) < 64


def slope(act):
    act = act.astype(F32)
    return 1.0 - act * act


def split_dot(value, perm):
    high = value.astype(BF)
    rest = value - high.astype(F32)
    middle = rest.astype(BF)
    low = (rest - middle.astype(F32)).astype(BF)
    return (dotn(low, perm) + dotn(middle, perm)) + dotn(high, perm)


def grid(rows, cols):
    return tuple(lax.broadcasted_iota(jnp.int32, (rows, cols), n) for n in (0, 1))


def one_hot(chosen):
    return jnp.where(chosen, 1.0, 0.0).astype(BF)


def select(core, s0_ref, s5_ref, e_ref, turn3_ref, turn4_ref):
    m, lane = grid(PITCH, 256)
    for s in range(3):
        after = m + 31 + s + HALO + core * COLS
        here = m - 17 + s + HALO + core * COLS
        wanted = jnp.where(m < 8, after, jnp.where(here >= 0, here + 128, -1))
        s0_ref[s * PITCH : (s + 1) * PITCH, :] = one_hot(lane == wanted)
    for u in range(6):
        col = 4 * jnp.where(m < 8, m + 32, m - 16) + u - 1
        beyond = jnp.where(col - 128 < FINE_HALO, col + 64, -1)
        beyond = jnp.where(col == 127, 204, beyond)
        here = jnp.where(col < 0, col + 140, jnp.where(col < 128, col, col + 12))
        here = jnp.where(col < -FINE_HALO, -1, here)
        s5_ref[u * PITCH : (u + 1) * PITCH, :] = one_hot(lane == jnp.where(m < 8, beyond, here))
    cell, lane = grid(512, 512)
    e_ref[...] = one_hot(lane == ((cell >> 5) & 3) * 128 + (cell & 31) * 4 + (cell >> 7))
    new, old = grid(256, 256)
    turn3_ref[...] = one_hot(old == 4 * (new & 63) + 2 * (new >> 7) + 1 - ((new >> 6) & 1))
    turn4_ref[...] = one_hot(old == 4 * (new & 63) + 2 * ((new >> 6) & 1) + (new >> 7))


def small_terms(perms, small, bias_ref, bias5_ref):
    b1_ref, b2_ref, b3_ref, b4_ref, b5_ref = small
    perm3, perm4 = perms

    def wide(value):
        return jnp.broadcast_to(value, (8, value.shape[1]))

    bias_ref[0:8, 0:128] = wide(jnp.concatenate([b1_ref[...]] * 2, axis=1))
    bias_ref[8:16, 0:128] = wide(jnp.concatenate([b2_ref[...]] * 2, axis=1))
    bias_ref[16:24, 0:256] = split_dot(wide(b3_ref[...]), perm3)
    four = split_dot(wide(b4_ref[...]), perm4)
    bias_ref[24:32, :] = jnp.concatenate([four, four], axis=1)
    chans = b5_ref.shape[1]
    five = jnp.concatenate([b5_ref[...], jnp.zeros((1, 128 - chans), F32)], axis=1)
    five = sum(lane_roll(five, 16 * n) for n in range(8))
    bias5_ref[...] = jnp.concatenate([jnp.broadcast_to(five, (128, 128)).T] * 2, axis=0)


def arrange(perms, weights, there, back):
    w1_ref, w2_ref, w3_ref, w4_ref, w5_ref = weights
    k1, k2, k3, k4, k5, k5s = there
    r5, r4, r3, r2 = back
    perm3, perm4 = perms
    chans = w1_ref.shape[2]
    w3p = dotn(w3_ref[...], perm3).astype(BF)
    w4p = dotn(w4_ref[...], perm4).astype(BF)
    for ref in (k1, k2, k3, k4, k5, k5s, r4, r3, r2):
        ref[...] = jnp.zeros(ref.shape, BF)
    for r in range(3):
        for s in range(3):
            at = s * 128 + r * 16
            k1[at : at + chans, :] = jnp.concatenate([w1_ref[r, s]] * 2, axis=1)
        part = w2_ref[r * 192 : (r + 1) * 192, :]
        k2[r * 256 : r * 256 + 192, :] = jnp.concatenate([part, part], axis=1)
        k3[r * 256 : r * 256 + 192, :] = w3p[r * 192 : (r + 1) * 192, :]
        for q in range(2):
            k4[r * 256 + q * 64 : r * 256 + q * 64 + 192, q * 256 : (q + 1) * 256] = w4p[
                r * 192 : (r + 1) * 192, :
            ]
        for s in range(3):
            t = 2 - r
            tap = (3 * r + s) * 64
            block = w3p[tap : tap + 64, :]
            r3[s * 64 : (s + 1) * 64, t * 256 : (t + 1) * 256] = block
            small = w2_ref[tap : tap + 64, :]
            r2[s * 64 : (s + 1) * 64, t * 128 + 64 : t * 128 + 128] = small
            if s == 2:
                r3[192:256, t * 256 : (t + 1) * 256] = block
                r2[192:256, t * 128 + 64 : t * 128 + 128] = small
            block = w4p[tap : tap + 64, :]
            for q in range(2):
                for q_src in range(2):
                    at = t * 512 + q_src * 256
                    if q - q_src + 1 == s:
                        r4[(1 - q) * 64 : (2 - q) * 64, at : at + 256] = block
                    if q_src == 1 - q and s == 2 - 2 * q:
                        r4[128 + (1 - q) * 64 : 128 + (2 - q) * 64, at : at + 256] = block
    gap_rows = jnp.zeros((16 - chans, 64), F32)
    turned = []
    for s in range(3):
        column = []
        for r in (2, 1, 0):
            column += [w5_ref[r, s].astype(F32), gap_rows]
        turned.append(jnp.concatenate(column + [jnp.zeros((80, 64), F32)], axis=0))
    w5 = [value.T for value in turned]
    turned = [value.astype(BF) for value in turned]
    empty = jnp.zeros((64, 64), BF)
    for t in range(6):
        at = 64 if t == 0 else (1536 if t == 5 else 512 + ((t - 1) // 2) * 512 + ((t - 1) % 2) * 64)
        side = 64 if t == 0 else (384 if t == 5 else 128 + ((t - 1) // 2) * 128 + ((t - 1) % 2) * 64)
        for b in range(3):
            p = t - 2 + b
            if not 0 <= p < 4:
                continue
            for src in range(4):
                for q in range(max(src - 1, 0), min(src + 1, 3) + 1):
                    k5[q * 64 + p * 16 : q * 64 + p * 16 + 16, at + src * 128 : at + src * 128 + 64] = (
                        turned[src - q + 1][b * 16 : b * 16 + 16, :]
                    )
        rows = [lane_roll(w5[s], 16 * (t - 2)).astype(BF)[:, :64] for s in (0, 2)]
        k5s[side : side + 64, :] = jnp.concatenate([rows[0], empty], axis=1)
        k5s[512 + side : 512 + side + 64, :] = jnp.concatenate([empty, rows[1]], axis=1)
    for p in range(4):
        for v in range(3):
            r5[p * 64 : (p + 1) * 64, v * 128 : (v + 1) * 128] = lane_roll(w5[2 - v], 16 * p).astype(BF)


def in_plane(extent, pos_ref, mask):
    row0 = pos_ref[0]
    col0 = pos_ref[1]
    m = lax.broadcasted_iota(jnp.int32, (PITCH, 128), 0)
    col = col0 + jnp.where(m < 8, m + 32, m - 16)
    col_ok = jnp.logical_and(col >= 0, col < extent[1])
    for k in range(CHUNKS):
        row = row0 + jnp.where(m < 8, k - 9, k - 8)
        ok = jnp.logical_and(col_ok, jnp.logical_and(row >= 0, row < extent[0]))
        mask[k * PITCH : (k + 1) * PITCH, :] = jnp.where(ok, 1.0, 0.0)


def forward(
    extent,
    pos_ref,
    dx_ref,
    w1_hbm,
    w2_hbm,
    w3_hbm,
    w4_hbm,
    w5_hbm,
    b1_ref,
    b2_ref,
    b3_ref,
    b4_ref,
    b5_ref,
    mask,
    s5_ref,
    turn3_ref,
    turn4_ref,
    r5,
    r4,
    r3,
    r2,
    x0,
    x1,
    x2,
    x3,
    a3,
    a4,
    fine_ref,
    bias_ref,
    bias5_ref,
    s0_ref,
    e_ref,
    k1,
    k2,
    k3,
    k4,
    k5,
    k5s,
    w1_ref,
    w2_ref,
    w3_ref,
    w4_ref,
    w5_ref,
    sems,
):
    copies = [
        pltpu.make_async_copy(src, dst, sems.at[n])
        for n, (src, dst) in enumerate(
            (
                (w1_hbm, w1_ref),
                (w2_hbm, w2_ref),
                (w3_hbm, w3_ref),
                (w4_hbm, w4_ref),
                (w5_hbm, w5_ref),
            )
        )
    ]
    for copy in copies:
        copy.start()
    small = (b1_ref, b2_ref, b3_ref, b4_ref, b5_ref)
    select(pos_ref[2], s0_ref, s5_ref, e_ref, turn3_ref, turn4_ref)
    in_plane(extent, pos_ref, mask)
    low = low_half()
    clear_margins(((x0, 2, 30), (x1, 3, 30), (x2, 4, 29), (x3, 5, 29), (a4, 5, 29)))

    def coarse_pair(n):
        lines = []
        for k in (2 * n, 2 * n + 1):
            before = dx_ref[pl.ds(k - 2, 3)].reshape(48, 128)
            here = dx_ref[pl.ds(k - 1, 3)].reshape(48, 128)
            lines += [jnp.concatenate([before, here], axis=1), jnp.zeros((80, 256), BF)]
        moved = dott(s0_ref[...], jnp.concatenate(lines, axis=0)).astype(BF)
        for half in range(2):
            at = pl.multiple_of((2 * n + half) * PITCH, 16)
            for s in range(3):
                x0[pl.ds(at, PITCH), s * 128 : (s + 1) * 128] = moved[
                    s * PITCH : (s + 1) * PITCH, half * 128 : (half + 1) * 128
                ]

    grouped(1, 15, GROUP0, coarse_pair)
    for copy in copies:
        copy.wait()
    perms = (turn3_ref[...].T, turn4_ref[...].T)
    small_terms(perms, small, bias_ref, bias5_ref)
    arrange(
        perms,
        (w1_ref, w2_ref, w3_ref, w4_ref, w5_ref),
        (k1, k2, k3, k4, k5, k5s),
        (r5, r4, r3, r2),
    )

    def narrow(read, weight, bias_at, variants):
        def work(start, size):
            wide = size + 32
            z = dotn(read(start - 16, wide), weight[...])
            z = jnp.tanh(z + bias_ref[8 * bias_at : 8 * bias_at + 1, 0:128])
            z = z * take(mask, start - 16, wide)
            inner = slice(16, 16 + size)
            left = jnp.where(low, roll(z, 1), z)
            put(variants, start, size, left[inner], 0, 128)
            put(variants, start, size, roll(z, -1)[inner], 128, 256)

        return work

    blocks(3, 27 // N1, N1, narrow(lambda at, n: take(x0, at, n), k1, 0, x1))
    blocks(4, 25 // N2, N2, narrow(lambda at, n: taps(x1, at, n), k2, 1, x2))

    def conv_three(start, size):
        wide = size + 32
        z = dotn(taps(x2, start - 16, wide), k3[...])
        z = jnp.tanh(z + bias_ref[16:17, 0:256])
        ok = take(mask, start - 16, wide)
        inner = slice(16, 16 + size)
        for p in range(2):
            half = z[:, p * 128 : (p + 1) * 128] * ok
            left = jnp.where(low, roll(half, 1), half)
            right = jnp.where(low, half, roll(half, -1))
            put(x3, start, size, left[inner], p * 256, p * 256 + 128)
            put(x3, start, size, right[inner], p * 256 + 128, p * 256 + 256)
            put(a3, start, size, half[inner], p * 128, p * 128 + 128)

    blocks(5, 24 // N3, N3, conv_three)

    def conv_four(start, size):
        ok = take(mask, start, size)
        for p in range(2):
            lines = []
            for r in range(3):
                phase, by = row_of(p + r - 1)
                lines.append(take(x3, start + by, size, phase * 256, phase * 256 + 256))
            z = dotn(jnp.concatenate(lines, axis=1), k4[...])
            z = jnp.tanh(z + bias_ref[24:25, 0:512])
            for q in range(4):
                at = p * 512 + q * 128
                put(a4, start, size, z[:, q * 128 : (q + 1) * 128] * ok, at, at + 128)

    blocks(5, 24 // N4, N4, conv_four)

    size = ROWS * PITCH
    wide = size + 32
    at = OWN - 16
    side = []
    for low_lane in (384, 0):
        side.append(take(a4, at - PITCH, wide, 512 + low_lane, 640 + low_lane))
        side.append(take(a4, at, wide, low_lane, low_lane + 128))
        side.append(take(a4, at, wide, 512 + low_lane, 640 + low_lane))
        side.append(take(a4, at + PITCH, wide, low_lane, low_lane + 128))
    side = dotn(jnp.concatenate(side, axis=1), k5s[...])
    side = jnp.where(low, roll(side, 1), roll(side, -1))[16 : 16 + size]
    side = side.reshape(ROWS, PITCH, 128)[:, 16:48, :].reshape(ROWS * COLS, 128).T
    field = jnp.concatenate(
        [own(a4, 512, 1024, -1), own(a4, 0, 1024), own(a4, 0, 512, 1)], axis=1
    )
    z = dott(k5[...], field) + bias5_ref[:, 0:1]
    z = [z[0:64] + side[0:64], z[64:128], z[128:192], z[192:256] + side[64:128]]
    z = jnp.concatenate(
        [jnp.concatenate([z[q][:, g * 128 : (g + 1) * 128] for q in range(4)], axis=1) for g in range(4)],
        axis=0,
    )
    high = z.astype(BF)
    rest = (z - high.astype(F32)).astype(BF)
    z = dotn(jnp.concatenate([rest, high], axis=0), e_ref[...])
    z = z[0:256] + z[256:512]
    for g in range(4):
        for n in range(4):
            for p in range(4):
                fine_ref[16 * g + 4 * n + p] = z[
                    g * 64 + p * 16 : g * 64 + p * 16 + 16, n * 128 : (n + 1) * 128
                ]


def backward(
    scale,
    pos_ref,
    center_ref,
    rim_ref,
    mask,
    s5_ref,
    r5,
    r4,
    r3,
    r2,
    x0,
    x1,
    x2,
    x3,
    a3,
    a4,
    keep_ref,
    send_ref,
    c5,
    b4,
    b3,
    b2,
    b1,
    g_ref,
):
    low = low_half()
    clear_margins(((c5, 5, 29), (b4, 5, 29), (b3, 6, 27), (b2, 7, 27)))

    def cot_pair(n):
        lines = []
        for k in (2 * n + 1, 2 * n + 2):
            at = pl.ds(4 * (k - 5), 6)
            here = jnp.concatenate(
                [center_ref[at].reshape(96, 128), rim_ref[at].reshape(96, 128)], axis=1
            )
            lines += [here, jnp.zeros((32, 256), BF)]
        moved = dott(s5_ref[...], jnp.concatenate(lines, axis=0)).astype(BF)
        for half in range(2):
            at = pl.multiple_of((2 * n + 1 + half) * PITCH, 16)
            for u in range(6):
                c5[pl.ds(at, PITCH), u * 128 : (u + 1) * 128] = moved[
                    u * PITCH : (u + 1) * PITCH, half * 128 : (half + 1) * 128
                ]

    grouped(2, 14, GROUP5, cot_pair)

    def back_four(start, size):
        ok = take(mask, start, size)
        for q in range(4):
            z = dott(take(c5, start, size, q * 128, q * 128 + 384), r5[...])
            for p in range(2):
                at = p * 512 + q * 128
                z_p = z[:, p * 128 : (p + 1) * 128] * ok
                put(b4, start, size, z_p * slope(take(a4, start, size, at, at + 128)), at, at + 128)

    blocks(5, 24 // M4, M4, back_four)

    def back_three(start, size):
        wide = size + 32
        ok = take(mask, start, size)
        inner = slice(16, 16 + size)
        for p in range(2):
            lines = []
            for t in range(3):
                phase, by = row_of(p + t - 1)
                lines.append(take(b4, start - 16 + by, wide, phase * 512, phase * 512 + 512))
            z = dott(jnp.concatenate(lines, axis=1), r4[...])
            moved = jnp.where(low, roll(z[:, 128:256], -1), roll(z[:, 128:256], 1))
            z = (z[:, 0:128] + moved)[inner] * ok
            at = p * 128
            put(b3, start, size, z * slope(take(a3, start, size, at, at + 128)), at, at + 128)

    blocks(6, 21 // M3, M3, back_three)

    def back_narrow(src, weight, act, out):
        def work(start, size):
            wide = size + 32
            z = dott(taps(src, start - 16, wide), weight[...])
            pair = jnp.where(low, roll(z[:, 0:128], -1), z[:, 0:128])
            z = pair + lane_roll(pair, 64) + roll(z[:, 128:256], 1)
            z = z[16 : 16 + size] * take(mask, start, size)
            z = jnp.where(low, 0.0, z * slope(take(act, start, size, 0, 128)))
            put(out, start, size, z, 0, 128)

        return work

    blocks(7, 20 // M2, M2, back_narrow(b3, r3, x2, b2))
    blocks(8, 18 // M1, M1, back_narrow(b2, r2, x1, b1))

    g_ref[1344:, :] = jnp.zeros((g_ref.shape[0] - 1344, 256), F32)
    g_ref[1152:1344, 192:256] = jnp.zeros((192, 64), F32)

    back = own(b4, 0, 1024)
    sums4 = jnp.sum(back.astype(F32), axis=0, keepdims=True)
    back = back.T
    for r in range(3):
        total = None
        for p in range(2):
            phase, by = row_of(p + r - 1)
            field = own(x3, phase * 256, phase * 256 + 256, by // PITCH)
            term = dotn(back[p * 512 : (p + 1) * 512, :], field)
            total = term if total is None else total + term
        total = total[0:256, 0:192] + total[256:512, 64:256]
        g_ref[r * 192 : (r + 1) * 192, :] = total.T * scale
    sums4 = sums4[:, 0:512] + sums4[:, 512:1024]
    sums4 = sums4[:, 0:256] + sums4[:, 256:512]

    back = own(b3, 0, 256)
    sums3 = jnp.sum(back.astype(F32), axis=0, keepdims=True)
    back = back.T
    for r in range(3):
        total = dotn(back, own(x2, 0, 256, r - 1))[:, 0:192]
        g_ref[576 + r * 192 : 576 + (r + 1) * 192, :] = total.T * scale

    back = own(b2, 0, 128)
    sums2 = jnp.sum(back.astype(F32), axis=0, keepdims=True)
    back = back.T
    for r in range(3):
        total = dotn(back[64:128, :], own(x1, 0, 256, r - 1))
        g_ref[1152:1344, r * 64 : (r + 1) * 64] = total[:, 0:192].T * scale

    back = own(b1, 0, 128)
    sums1 = jnp.sum(back.astype(F32), axis=0, keepdims=True)
    back = back.T
    total = dotn(back[64:128, :], own(x0, 0, 384)).T * scale
    for s in range(3):
        g_ref[1152 + s * 48 : 1152 + (s + 1) * 48, 192:256] = total[s * 128 : s * 128 + 48, :]

    cot = own(c5, 0, 768)
    sums5 = jnp.sum(cot.astype(F32), axis=0, keepdims=True)
    cot = cot.T
    total = None
    for q in range(4):
        field = jnp.concatenate(
            [own(a4, q * 128, q * 128 + 128), own(a4, 512 + q * 128, 640 + q * 128)], axis=1
        )
        term = dotn(cot[q * 128 : q * 128 + 384, :], field)
        total = term if total is None else total + term
    total = total * scale
    for r in range(3):
        for s in range(3):
            sum_p = None
            for p in range(4):
                at = (2 - s) * 128 + (p + 2 - r) * 16
                term = total[at : at + 16, p * 64 : (p + 1) * 64]
                sum_p = term if sum_p is None else sum_p + term
            g_ref[1344 + s * 16 : 1344 + (s + 1) * 16, r * 64 : (r + 1) * 64] = sum_p

    sums5 = sums5[:, 128:256] + sums5[:, 256:384] + sums5[:, 384:512] + sums5[:, 512:640]
    five = sums5
    for t in range(1, 4):
        five = five + lane_roll(sums5, -16 * t)
    biases = [
        sums4 * scale,
        sums3 * scale,
        jnp.concatenate([sums2, sums1], axis=1) * scale,
        jnp.concatenate([five, jnp.zeros((1, 128), F32)], axis=1) * scale,
    ]
    for n, value in enumerate(biases):
        high = value.astype(BF).astype(F32)
        g_ref[1392 + 2 * n : 1393 + 2 * n, :] = high
        g_ref[1393 + 2 * n : 1394 + 2 * n, :] = value - high

    half = g_ref.shape[0] // 2
    core = pos_ref[2]
    keep_ref[...] = g_ref[pl.ds(pl.multiple_of(core * half, 16), half), :]
    send_ref[...] = g_ref[pl.ds(pl.multiple_of((1 - core) * half, 16), half), :].astype(BF)


def finish(chans, places, pos_ref, mine_ref, other_ref, turn3_ref, turn4_ref, g1, g2, g3, g4, g5, c1, c2, c3, c4, c5, full):
    half = full.shape[0] // 2
    size = half // places
    core = pos_ref[2]
    for b in range(places):
        at = pl.multiple_of(lax.bitwise_xor(pos_ref[3], b) * size, 16)
        here = pl.multiple_of(core * half + b * size, 16)
        there = pl.multiple_of((1 - core) * half + b * size, 16)
        full[pl.ds(here, size), :] = mine_ref[pl.ds(at, size), :]
        full[pl.ds(there, size), :] = other_ref[pl.ds(at, size), :]
    g4[...] = dotn(full[0:576, :], turn4_ref[...])
    g3[...] = dotn(full[576:1152, :], turn3_ref[...])
    for r in range(3):
        g2[r * 192 : (r + 1) * 192, :] = full[1152:1344, r * 64 : (r + 1) * 64].astype(F32)
        for s in range(3):
            at = 1152 + s * 48 + r * 16
            g1[r, s] = full[at : at + 16, 192:256].astype(F32)[:chans]
            at = 1344 + s * 16
            g5[r, s] = full[at : at + 16, r * 64 : (r + 1) * 64].astype(F32)[:chans]
    terms = full[1392:1408, :]
    turned4 = dotn(terms, turn4_ref[...])
    turned3 = dotn(terms, turn3_ref[...])
    terms = terms.astype(F32)
    c4[...] = turned4[0:1] + turned4[1:2]
    c3[...] = turned3[2:3] + turned3[3:4]
    sums = [None, None, terms[4:5] + terms[5:6], terms[6:7] + terms[7:8]]
    c2[...] = sums[2][:, 64:128]
    c1[...] = sums[2][:, 192:256]
    c5[...] = sums[3][:, 16 : 16 + chans]


def exchange(axis, first, last):
    count = lax.axis_size(axis)
    odd = lax.axis_index(axis) % 2 == 1
    even_swap = [(i, i ^ 1) for i in range(count)]
    odd_swap = [(i, ((i + 1) ^ 1) - 1) for i in range(1, count - 1)]
    one = lax.ppermute(jnp.where(odd, first, last), axis, even_swap)
    two = lax.ppermute(jnp.where(odd, last, first), axis, odd_swap)
    return jnp.where(odd, one, two), jnp.where(odd, two, one)


def swap(block, axis, flip):
    return lax.ppermute(block, axis, [(i, i ^ flip) for i in range(lax.axis_size(axis))])


def chip_window(coarse):
    gy, at = lax.axis_size("gy"), lax.axis_index("gy")
    chans, each, ny = coarse.shape
    cols = 2 * ny // gy
    block = jnp.pad(coarse.transpose(1, 0, 2), ((0, 0), (0, 16 - chans), (HALO, HALO)))
    other = swap(block, "gy", 1)
    block = jnp.where(
        at % 2 == 0, jnp.concatenate([block, other]), jnp.concatenate([other, block])
    )
    held = jnp.stack(
        [block[:, :, cols * c : cols * (c + 1) + 2 * HALO] for c in range(gy // 2)]
    )
    flip, bits = gy // 2, 0
    while flip > 1:
        half = held.shape[0] // 2
        high = (at & flip) != 0
        mine = jnp.where(high, held[half:], held[:half])
        other = swap(jnp.where(high, held[:half], held[half:]), "gy", flip)
        held = jnp.where(
            high,
            jnp.concatenate([other, mine], axis=1),
            jnp.concatenate([mine, other], axis=1),
        )
        flip, bits = flip // 2, bits + 1
    tail = (2 * each,) + held.shape[2:]
    held = held.reshape((2,) * bits + tail)
    held = held.transpose(tuple(reversed(range(bits))) + (bits, bits + 1, bits + 2))
    return held.reshape((gy * each,) + tail[1:])


def halo_lines(coarse, cotangent):
    n = FINE_HALO
    chans = coarse.shape[0]
    left, right = exchange(
        "gy", cotangent[:, :, :n].transpose(2, 0, 1), cotangent[:, :, -n:].transpose(2, 0, 1)
    )
    got = chip_window(coarse)
    wide = got.shape[2]
    cot = jnp.pad(cotangent.transpose(1, 0, 2), ((0, 0), (0, 16 - chans), (0, 0)))
    rim = jnp.concatenate([left.transpose(2, 1, 0), right.transpose(2, 1, 0)], axis=2)
    rim = jnp.pad(rim, ((0, 0), (0, 16 - chans), (0, 0)))

    def edge(cot_rows, coarse_rows):
        side = jnp.pad(got[coarse_rows], ((0, n - HALO), (0, 0), (0, 128 - 2 * n - wide)))
        side = jnp.concatenate([rim[cot_rows], side], axis=2)
        return jnp.concatenate([cot[cot_rows], side])

    first = edge(slice(0, n), slice(0, HALO))
    last = edge(slice(-n, None), slice(-HALO, None))
    above, below = exchange("gx", first, last)
    lanes = slice(2 * n, 2 * n + wide)
    whole = jnp.concatenate([above[n : n + HALO, :, lanes], got, below[n : n + HALO, :, lanes]])
    lines0 = jnp.pad(whole, ((2, 2), (0, 0), (0, 128 - wide)))
    rim = jnp.concatenate([above[n:, :, : 2 * n], rim, below[n:, :, : 2 * n]])
    center = jnp.concatenate([above[:n], cot, below[:n]])
    before = jnp.concatenate([rim[:, :, n:], center[:, :, 127:]], axis=2)
    rim = jnp.pad(rim, ((1, 9), (0, 0), (0, 64 - 2 * n)))
    before = jnp.pad(before, ((5, 5), (0, 0), (0, 63 - n)))
    return lines0, jnp.pad(center, ((1, 9), (0, 0), (0, 0))), jnp.concatenate([rim, before], axis=2)


def total_over_all(keep, send):
    gx, gy = lax.axis_size("gx"), lax.axis_size("gy")
    at_x = lax.axis_index("gx")

    def tree(terms):
        while len(terms) > 1:
            terms = [terms[n] + terms[n + 1] for n in range(0, len(terms), 2)]
        return terms[0]

    value = keep + swap(send, "gy", 1).astype(F32)
    size = value.shape[0] // gx

    def part(place):
        return lax.dynamic_slice_in_dim(value, place * size, size, 0)

    terms = [part(at_x)]
    for d in range(1, gx):
        terms.append(swap(part(at_x ^ d).astype(BF), "gx", d).astype(F32))
    block = tree(terms)
    flip = 2
    while flip < gy:
        block = block.astype(BF)
        block = block.astype(F32) + swap(block, "gy", flip).astype(F32)
        flip *= 2
    block = block.astype(BF)
    mine = jnp.concatenate([block] + [swap(block, "gx", d) for d in range(1, gx)])
    return mine, swap(mine, "gy", 1)


def local(
    coarse,
    weight_one,
    weight_two,
    weight_three,
    weight_four,
    weight_five,
    bias_one,
    bias_two,
    bias_three,
    bias_four,
    bias_five,
    cotangent,
):
    gx, gy = lax.axis_size("gx"), lax.axis_size("gy")
    chans = coarse.shape[0]
    tile_rows = coarse.shape[1] * gy
    tile_cols = coarse.shape[2] // gy
    assert (tile_rows, tile_cols) == (ROWS, COLS)
    at_x, at_y = lax.axis_index("gx"), lax.axis_index("gy")
    pos = jnp.stack([at_x * ROWS, at_y * COLS, at_y % 2, at_x]).astype(jnp.int32)
    extent = (ROWS * gx, COLS * gy)
    scale = float((16 * extent[0] * extent[1]) ** -0.5)

    smem = pl.BlockSpec(memory_space=pltpu.SMEM)
    vmem = pl.BlockSpec(memory_space=pltpu.VMEM)
    params = pltpu.CompilerParams(vmem_limit_bytes=LIMIT * 1024 * 1024)

    def near(value):
        return pltpu.with_memory_space_constraint(value, pltpu.VMEM)

    def buf(width, kind=BF):
        return pltpu.VMEM((CELLS, width), kind)

    lines0, center, rim = halo_lines(coarse, cotangent)
    shared = (
        buf(128, F32),
        pltpu.VMEM((6 * PITCH, 256), BF),
        pltpu.VMEM((256, 256), BF),
        pltpu.VMEM((256, 256), BF),
        pltpu.VMEM((256, 384), BF),
        pltpu.VMEM((256, 1536), BF),
        pltpu.VMEM((256, 768), BF),
        pltpu.VMEM((256, 384), BF),
        buf(384),
        buf(256),
        buf(256),
        buf(512),
        buf(256),
        buf(1024),
    )
    hbm = pl.BlockSpec(memory_space=pltpu.HBM)
    weights = (
        weight_one,
        weight_two.reshape(576, 64),
        weight_three.reshape(576, 256),
        weight_four.reshape(576, 256),
        weight_five.transpose(0, 1, 3, 2),
    )
    *fields, fine = pl.pallas_call(
        lambda *refs: forward(extent, *refs),
        out_shape=shared + (jax.ShapeDtypeStruct((4 * ROWS, 16, 4 * COLS), F32),),
        in_specs=[smem, vmem] + [hbm] * 5 + [vmem] * 5,
        out_specs=(vmem,) * 15,
        scratch_shapes=[
            pltpu.VMEM((32, 512), F32),
            pltpu.VMEM((256, 128), F32),
            pltpu.VMEM((3 * PITCH, 256), BF),
            pltpu.VMEM((512, 512), BF),
            pltpu.VMEM((384, 128), BF),
            pltpu.VMEM((768, 128), BF),
            pltpu.VMEM((768, 256), BF),
            pltpu.VMEM((768, 512), BF),
            pltpu.VMEM((256, 2048), BF),
            pltpu.VMEM((1024, 128), BF),
        ]
        + [pltpu.VMEM(w.shape, BF) for w in weights]
        + [pltpu.SemaphoreType.DMA((5,))],
        compiler_params=params,
        name="forward",
    )(
        pos,
        lines0,
        *[pltpu.with_memory_space_constraint(w, pltpu.HBM) for w in weights],
        bias_one.reshape(1, -1),
        bias_two.reshape(1, -1),
        bias_three.reshape(1, -1),
        bias_four.reshape(1, -1),
        bias_five.reshape(1, -1),
    )
    fields = [near(f) for f in fields]
    half = -(-TERMS // (32 * gx)) * 16 * gx
    keep, send = pl.pallas_call(
        lambda *refs: backward(scale, *refs),
        out_shape=(pltpu.VMEM((half, 256), F32), pltpu.VMEM((half, 256), BF)),
        in_specs=[smem] + [vmem] * 14,
        out_specs=(vmem,) * 2,
        scratch_shapes=[
            buf(768),
            buf(1024),
            buf(256),
            buf(128),
            buf(128),
            pltpu.VMEM((2 * half, 256), F32),
        ],
        compiler_params=params,
        name="backward",
    )(pos, center, rim, *fields[:2], *fields[4:])
    mine, other = total_over_all(keep, send)

    def out(*shape):
        return jax.ShapeDtypeStruct(shape, F32)

    g1, g2, g3, g4, g5, c1, c2, c3, c4, c5 = pl.pallas_call(
        lambda *refs: finish(chans, gx, *refs),
        out_shape=(
            out(3, 3, chans, 64),
            out(576, 64),
            out(576, 256),
            out(576, 256),
            out(3, 3, chans, 64),
            out(1, 64),
            out(1, 64),
            out(1, 256),
            out(1, 256),
            out(1, chans),
        ),
        in_specs=[smem] + [vmem] * 4,
        out_specs=(vmem,) * 10,
        scratch_shapes=[pltpu.VMEM((2 * half, 256), BF)],
        compiler_params=params,
        name="finish",
    )(pos, mine, other, fields[2], fields[3])
    return (
        fine.transpose(1, 0, 2)[:chans],
        g1,
        g2.reshape(3, 3, 64, 64),
        g3.reshape(3, 3, 64, 256),
        g4.reshape(3, 3, 64, 256),
        g5.transpose(0, 1, 3, 2),
        c1.reshape(64),
        c2.reshape(64),
        c3.reshape(256),
        c4.reshape(256),
        c5.reshape(chans),
    )


def solution(mesh):
    in_specs = (
        P(None, ("gx", "gy"), None),
        P(),
        P(),
        P(),
        P(),
        P(),
        P(),
        P(),
        P(),
        P(),
        P(),
        P(None, "gx", "gy"),
    )
    out_specs = (P(None, "gx", "gy"), P(), P(), P(), P(), P(), P(), P(), P(), P(), P())
    return jax.shard_map(local, mesh=mesh, in_specs=in_specs, out_specs=out_specs, check_vma=False)
```

```python
import jax
import jax.numpy as jnp
from jax import lax
from jax.experimental import pallas as pl
from jax.experimental.pallas import tpu as pltpu
from jax.sharding import PartitionSpec as P

BF = jnp.bfloat16
F32 = jnp.float32

ROWS, COLS, PITCH, CHUNKS = 16, 32, 48, 32
CELLS = PITCH * CHUNKS
OWN = PITCH * 8
HALO = 6
FINE_HALO = 12
TERMS = 1400
GROUP0, GROUP5 = 7, 6
N1, N2, N3, N4 = 3, 5, 3, 4
M4, M3, M2, M1 = 4, 3, 4, 3
LIMIT = 12


def dotn(left, right):
    return lax.dot_general(left, right, (((1,), (0,)), ((), ())), preferred_element_type=F32)


def dott(left, right):
    return lax.dot_general(left, right, (((1,), (1,)), ((), ())), preferred_element_type=F32)


def take(ref, start, count, low=0, high=None):
    high = ref.shape[1] if high is None else high
    if not isinstance(start, int):
        start = pl.multiple_of(start, 16)
    return ref[pl.ds(start, count), low:high]


def taps(ref, start, count):
    return jnp.concatenate([take(ref, start + d, count) for d in (-PITCH, 0, PITCH)], axis=1)


def own(ref, low, high, row=0):
    block = ref[OWN + PITCH * row : OWN + PITCH * (row + ROWS), low:high]
    return block.reshape(ROWS, PITCH, high - low)[:, 16:48, :].reshape(ROWS * COLS, high - low)


def roll(value, by):
    return pltpu.roll(value, by % value.shape[0], 0)


def lane_roll(value, by):
    return pltpu.roll(value, by % value.shape[1], 1)


def grouped(first, last, group, work):
    def step(n, _):
        for k in range(group):
            work(first + n * group + k)
        return 0

    lax.fori_loop(0, (last - first) // group, step, 0)


def blocks(first, chunks_each, count, work):
    size = chunks_each * PITCH
    if count == 1:
        work(first * PITCH, size)
        return

    def step(n, _):
        work(pl.multiple_of(first * PITCH + n * size, 16), size)
        return 0

    lax.fori_loop(0, count, step, 0)


def clear_margins(fields):
    for ref, first, last in fields:
        ref[0 : first * PITCH, :] = jnp.zeros((first * PITCH, ref.shape[1]), BF)
        if last < CHUNKS:
            ref[last * PITCH :, :] = jnp.zeros((CELLS - last * PITCH, ref.shape[1]), BF)


def put(ref, start, size, value, low, high):
    ref[pl.ds(start, size), low:high] = value.astype(BF)


def row_of(t):
    return t % 2, PITCH * (t // 2)


def low_half():
    return lax.broadcasted_iota(jnp.int32, (1, 128), 1) < 64


def slope(act):
    act = act.astype(F32)
    return 1.0 - act * act


def split_dot(value, perm):
    high = value.astype(BF)
    rest = value - high.astype(F32)
    middle = rest.astype(BF)
    low = (rest - middle.astype(F32)).astype(BF)
    return (dotn(low, perm) + dotn(middle, perm)) + dotn(high, perm)


def grid(rows, cols):
    return tuple(lax.broadcasted_iota(jnp.int32, (rows, cols), n) for n in (0, 1))


def one_hot(chosen):
    return jnp.where(chosen, 1.0, 0.0).astype(BF)


def select(core, s0_ref, s5_ref, turn3_ref, turn4_ref):
    m, lane = grid(PITCH, 256)
    for s in range(3):
        after = m + 31 + s + HALO + core * COLS
        here = m - 17 + s + HALO + core * COLS
        wanted = jnp.where(m < 8, after, jnp.where(here >= 0, here + 128, -1))
        s0_ref[s * PITCH : (s + 1) * PITCH, :] = one_hot(lane == wanted)
    for u in range(6):
        col = 4 * jnp.where(m < 8, m + 32, m - 16) + u - 1
        beyond = jnp.where(col - 128 < FINE_HALO, col + 64, -1)
        beyond = jnp.where(col == 127, 204, beyond)
        here = jnp.where(col < 0, col + 140, jnp.where(col < 128, col, col + 12))
        here = jnp.where(col < -FINE_HALO, -1, here)
        s5_ref[u * PITCH : (u + 1) * PITCH, :] = one_hot(lane == jnp.where(m < 8, beyond, here))
    new, old = grid(256, 256)
    turn3_ref[...] = one_hot(old == 4 * (new & 63) + 2 * (new >> 7) + 1 - ((new >> 6) & 1))
    turn4_ref[...] = one_hot(old == 4 * (new & 63) + 2 * ((new >> 6) & 1) + (new >> 7))


def small_terms(perms, small, bias_ref):
    b1_ref, b2_ref, b3_ref, b4_ref = small
    perm3, perm4 = perms

    def wide(value):
        return jnp.broadcast_to(value, (8, value.shape[1]))

    bias_ref[0:8, 0:128] = wide(jnp.concatenate([b1_ref[...]] * 2, axis=1))
    bias_ref[8:16, 0:128] = wide(jnp.concatenate([b2_ref[...]] * 2, axis=1))
    bias_ref[16:24, 0:256] = split_dot(wide(b3_ref[...]), perm3)
    four = split_dot(wide(b4_ref[...]), perm4)
    bias_ref[24:32, :] = jnp.concatenate([four, four], axis=1)


def arrange(perms, weights, there, back):
    w1_ref, w2_ref, w3_ref, w4_ref, w5_ref = weights
    k1, k2, k3, k4 = there
    r5, r4, r3, r2 = back
    perm3, perm4 = perms
    chans = w1_ref.shape[2]
    w3p = dotn(w3_ref[...], perm3).astype(BF)
    w4p = dotn(w4_ref[...], perm4).astype(BF)
    for ref in (k1, k2, k3, k4, r4, r3, r2):
        ref[...] = jnp.zeros(ref.shape, BF)
    for r in range(3):
        for s in range(3):
            at = s * 128 + r * 16
            k1[at : at + chans, :] = jnp.concatenate([w1_ref[r, s]] * 2, axis=1)
        part = w2_ref[r * 192 : (r + 1) * 192, :]
        k2[r * 256 : r * 256 + 192, :] = jnp.concatenate([part, part], axis=1)
        k3[r * 256 : r * 256 + 192, :] = w3p[r * 192 : (r + 1) * 192, :]
        for q in range(2):
            k4[r * 256 + q * 64 : r * 256 + q * 64 + 192, q * 256 : (q + 1) * 256] = w4p[
                r * 192 : (r + 1) * 192, :
            ]
        for s in range(3):
            t = 2 - r
            tap = (3 * r + s) * 64
            block = w3p[tap : tap + 64, :]
            r3[s * 64 : (s + 1) * 64, t * 256 : (t + 1) * 256] = block
            small = w2_ref[tap : tap + 64, :]
            r2[s * 64 : (s + 1) * 64, t * 128 + 64 : t * 128 + 128] = small
            if s == 2:
                r3[192:256, t * 256 : (t + 1) * 256] = block
                r2[192:256, t * 128 + 64 : t * 128 + 128] = small
            block = w4p[tap : tap + 64, :]
            for q in range(2):
                for q_src in range(2):
                    at = t * 512 + q_src * 256
                    if q - q_src + 1 == s:
                        r4[(1 - q) * 64 : (2 - q) * 64, at : at + 256] = block
                    if q_src == 1 - q and s == 2 - 2 * q:
                        r4[128 + (1 - q) * 64 : 128 + (2 - q) * 64, at : at + 256] = block
    columns = output_columns(w5_ref)
    for p in range(4):
        for v in range(3):
            r5[p * 64 : (p + 1) * 64, v * 128 : (v + 1) * 128] = lane_roll(
                columns[2 - v].T, 16 * p
            ).astype(BF)


def output_columns(w5_ref):
    gap_rows = jnp.zeros((16 - w5_ref.shape[2], 64), F32)
    columns = []
    for s in range(3):
        column = []
        for r in (2, 1, 0):
            column += [w5_ref[r, s].astype(F32), gap_rows]
        columns.append(jnp.concatenate(column + [jnp.zeros((80, 64), F32)], axis=0))
    return columns


def fine_field(kept_hbm, w5_ref, b5_ref, fine_ref, e_ref, k5, k5s, a4, sem):
    copy = pltpu.make_async_copy(kept_hbm, a4, sem)
    copy.start()
    low = low_half()
    cell, lane = grid(512, 512)
    e_ref[...] = one_hot(lane == ((cell >> 5) & 3) * 128 + (cell & 31) * 4 + (cell >> 7))
    k5[...] = jnp.zeros(k5.shape, BF)
    k5s[...] = jnp.zeros(k5s.shape, BF)
    columns = output_columns(w5_ref)
    w5 = [value.T for value in columns]
    columns = [value.astype(BF) for value in columns]
    empty = jnp.zeros((64, 64), BF)
    for t in range(6):
        at = 64 if t == 0 else (1536 if t == 5 else 512 + ((t - 1) // 2) * 512 + ((t - 1) % 2) * 64)
        side = 64 if t == 0 else (384 if t == 5 else 128 + ((t - 1) // 2) * 128 + ((t - 1) % 2) * 64)
        for b in range(3):
            p = t - 2 + b
            if not 0 <= p < 4:
                continue
            for src in range(4):
                for q in range(max(src - 1, 0), min(src + 1, 3) + 1):
                    k5[q * 64 + p * 16 : q * 64 + p * 16 + 16, at + src * 128 : at + src * 128 + 64] = (
                        columns[src - q + 1][b * 16 : b * 16 + 16, :]
                    )
        rows = [lane_roll(w5[s], 16 * (t - 2)).astype(BF)[:, :64] for s in (0, 2)]
        k5s[side : side + 64, :] = jnp.concatenate([rows[0], empty], axis=1)
        k5s[512 + side : 512 + side + 64, :] = jnp.concatenate([empty, rows[1]], axis=1)
    chans = b5_ref.shape[1]
    five = jnp.concatenate([b5_ref[...], jnp.zeros((1, 128 - chans), F32)], axis=1)
    five = sum(lane_roll(five, 16 * n) for n in range(8))
    five = jnp.concatenate([jnp.broadcast_to(five, (128, 128)).T] * 2, axis=0)
    copy.wait()
    size = ROWS * PITCH
    wide = size + 32
    at = OWN - 16
    side = []
    for low_lane in (384, 0):
        side.append(take(a4, at - PITCH, wide, 512 + low_lane, 640 + low_lane))
        side.append(take(a4, at, wide, low_lane, low_lane + 128))
        side.append(take(a4, at, wide, 512 + low_lane, 640 + low_lane))
        side.append(take(a4, at + PITCH, wide, low_lane, low_lane + 128))
    side = dotn(jnp.concatenate(side, axis=1), k5s[...])
    side = jnp.where(low, roll(side, 1), roll(side, -1))[16 : 16 + size]
    side = side.reshape(ROWS, PITCH, 128)[:, 16:48, :].reshape(ROWS * COLS, 128).T
    field = jnp.concatenate(
        [own(a4, 512, 1024, -1), own(a4, 0, 1024), own(a4, 0, 512, 1)], axis=1
    )
    z = dott(k5[...], field) + five[:, 0:1]
    z = [z[0:64] + side[0:64], z[64:128], z[128:192], z[192:256] + side[64:128]]
    z = jnp.concatenate(
        [jnp.concatenate([z[q][:, g * 128 : (g + 1) * 128] for q in range(4)], axis=1) for g in range(4)],
        axis=0,
    )
    high = z.astype(BF)
    rest = (z - high.astype(F32)).astype(BF)
    z = dotn(jnp.concatenate([rest, high], axis=0), e_ref[...])
    z = z[0:256] + z[256:512]
    for g in range(4):
        for n in range(4):
            for p in range(4):
                fine_ref[16 * g + 4 * n + p] = z[
                    g * 64 + p * 16 : g * 64 + p * 16 + 16, n * 128 : (n + 1) * 128
                ]


def in_plane(extent, pos_ref, mask):
    row0 = pos_ref[0]
    col0 = pos_ref[1]
    m = lax.broadcasted_iota(jnp.int32, (PITCH, 128), 0)
    col = col0 + jnp.where(m < 8, m + 32, m - 16)
    col_ok = jnp.logical_and(col >= 0, col < extent[1])
    for k in range(CHUNKS):
        row = row0 + jnp.where(m < 8, k - 9, k - 8)
        ok = jnp.logical_and(col_ok, jnp.logical_and(row >= 0, row < extent[0]))
        mask[k * PITCH : (k + 1) * PITCH, :] = jnp.where(ok, 1.0, 0.0)


def forward(
    extent,
    pos_ref,
    window_ref,
    above_ref,
    below_ref,
    w1_hbm,
    w2_hbm,
    w3_hbm,
    w4_hbm,
    w5_hbm,
    b1_ref,
    b2_ref,
    b3_ref,
    b4_ref,
    mask,
    s5_ref,
    turn3_ref,
    turn4_ref,
    r5,
    r4,
    r3,
    r2,
    x0,
    x1,
    x2,
    x3,
    a3,
    a4,
    bias_ref,
    s0_ref,
    k1,
    k2,
    k3,
    k4,
    w1_ref,
    w2_ref,
    w3_ref,
    w4_ref,
    w5_ref,
    dx_ref,
    sems,
):
    copies = [
        pltpu.make_async_copy(src, dst, sems.at[n])
        for n, (src, dst) in enumerate(
            (
                (w1_hbm, w1_ref),
                (w2_hbm, w2_ref),
                (w3_hbm, w3_ref),
                (w4_hbm, w4_ref),
                (w5_hbm, w5_ref),
            )
        )
    ]
    for copy in copies:
        copy.start()
    small = (b1_ref, b2_ref, b3_ref, b4_ref)
    select(pos_ref[2], s0_ref, s5_ref, turn3_ref, turn4_ref)
    in_plane(extent, pos_ref, mask)
    low = low_half()
    clear_margins(((x0, 2, 30), (x1, 3, 30), (x2, 4, 29), (x3, 5, 29), (a4, 5, 29)))

    lane = lax.broadcasted_iota(jnp.int32, (1, 128), 1)
    dx_ref[0:2] = jnp.zeros((2, 16, 128), BF)
    dx_ref[8:24] = window_ref[...]
    dx_ref[30:32] = jnp.zeros((2, 16, 128), BF)
    for ref, at in ((above_ref, 2), (below_ref, 24)):
        sent = ref[FINE_HALO : FINE_HALO + HALO].reshape(HALO * 16, 128).astype(F32)
        sent = jnp.where(lane < 2 * COLS + 2 * HALO, lane_roll(sent, -2 * FINE_HALO), 0.0)
        dx_ref[at : at + HALO] = sent.astype(BF).reshape(HALO, 16, 128)

    def coarse_pair(n):
        lines = []
        for k in (2 * n, 2 * n + 1):
            before = dx_ref[pl.ds(k - 2, 3)].reshape(48, 128)
            here = dx_ref[pl.ds(k - 1, 3)].reshape(48, 128)
            lines += [jnp.concatenate([before, here], axis=1), jnp.zeros((80, 256), BF)]
        moved = dott(s0_ref[...], jnp.concatenate(lines, axis=0)).astype(BF)
        for half in range(2):
            at = pl.multiple_of((2 * n + half) * PITCH, 16)
            for s in range(3):
                x0[pl.ds(at, PITCH), s * 128 : (s + 1) * 128] = moved[
                    s * PITCH : (s + 1) * PITCH, half * 128 : (half + 1) * 128
                ]

    grouped(1, 15, GROUP0, coarse_pair)
    for copy in copies:
        copy.wait()
    perms = (turn3_ref[...].T, turn4_ref[...].T)
    small_terms(perms, small, bias_ref)
    arrange(
        perms,
        (w1_ref, w2_ref, w3_ref, w4_ref, w5_ref),
        (k1, k2, k3, k4),
        (r5, r4, r3, r2),
    )

    def narrow(read, weight, bias_at, variants):
        def work(start, size):
            wide = size + 32
            z = dotn(read(start - 16, wide), weight[...])
            z = jnp.tanh(z + bias_ref[8 * bias_at : 8 * bias_at + 1, 0:128])
            z = z * take(mask, start - 16, wide)
            inner = slice(16, 16 + size)
            left = jnp.where(low, roll(z, 1), z)
            put(variants, start, size, left[inner], 0, 128)
            put(variants, start, size, roll(z, -1)[inner], 128, 256)

        return work

    blocks(3, 27 // N1, N1, narrow(lambda at, n: take(x0, at, n), k1, 0, x1))
    blocks(4, 25 // N2, N2, narrow(lambda at, n: taps(x1, at, n), k2, 1, x2))

    def conv_three(start, size):
        wide = size + 32
        z = dotn(taps(x2, start - 16, wide), k3[...])
        z = jnp.tanh(z + bias_ref[16:17, 0:256])
        ok = take(mask, start - 16, wide)
        inner = slice(16, 16 + size)
        for p in range(2):
            half = z[:, p * 128 : (p + 1) * 128] * ok
            left = jnp.where(low, roll(half, 1), half)
            right = jnp.where(low, half, roll(half, -1))
            put(x3, start, size, left[inner], p * 256, p * 256 + 128)
            put(x3, start, size, right[inner], p * 256 + 128, p * 256 + 256)
            put(a3, start, size, half[inner], p * 128, p * 128 + 128)

    blocks(5, 24 // N3, N3, conv_three)

    def conv_four(start, size):
        ok = take(mask, start, size)
        for p in range(2):
            lines = []
            for r in range(3):
                phase, by = row_of(p + r - 1)
                lines.append(take(x3, start + by, size, phase * 256, phase * 256 + 256))
            z = dotn(jnp.concatenate(lines, axis=1), k4[...])
            z = jnp.tanh(z + bias_ref[24:25, 0:512])
            for q in range(4):
                at = p * 512 + q * 128
                put(a4, start, size, z[:, q * 128 : (q + 1) * 128] * ok, at, at + 128)

    blocks(5, 24 // N4, N4, conv_four)


def backward(
    scale,
    pos_ref,
    above_ref,
    below_ref,
    cot_ref,
    sides_ref,
    mask,
    s5_ref,
    r5,
    r4,
    r3,
    r2,
    x0,
    x1,
    x2,
    x3,
    a3,
    a4,
    keep_ref,
    send_ref,
    kept_hbm,
    c5,
    b4,
    b3,
    b2,
    b1,
    g_ref,
    center_ref,
    rim_ref,
    sem,
):
    kept = pltpu.make_async_copy(a4, kept_hbm, sem)
    kept.start()
    low = low_half()
    clear_margins(((c5, 5, 29), (b4, 5, 29), (b3, 6, 27), (b2, 7, 27)))

    n = FINE_HALO
    rows = 4 * ROWS
    lane = lax.broadcasted_iota(jnp.int32, (1, 128), 1)
    for ref, inside, parts in (
        (center_ref, cot_ref, slice(0, n)),
        (rim_ref, sides_ref, slice(n, 2 * n)),
    ):
        ref[0] = jnp.zeros((16, 128), BF)
        ref[1 : n + 1] = above_ref[parts]
        ref[n + 1 : n + 1 + rows] = inside[...]
        ref[n + 1 + rows : 2 * n + 1 + rows] = below_ref[parts]
        ref[2 * n + 1 + rows :] = jnp.zeros((9, 16, 128), BF)
    count = (2 * n + 10 + rows) * 16
    sides = rim_ref[...].reshape(count, 128).astype(F32)
    before = lane_roll(sides[: count - 64], 64 - n)
    corner = lane_roll(center_ref[...].reshape(count, 128).astype(F32)[: count - 64], 77)
    before = jnp.where(lane < 64 + n, before, corner)
    before = jnp.concatenate([jnp.zeros((64, 128), F32), before], axis=0)
    sides = jnp.where(lane < 2 * n, sides, jnp.where(lane < 64, 0.0, before))
    sides = jnp.where(lane < 65 + n, sides, 0.0)
    rim_ref[...] = sides.astype(BF).reshape(count // 16, 16, 128)

    def cot_pair(n):
        lines = []
        for k in (2 * n + 1, 2 * n + 2):
            at = pl.ds(4 * (k - 5), 6)
            here = jnp.concatenate(
                [center_ref[at].reshape(96, 128), rim_ref[at].reshape(96, 128)], axis=1
            )
            lines += [here, jnp.zeros((32, 256), BF)]
        moved = dott(s5_ref[...], jnp.concatenate(lines, axis=0)).astype(BF)
        for half in range(2):
            at = pl.multiple_of((2 * n + 1 + half) * PITCH, 16)
            for u in range(6):
                c5[pl.ds(at, PITCH), u * 128 : (u + 1) * 128] = moved[
                    u * PITCH : (u + 1) * PITCH, half * 128 : (half + 1) * 128
                ]

    grouped(2, 14, GROUP5, cot_pair)

    def back_four(start, size):
        ok = take(mask, start, size)
        for q in range(4):
            z = dott(take(c5, start, size, q * 128, q * 128 + 384), r5[...])
            for p in range(2):
                at = p * 512 + q * 128
                z_p = z[:, p * 128 : (p + 1) * 128] * ok
                put(b4, start, size, z_p * slope(take(a4, start, size, at, at + 128)), at, at + 128)

    blocks(5, 24 // M4, M4, back_four)

    def back_three(start, size):
        wide = size + 32
        ok = take(mask, start, size)
        inner = slice(16, 16 + size)
        for p in range(2):
            lines = []
            for t in range(3):
                phase, by = row_of(p + t - 1)
                lines.append(take(b4, start - 16 + by, wide, phase * 512, phase * 512 + 512))
            z = dott(jnp.concatenate(lines, axis=1), r4[...])
            moved = jnp.where(low, roll(z[:, 128:256], -1), roll(z[:, 128:256], 1))
            z = (z[:, 0:128] + moved)[inner] * ok
            at = p * 128
            put(b3, start, size, z * slope(take(a3, start, size, at, at + 128)), at, at + 128)

    blocks(6, 21 // M3, M3, back_three)

    def back_narrow(src, weight, act, out):
        def work(start, size):
            wide = size + 32
            z = dott(taps(src, start - 16, wide), weight[...])
            pair = jnp.where(low, roll(z[:, 0:128], -1), z[:, 0:128])
            z = pair + lane_roll(pair, 64) + roll(z[:, 128:256], 1)
            z = z[16 : 16 + size] * take(mask, start, size)
            z = jnp.where(low, 0.0, z * slope(take(act, start, size, 0, 128)))
            put(out, start, size, z, 0, 128)

        return work

    blocks(7, 20 // M2, M2, back_narrow(b3, r3, x2, b2))
    blocks(8, 18 // M1, M1, back_narrow(b2, r2, x1, b1))

    g_ref[1344:, :] = jnp.zeros((g_ref.shape[0] - 1344, 256), F32)
    g_ref[1152:1344, 192:256] = jnp.zeros((192, 64), F32)

    back = own(b4, 0, 1024)
    sums4 = jnp.sum(back.astype(F32), axis=0, keepdims=True)
    back = back.T
    for r in range(3):
        total = None
        for p in range(2):
            phase, by = row_of(p + r - 1)
            field = own(x3, phase * 256, phase * 256 + 256, by // PITCH)
            term = dotn(back[p * 512 : (p + 1) * 512, :], field)
            total = term if total is None else total + term
        total = total[0:256, 0:192] + total[256:512, 64:256]
        g_ref[r * 192 : (r + 1) * 192, :] = total.T * scale
    sums4 = sums4[:, 0:512] + sums4[:, 512:1024]
    sums4 = sums4[:, 0:256] + sums4[:, 256:512]

    back = own(b3, 0, 256)
    sums3 = jnp.sum(back.astype(F32), axis=0, keepdims=True)
    back = back.T
    for r in range(3):
        total = dotn(back, own(x2, 0, 256, r - 1))[:, 0:192]
        g_ref[576 + r * 192 : 576 + (r + 1) * 192, :] = total.T * scale

    back = own(b2, 0, 128)
    sums2 = jnp.sum(back.astype(F32), axis=0, keepdims=True)
    back = back.T
    for r in range(3):
        total = dotn(back[64:128, :], own(x1, 0, 256, r - 1))
        g_ref[1152:1344, r * 64 : (r + 1) * 64] = total[:, 0:192].T * scale

    back = own(b1, 0, 128)
    sums1 = jnp.sum(back.astype(F32), axis=0, keepdims=True)
    back = back.T
    total = dotn(back[64:128, :], own(x0, 0, 384)).T * scale
    for s in range(3):
        g_ref[1152 + s * 48 : 1152 + (s + 1) * 48, 192:256] = total[s * 128 : s * 128 + 48, :]

    cot = own(c5, 0, 768)
    sums5 = jnp.sum(cot.astype(F32), axis=0, keepdims=True)
    cot = cot.T
    total = None
    for q in range(4):
        field = jnp.concatenate(
            [own(a4, q * 128, q * 128 + 128), own(a4, 512 + q * 128, 640 + q * 128)], axis=1
        )
        term = dotn(cot[q * 128 : q * 128 + 384, :], field)
        total = term if total is None else total + term
    total = total * scale
    for r in range(3):
        for s in range(3):
            sum_p = None
            for p in range(4):
                at = (2 - s) * 128 + (p + 2 - r) * 16
                term = total[at : at + 16, p * 64 : (p + 1) * 64]
                sum_p = term if sum_p is None else sum_p + term
            g_ref[1344 + s * 16 : 1344 + (s + 1) * 16, r * 64 : (r + 1) * 64] = sum_p

    sums5 = sums5[:, 128:256] + sums5[:, 256:384] + sums5[:, 384:512] + sums5[:, 512:640]
    five = sums5
    for t in range(1, 4):
        five = five + lane_roll(sums5, -16 * t)
    biases = [
        sums4 * scale,
        sums3 * scale,
        jnp.concatenate([sums2, sums1], axis=1) * scale,
        jnp.concatenate([five, jnp.zeros((1, 128), F32)], axis=1) * scale,
    ]
    for n, value in enumerate(biases):
        high = value.astype(BF).astype(F32)
        g_ref[1392 + 2 * n : 1393 + 2 * n, :] = high
        g_ref[1393 + 2 * n : 1394 + 2 * n, :] = value - high

    half = g_ref.shape[0] // 2
    core = pos_ref[2]
    keep_ref[...] = g_ref[pl.ds(pl.multiple_of(core * half, 16), half), :]
    send_ref[...] = g_ref[pl.ds(pl.multiple_of((1 - core) * half, 16), half), :].astype(BF)
    kept.wait()


def finish(chans, places, pos_ref, mine_ref, other_ref, turn3_ref, turn4_ref, g1, g2, g3, g4, g5, c1, c2, c3, c4, c5, full):
    half = full.shape[0] // 2
    size = half // places
    core = pos_ref[2]
    for b in range(places):
        at = pl.multiple_of(lax.bitwise_xor(pos_ref[3], b) * size, 16)
        here = pl.multiple_of(core * half + b * size, 16)
        there = pl.multiple_of((1 - core) * half + b * size, 16)
        full[pl.ds(here, size), :] = mine_ref[pl.ds(at, size), :]
        full[pl.ds(there, size), :] = other_ref[pl.ds(at, size), :]
    g4[...] = dotn(full[0:576, :], turn4_ref[...])
    g3[...] = dotn(full[576:1152, :], turn3_ref[...])
    for r in range(3):
        g2[r * 192 : (r + 1) * 192, :] = full[1152:1344, r * 64 : (r + 1) * 64].astype(F32)
        for s in range(3):
            at = 1152 + s * 48 + r * 16
            g1[r, s] = full[at : at + 16, 192:256].astype(F32)[:chans]
            at = 1344 + s * 16
            g5[r, s] = full[at : at + 16, r * 64 : (r + 1) * 64].astype(F32)[:chans]
    terms = full[1392:1408, :]
    turned4 = dotn(terms, turn4_ref[...])
    turned3 = dotn(terms, turn3_ref[...])
    terms = terms.astype(F32)
    c4[...] = turned4[0:1] + turned4[1:2]
    c3[...] = turned3[2:3] + turned3[3:4]
    sums = [None, None, terms[4:5] + terms[5:6], terms[6:7] + terms[7:8]]
    c2[...] = sums[2][:, 64:128]
    c1[...] = sums[2][:, 192:256]
    c5[...] = sums[3][:, 16 : 16 + chans]


def exchange(axis, first, last):
    count = lax.axis_size(axis)
    odd = lax.axis_index(axis) % 2 == 1
    even_swap = [(i, i ^ 1) for i in range(count)]
    odd_swap = [(i, ((i + 1) ^ 1) - 1) for i in range(1, count - 1)]
    one = lax.ppermute(jnp.where(odd, first, last), axis, even_swap)
    two = lax.ppermute(jnp.where(odd, last, first), axis, odd_swap)
    return jnp.where(odd, one, two), jnp.where(odd, two, one)


def swap(block, axis, flip):
    return lax.ppermute(block, axis, [(i, i ^ flip) for i in range(lax.axis_size(axis))])


def chip_window(coarse, beside):
    gy, at = lax.axis_size("gy"), lax.axis_index("gy")
    chans, each, ny = coarse.shape
    cols = 2 * ny // gy
    block = jnp.pad(coarse.transpose(1, 0, 2), ((0, 0), (0, 16 - chans), (HALO, HALO)))
    other = swap(block, "gy", 1)
    block = jnp.where(
        at % 2 == 0, jnp.concatenate([block, other]), jnp.concatenate([other, block])
    )
    held = jnp.stack(
        [block[:, :, cols * c : cols * (c + 1) + 2 * HALO] for c in range(gy // 2)]
    )
    flip, bits = gy // 2, 0
    while flip > 1:
        half = held.shape[0] // 2
        high = (at & flip) != 0
        mine = jnp.where(high, held[half:], held[:half])
        other = swap(jnp.where(high, held[:half], held[half:]), "gy", flip)
        held = jnp.where(
            high,
            jnp.concatenate([other, mine], axis=1),
            jnp.concatenate([mine, other], axis=1),
        )
        flip, bits = flip // 2, bits + 1
        if bits == 1:
            held, beside = lax.optimization_barrier((held, beside))
    tail = (2 * each,) + held.shape[2:]
    held = held.reshape((2,) * bits + tail)
    held = held.transpose(tuple(reversed(range(bits))) + (bits, bits + 1, bits + 2))
    return held.reshape((gy * each,) + tail[1:]), beside


def halo_pieces(coarse, cotangent):
    n = FINE_HALO
    spare = 16 - coarse.shape[0]
    edges = (cotangent[:, :, :n].transpose(2, 0, 1), cotangent[:, :, -n:].transpose(2, 0, 1))
    got, edges = chip_window(coarse, edges)
    left, right = exchange("gy", *edges)
    wide = got.shape[2]
    cot = jnp.pad(cotangent.transpose(1, 0, 2), ((0, 0), (0, spare), (0, 0)))
    rim = jnp.concatenate([left.transpose(2, 1, 0), right.transpose(2, 1, 0)], axis=2)
    rim = jnp.pad(rim, ((0, 0), (0, spare), (0, 0)))

    def edge(cot_rows, coarse_rows):
        side = jnp.pad(got[coarse_rows], ((0, n - HALO), (0, 0), (0, 128 - 2 * n - wide)))
        side = jnp.concatenate([rim[cot_rows], side], axis=2)
        return jnp.concatenate([cot[cot_rows], side])

    first = edge(slice(0, n), slice(0, HALO))
    last = edge(slice(-n, None), slice(-HALO, None))
    above, below = exchange("gx", first, last)
    got = jnp.pad(got, ((0, 0), (0, 0), (0, 128 - wide)))
    return got, above, below, cot, jnp.pad(rim, ((0, 0), (0, 0), (0, 128 - 2 * n)))


def total_over_all(keep, send, beside):
    gx, gy = lax.axis_size("gx"), lax.axis_size("gy")
    at_x = lax.axis_index("gx")

    def tree(terms):
        while len(terms) > 1:
            terms = [terms[n] + terms[n + 1] for n in range(0, len(terms), 2)]
        return terms[0]

    value = keep + swap(send, "gy", 1).astype(F32)
    size = value.shape[0] // gx

    def part(place):
        return lax.dynamic_slice_in_dim(value, place * size, size, 0)

    terms = [swap(part(at_x ^ d).astype(BF), "gx", d) for d in range(1, gx)]
    terms, beside = lax.optimization_barrier((terms, beside))
    block = tree([part(at_x)] + [term.astype(F32) for term in terms])
    flip = 2
    while flip < gy:
        block = block.astype(BF)
        block = block.astype(F32) + swap(block, "gy", flip).astype(F32)
        flip *= 2
    block = block.astype(BF)
    mine = jnp.concatenate([block] + [swap(block, "gx", d) for d in range(1, gx)])
    return mine, swap(mine, "gy", 1), beside


def local(
    coarse,
    weight_one,
    weight_two,
    weight_three,
    weight_four,
    weight_five,
    bias_one,
    bias_two,
    bias_three,
    bias_four,
    bias_five,
    cotangent,
):
    gx, gy = lax.axis_size("gx"), lax.axis_size("gy")
    chans = coarse.shape[0]
    tile_rows = coarse.shape[1] * gy
    tile_cols = coarse.shape[2] // gy
    assert (tile_rows, tile_cols) == (ROWS, COLS)
    at_x, at_y = lax.axis_index("gx"), lax.axis_index("gy")
    pos = jnp.stack([at_x * ROWS, at_y * COLS, at_y % 2, at_x]).astype(jnp.int32)
    extent = (ROWS * gx, COLS * gy)
    scale = float((16 * extent[0] * extent[1]) ** -0.5)

    smem = pl.BlockSpec(memory_space=pltpu.SMEM)
    vmem = pl.BlockSpec(memory_space=pltpu.VMEM)
    params = pltpu.CompilerParams(vmem_limit_bytes=LIMIT * 1024 * 1024)

    def near(value):
        return pltpu.with_memory_space_constraint(value, pltpu.VMEM)

    def buf(width, kind=BF):
        return pltpu.VMEM((CELLS, width), kind)

    window, above, below, cot, rim = halo_pieces(coarse, cotangent)
    shared = (
        buf(128, F32),
        pltpu.VMEM((6 * PITCH, 256), BF),
        pltpu.VMEM((256, 256), BF),
        pltpu.VMEM((256, 256), BF),
        pltpu.VMEM((256, 384), BF),
        pltpu.VMEM((256, 1536), BF),
        pltpu.VMEM((256, 768), BF),
        pltpu.VMEM((256, 384), BF),
        buf(384),
        buf(256),
        buf(256),
        buf(512),
        buf(256),
        buf(1024),
    )
    hbm = pl.BlockSpec(memory_space=pltpu.HBM)
    weights = (
        weight_one,
        weight_two.reshape(576, 64),
        weight_three.reshape(576, 256),
        weight_four.reshape(576, 256),
        weight_five.transpose(0, 1, 3, 2),
    )
    fields = pl.pallas_call(
        lambda *refs: forward(extent, *refs),
        out_shape=shared,
        in_specs=[smem] + [vmem] * 3 + [hbm] * 5 + [vmem] * 4,
        out_specs=(vmem,) * 14,
        scratch_shapes=[
            pltpu.VMEM((32, 512), F32),
            pltpu.VMEM((3 * PITCH, 256), BF),
            pltpu.VMEM((384, 128), BF),
            pltpu.VMEM((768, 128), BF),
            pltpu.VMEM((768, 256), BF),
            pltpu.VMEM((768, 512), BF),
        ]
        + [pltpu.VMEM(w.shape, BF) for w in weights]
        + [pltpu.VMEM((32, 16, 128), BF)]
        + [pltpu.SemaphoreType.DMA((5,))],
        compiler_params=params,
        name="forward",
    )(
        pos,
        window,
        above,
        below,
        *[pltpu.with_memory_space_constraint(w, pltpu.HBM) for w in weights],
        bias_one.reshape(1, -1),
        bias_two.reshape(1, -1),
        bias_three.reshape(1, -1),
        bias_four.reshape(1, -1),
    )
    fields = [near(f) for f in fields]
    half = -(-TERMS // (32 * gx)) * 16 * gx
    keep, send, kept = pl.pallas_call(
        lambda *refs: backward(scale, *refs),
        out_shape=(
            pltpu.VMEM((half, 256), F32),
            pltpu.VMEM((half, 256), BF),
            pltpu.HBM((CELLS, 1024), BF),
        ),
        in_specs=[smem] + [vmem] * 16,
        out_specs=(vmem, vmem, hbm),
        scratch_shapes=[
            buf(768),
            buf(1024),
            buf(256),
            buf(128),
            buf(128),
            pltpu.VMEM((2 * half, 256), F32),
            pltpu.VMEM((98, 16, 128), BF),
            pltpu.VMEM((98, 16, 128), BF),
            pltpu.SemaphoreType.DMA,
        ],
        compiler_params=params,
        name="backward",
    )(pos, above, below, cot, rim, *fields[:2], *fields[4:])
    fine = pl.pallas_call(
        fine_field,
        out_shape=jax.ShapeDtypeStruct((4 * ROWS, 16, 4 * COLS), F32),
        in_specs=[hbm, vmem, vmem],
        out_specs=vmem,
        scratch_shapes=[
            pltpu.VMEM((512, 512), BF),
            pltpu.VMEM((256, 2048), BF),
            pltpu.VMEM((1024, 128), BF),
            buf(1024),
            pltpu.SemaphoreType.DMA,
        ],
        compiler_params=params,
        name="fine",
    )(pltpu.with_memory_space_constraint(kept, pltpu.HBM), weights[4], bias_five.reshape(1, -1))
    mine, other, fine = total_over_all(keep, send, fine)

    def out(*shape):
        return jax.ShapeDtypeStruct(shape, F32)

    g1, g2, g3, g4, g5, c1, c2, c3, c4, c5 = pl.pallas_call(
        lambda *refs: finish(chans, gx, *refs),
        out_shape=(
            out(3, 3, chans, 64),
            out(576, 64),
            out(576, 256),
            out(576, 256),
            out(3, 3, chans, 64),
            out(1, 64),
            out(1, 64),
            out(1, 256),
            out(1, 256),
            out(1, chans),
        ),
        in_specs=[smem] + [vmem] * 4,
        out_specs=(vmem,) * 10,
        scratch_shapes=[pltpu.VMEM((2 * half, 256), BF)],
        compiler_params=params,
        name="finish",
    )(pos, mine, other, fields[2], fields[3])
    return (
        fine.transpose(1, 0, 2)[:chans],
        g1,
        g2.reshape(3, 3, 64, 64),
        g3.reshape(3, 3, 64, 256),
        g4.reshape(3, 3, 64, 256),
        g5.transpose(0, 1, 3, 2),
        c1.reshape(64),
        c2.reshape(64),
        c3.reshape(256),
        c4.reshape(256),
        c5.reshape(chans),
    )


def solution(mesh):
    in_specs = (
        P(None, ("gx", "gy"), None),
        P(),
        P(),
        P(),
        P(),
        P(),
        P(),
        P(),
        P(),
        P(),
        P(),
        P(None, "gx", "gy"),
    )
    out_specs = (P(None, "gx", "gy"), P(), P(), P(), P(), P(), P(), P(), P(), P(), P())
    return jax.shard_map(local, mesh=mesh, in_specs=in_specs, out_specs=out_specs, check_vma=False)
```

```python
import jax
import jax.numpy as jnp
from jax import lax
from jax.experimental import pallas as pl
from jax.experimental.pallas import tpu as pltpu
from jax.sharding import PartitionSpec as P

BF = jnp.bfloat16
F32 = jnp.float32

ROWS, COLS, PITCH, CHUNKS = 16, 32, 48, 32
CELLS = PITCH * CHUNKS
OWN = PITCH * 8
NEAR = OWN - PITCH - 16
NEAR_CELLS = PITCH * (ROWS + 2) + 32
HALO = 6
FINE_HALO = 12
TERMS = 1400
GROUP0, GROUP5 = 7, 12
N1, N2, N3, N4 = 1, 1, 1, 1
M4, M3, M2, M1 = 1, 1, 1, 1
LIMIT = 16


def dotn(left, right):
    return lax.dot_general(left, right, (((1,), (0,)), ((), ())), preferred_element_type=F32)


def dott(left, right):
    return lax.dot_general(left, right, (((1,), (1,)), ((), ())), preferred_element_type=F32)


def take(ref, start, count, low=0, high=None):
    high = ref.shape[1] if high is None else high
    if not isinstance(start, int):
        start = pl.multiple_of(start, 16)
    return ref[pl.ds(start, count), low:high]


def taps(ref, start, count):
    return jnp.concatenate([take(ref, start + d, count) for d in (-PITCH, 0, PITCH)], axis=1)


def own(ref, low, high, row=0):
    block = ref[OWN + PITCH * row : OWN + PITCH * (row + ROWS), low:high]
    return block.reshape(ROWS, PITCH, high - low)[:, 16:48, :].reshape(ROWS * COLS, high - low)


def roll(value, by):
    return pltpu.roll(value, by % value.shape[0], 0)


def lane_roll(value, by):
    return pltpu.roll(value, by % value.shape[1], 1)


def grouped(first, last, group, work):
    def step(n, _):
        for k in range(group):
            work(first + n * group + k)
        return 0

    lax.fori_loop(0, (last - first) // group, step, 0)


def blocks(first, chunks_each, count, work):
    size = chunks_each * PITCH
    if count == 1:
        work(first * PITCH, size)
        return

    def step(n, _):
        work(pl.multiple_of(first * PITCH + n * size, 16), size)
        return 0

    lax.fori_loop(0, count, step, 0)


def clear_margins(fields):
    for ref, first, last in fields:
        ref[0 : first * PITCH, :] = jnp.zeros((first * PITCH, ref.shape[1]), BF)
        if last < CHUNKS:
            ref[last * PITCH :, :] = jnp.zeros((CELLS - last * PITCH, ref.shape[1]), BF)


def put(ref, start, size, value, low, high):
    ref[pl.ds(start, size), low:high] = value.astype(BF)


def row_of(t):
    return t % 2, PITCH * (t // 2)


def low_half():
    return lax.broadcasted_iota(jnp.int32, (1, 128), 1) < 64


def slope(act):
    act = act.astype(F32)
    return 1.0 - act * act


def split_dot(value, perm):
    high = value.astype(BF)
    rest = value - high.astype(F32)
    middle = rest.astype(BF)
    low = (rest - middle.astype(F32)).astype(BF)
    return (dotn(low, perm) + dotn(middle, perm)) + dotn(high, perm)


def grid(rows, cols):
    return tuple(lax.broadcasted_iota(jnp.int32, (rows, cols), n) for n in (0, 1))


def one_hot(chosen):
    return jnp.where(chosen, 1.0, 0.0).astype(BF)


def select(core, s0_ref, s5_ref, turn3_ref, turn4_ref):
    m, lane = grid(PITCH, 256)
    for s in range(3):
        after = m + 31 + s + HALO + core * COLS
        here = m - 17 + s + HALO + core * COLS
        wanted = jnp.where(m < 8, after, jnp.where(here >= 0, here + 128, -1))
        s0_ref[s * PITCH : (s + 1) * PITCH, :] = one_hot(lane == wanted)
    for u in range(6):
        col = 4 * jnp.where(m < 8, m + 32, m - 16) + u - 1
        beyond = jnp.where(col - 128 < FINE_HALO, col + 64, -1)
        beyond = jnp.where(col == 127, 204, beyond)
        here = jnp.where(col < 0, col + 140, jnp.where(col < 128, col, col + 12))
        here = jnp.where(col < -FINE_HALO, -1, here)
        s5_ref[u * PITCH : (u + 1) * PITCH, :] = one_hot(lane == jnp.where(m < 8, beyond, here))
    new, old = grid(256, 256)
    turn3_ref[...] = one_hot(old == 4 * (new & 63) + 2 * (new >> 7) + 1 - ((new >> 6) & 1))
    turn4_ref[...] = one_hot(old == 4 * (new & 63) + 2 * ((new >> 6) & 1) + (new >> 7))


def small_terms(perms, small, bias_ref):
    b1_ref, b2_ref, b3_ref, b4_ref = small
    perm3, perm4 = perms

    def wide(value):
        return jnp.broadcast_to(value, (8, value.shape[1]))

    bias_ref[0:8, 0:128] = wide(jnp.concatenate([b1_ref[...]] * 2, axis=1))
    bias_ref[8:16, 0:128] = wide(jnp.concatenate([b2_ref[...]] * 2, axis=1))
    bias_ref[16:24, 0:256] = split_dot(wide(b3_ref[...]), perm3)
    four = split_dot(wide(b4_ref[...]), perm4)
    bias_ref[24:32, :] = jnp.concatenate([four, four], axis=1)


def arrange(perms, weights, there, back):
    w1_ref, w2_ref, w3_ref, w4_ref, w5_ref = weights
    k1, k2, k3, k4 = there
    r5, r4, r3, r2 = back
    perm3, perm4 = perms
    chans = w1_ref.shape[2]
    w3p = dotn(w3_ref[...], perm3).astype(BF)
    w4p = dotn(w4_ref[...], perm4).astype(BF)
    for ref in (k1, k2, k3, k4, r4, r3, r2):
        ref[...] = jnp.zeros(ref.shape, BF)
    for r in range(3):
        for s in range(3):
            at = s * 128 + r * 16
            k1[at : at + chans, :] = jnp.concatenate([w1_ref[r, s]] * 2, axis=1)
        part = w2_ref[r * 192 : (r + 1) * 192, :]
        k2[r * 256 : r * 256 + 192, :] = jnp.concatenate([part, part], axis=1)
        k3[r * 256 : r * 256 + 192, :] = w3p[r * 192 : (r + 1) * 192, :]
        for q in range(2):
            k4[r * 256 + q * 64 : r * 256 + q * 64 + 192, q * 256 : (q + 1) * 256] = w4p[
                r * 192 : (r + 1) * 192, :
            ]
        for s in range(3):
            t = 2 - r
            tap = (3 * r + s) * 64
            block = w3p[tap : tap + 64, :]
            r3[s * 64 : (s + 1) * 64, t * 256 : (t + 1) * 256] = block
            small = w2_ref[tap : tap + 64, :]
            r2[s * 64 : (s + 1) * 64, t * 128 + 64 : t * 128 + 128] = small
            if s == 2:
                r3[192:256, t * 256 : (t + 1) * 256] = block
                r2[192:256, t * 128 + 64 : t * 128 + 128] = small
            block = w4p[tap : tap + 64, :]
            for q in range(2):
                for q_src in range(2):
                    at = t * 512 + q_src * 256
                    if q - q_src + 1 == s:
                        r4[(1 - q) * 64 : (2 - q) * 64, at : at + 256] = block
                    if q_src == 1 - q and s == 2 - 2 * q:
                        r4[128 + (1 - q) * 64 : 128 + (2 - q) * 64, at : at + 256] = block
    columns = output_columns(w5_ref)
    for p in range(4):
        for v in range(3):
            r5[p * 64 : (p + 1) * 64, v * 128 : (v + 1) * 128] = lane_roll(
                columns[2 - v].T, 16 * p
            ).astype(BF)


def output_columns(w5_ref):
    gap_rows = jnp.zeros((16 - w5_ref.shape[2], 64), F32)
    columns = []
    for s in range(3):
        column = []
        for r in (2, 1, 0):
            column += [w5_ref[r, s].astype(F32), gap_rows]
        columns.append(jnp.concatenate(column + [jnp.zeros((80, 64), F32)], axis=0))
    return columns


def fine_field(kept_hbm, w5_ref, b5_ref, fine_ref, e_ref, k5, k5s, a4, sem):
    copy = pltpu.make_async_copy(kept_hbm, a4.at[pl.ds(NEAR, NEAR_CELLS)], sem)
    copy.start()
    low = low_half()
    cell, lane = grid(512, 512)
    e_ref[...] = one_hot(lane == ((cell >> 5) & 3) * 128 + (cell & 31) * 4 + (cell >> 7))
    k5[...] = jnp.zeros(k5.shape, BF)
    k5s[...] = jnp.zeros(k5s.shape, BF)
    columns = output_columns(w5_ref)
    w5 = [value.T for value in columns]
    columns = [value.astype(BF) for value in columns]
    empty = jnp.zeros((64, 64), BF)
    for t in range(6):
        at = 64 if t == 0 else (1536 if t == 5 else 512 + ((t - 1) // 2) * 512 + ((t - 1) % 2) * 64)
        side = 64 if t == 0 else (384 if t == 5 else 128 + ((t - 1) // 2) * 128 + ((t - 1) % 2) * 64)
        for b in range(3):
            p = t - 2 + b
            if not 0 <= p < 4:
                continue
            for src in range(4):
                for q in range(max(src - 1, 0), min(src + 1, 3) + 1):
                    k5[q * 64 + p * 16 : q * 64 + p * 16 + 16, at + src * 128 : at + src * 128 + 64] = (
                        columns[src - q + 1][b * 16 : b * 16 + 16, :]
                    )
        rows = [lane_roll(w5[s], 16 * (t - 2)).astype(BF)[:, :64] for s in (0, 2)]
        k5s[side : side + 64, :] = jnp.concatenate([rows[0], empty], axis=1)
        k5s[512 + side : 512 + side + 64, :] = jnp.concatenate([empty, rows[1]], axis=1)
    chans = b5_ref.shape[1]
    five = jnp.concatenate([b5_ref[...], jnp.zeros((1, 128 - chans), F32)], axis=1)
    five = sum(lane_roll(five, 16 * n) for n in range(8))
    five = jnp.concatenate([jnp.broadcast_to(five, (128, 128)).T] * 2, axis=0)
    copy.wait()
    size = ROWS * PITCH
    wide = size + 32
    at = OWN - 16
    side = []
    for low_lane in (384, 0):
        side.append(take(a4, at - PITCH, wide, 512 + low_lane, 640 + low_lane))
        side.append(take(a4, at, wide, low_lane, low_lane + 128))
        side.append(take(a4, at, wide, 512 + low_lane, 640 + low_lane))
        side.append(take(a4, at + PITCH, wide, low_lane, low_lane + 128))
    side = dotn(jnp.concatenate(side, axis=1), k5s[...])
    side = jnp.where(low, roll(side, 1), roll(side, -1))[16 : 16 + size]
    side = side.reshape(ROWS, PITCH, 128)[:, 16:48, :].reshape(ROWS * COLS, 128).T
    field = jnp.concatenate(
        [own(a4, 512, 1024, -1), own(a4, 0, 1024), own(a4, 0, 512, 1)], axis=1
    )
    z = dott(k5[...], field) + five[:, 0:1]
    z = [z[0:64] + side[0:64], z[64:128], z[128:192], z[192:256] + side[64:128]]
    z = jnp.concatenate(
        [jnp.concatenate([z[q][:, g * 128 : (g + 1) * 128] for q in range(4)], axis=1) for g in range(4)],
        axis=0,
    )
    high = z.astype(BF)
    rest = (z - high.astype(F32)).astype(BF)
    z = dotn(jnp.concatenate([rest, high], axis=0), e_ref[...])
    z = z[0:256] + z[256:512]
    for g in range(4):
        for n in range(4):
            for p in range(4):
                fine_ref[16 * g + 4 * n + p] = z[
                    g * 64 + p * 16 : g * 64 + p * 16 + 16, n * 128 : (n + 1) * 128
                ]


def in_plane(extent, pos_ref, mask):
    row0 = pos_ref[0]
    col0 = pos_ref[1]
    m = lax.broadcasted_iota(jnp.int32, (PITCH, 128), 0)
    col = col0 + jnp.where(m < 8, m + 32, m - 16)
    col_ok = jnp.logical_and(col >= 0, col < extent[1])
    for k in range(CHUNKS):
        row = row0 + jnp.where(m < 8, k - 9, k - 8)
        ok = jnp.logical_and(col_ok, jnp.logical_and(row >= 0, row < extent[0]))
        mask[k * PITCH : (k + 1) * PITCH, :] = jnp.where(ok, 1.0, 0.0)


def forward(
    extent,
    pos_ref,
    window_ref,
    above_ref,
    below_ref,
    w1_hbm,
    w2_hbm,
    w3_hbm,
    w4_hbm,
    w5_hbm,
    b1_ref,
    b2_ref,
    b3_ref,
    b4_ref,
    mask,
    s5_ref,
    turn3_ref,
    turn4_ref,
    r5,
    r4,
    r3,
    r2,
    x0,
    x1,
    x2,
    x3,
    a3,
    a4,
    bias_ref,
    s0_ref,
    k1,
    k2,
    k3,
    k4,
    w1_ref,
    w2_ref,
    w3_ref,
    w4_ref,
    w5_ref,
    dx_ref,
    sems,
):
    copies = [
        pltpu.make_async_copy(src, dst, sems.at[n])
        for n, (src, dst) in enumerate(
            (
                (w1_hbm, w1_ref),
                (w2_hbm, w2_ref),
                (w3_hbm, w3_ref),
                (w4_hbm, w4_ref),
                (w5_hbm, w5_ref),
            )
        )
    ]
    for copy in copies:
        copy.start()
    small = (b1_ref, b2_ref, b3_ref, b4_ref)
    select(pos_ref[2], s0_ref, s5_ref, turn3_ref, turn4_ref)
    in_plane(extent, pos_ref, mask)
    low = low_half()
    clear_margins(((x0, 2, 30), (x1, 3, 30), (x2, 4, 29), (x3, 5, 29), (a4, 5, 29)))

    lane = lax.broadcasted_iota(jnp.int32, (1, 128), 1)
    dx_ref[0:2] = jnp.zeros((2, 16, 128), BF)
    dx_ref[8:24] = window_ref[...]
    dx_ref[30:32] = jnp.zeros((2, 16, 128), BF)
    for ref, at in ((above_ref, 2), (below_ref, 24)):
        sent = ref[FINE_HALO : FINE_HALO + HALO].reshape(HALO * 16, 128).astype(F32)
        sent = jnp.where(lane < 2 * COLS + 2 * HALO, lane_roll(sent, -2 * FINE_HALO), 0.0)
        dx_ref[at : at + HALO] = sent.astype(BF).reshape(HALO, 16, 128)

    def coarse_pair(n):
        lines = []
        for k in (2 * n, 2 * n + 1):
            before = dx_ref[pl.ds(k - 2, 3)].reshape(48, 128)
            here = dx_ref[pl.ds(k - 1, 3)].reshape(48, 128)
            lines += [jnp.concatenate([before, here], axis=1), jnp.zeros((80, 256), BF)]
        moved = dott(s0_ref[...], jnp.concatenate(lines, axis=0)).astype(BF)
        for half in range(2):
            at = pl.multiple_of((2 * n + half) * PITCH, 16)
            for s in range(3):
                x0[pl.ds(at, PITCH), s * 128 : (s + 1) * 128] = moved[
                    s * PITCH : (s + 1) * PITCH, half * 128 : (half + 1) * 128
                ]

    grouped(1, 15, GROUP0, coarse_pair)
    for copy in copies:
        copy.wait()
    perms = (turn3_ref[...].T, turn4_ref[...].T)
    small_terms(perms, small, bias_ref)
    arrange(
        perms,
        (w1_ref, w2_ref, w3_ref, w4_ref, w5_ref),
        (k1, k2, k3, k4),
        (r5, r4, r3, r2),
    )

    def narrow(read, weight, bias_at, variants):
        def work(start, size):
            wide = size + 32
            z = dotn(read(start - 16, wide), weight[...])
            z = jnp.tanh(z + bias_ref[8 * bias_at : 8 * bias_at + 1, 0:128])
            z = z * take(mask, start - 16, wide)
            inner = slice(16, 16 + size)
            left = jnp.where(low, roll(z, 1), z)
            put(variants, start, size, left[inner], 0, 128)
            put(variants, start, size, roll(z, -1)[inner], 128, 256)

        return work

    blocks(3, 27 // N1, N1, narrow(lambda at, n: take(x0, at, n), k1, 0, x1))
    blocks(4, 25 // N2, N2, narrow(lambda at, n: taps(x1, at, n), k2, 1, x2))

    def conv_three(start, size):
        wide = size + 32
        z = dotn(taps(x2, start - 16, wide), k3[...])
        z = jnp.tanh(z + bias_ref[16:17, 0:256])
        ok = take(mask, start - 16, wide)
        inner = slice(16, 16 + size)
        for p in range(2):
            half = z[:, p * 128 : (p + 1) * 128] * ok
            left = jnp.where(low, roll(half, 1), half)
            right = jnp.where(low, half, roll(half, -1))
            put(x3, start, size, left[inner], p * 256, p * 256 + 128)
            put(x3, start, size, right[inner], p * 256 + 128, p * 256 + 256)
            put(a3, start, size, half[inner], p * 128, p * 128 + 128)

    blocks(5, 24 // N3, N3, conv_three)

    def conv_four(start, size):
        ok = take(mask, start, size)
        for p in range(2):
            lines = []
            for r in range(3):
                phase, by = row_of(p + r - 1)
                lines.append(take(x3, start + by, size, phase * 256, phase * 256 + 256))
            z = dotn(jnp.concatenate(lines, axis=1), k4[...])
            z = jnp.tanh(z + bias_ref[24:25, 0:512])
            for q in range(4):
                at = p * 512 + q * 128
                put(a4, start, size, z[:, q * 128 : (q + 1) * 128] * ok, at, at + 128)

    blocks(5, 24 // N4, N4, conv_four)


def backward(
    scale,
    pos_ref,
    above_ref,
    below_ref,
    cot_ref,
    sides_ref,
    mask,
    s5_ref,
    r5,
    r4,
    r3,
    r2,
    x0,
    x1,
    x2,
    x3,
    a3,
    a4,
    keep_ref,
    send_ref,
    kept_hbm,
    c5,
    b4,
    b3,
    b2,
    b1,
    g_ref,
    center_ref,
    rim_ref,
    sem,
):
    kept = pltpu.make_async_copy(a4.at[pl.ds(NEAR, NEAR_CELLS)], kept_hbm, sem)
    kept.start()
    low = low_half()
    clear_margins(((c5, 5, 29), (b4, 5, 29), (b3, 6, 27), (b2, 7, 27)))

    n = FINE_HALO
    rows = 4 * ROWS
    lane = lax.broadcasted_iota(jnp.int32, (1, 128), 1)
    for ref, inside, parts in (
        (center_ref, cot_ref, slice(0, n)),
        (rim_ref, sides_ref, slice(n, 2 * n)),
    ):
        ref[0] = jnp.zeros((16, 128), BF)
        ref[1 : n + 1] = above_ref[parts]
        ref[n + 1 : n + 1 + rows] = inside[...]
        ref[n + 1 + rows : 2 * n + 1 + rows] = below_ref[parts]
        ref[2 * n + 1 + rows :] = jnp.zeros((9, 16, 128), BF)
    count = (2 * n + 10 + rows) * 16
    sides = rim_ref[...].reshape(count, 128).astype(F32)
    before = lane_roll(sides[: count - 64], 64 - n)
    corner = lane_roll(center_ref[...].reshape(count, 128).astype(F32)[: count - 64], 77)
    before = jnp.where(lane < 64 + n, before, corner)
    before = jnp.concatenate([jnp.zeros((64, 128), F32), before], axis=0)
    sides = jnp.where(lane < 2 * n, sides, jnp.where(lane < 64, 0.0, before))
    sides = jnp.where(lane < 65 + n, sides, 0.0)
    rim_ref[...] = sides.astype(BF).reshape(count // 16, 16, 128)

    def cot_pair(n):
        lines = []
        for k in (2 * n + 1, 2 * n + 2):
            at = pl.ds(4 * (k - 5), 6)
            here = jnp.concatenate(
                [center_ref[at].reshape(96, 128), rim_ref[at].reshape(96, 128)], axis=1
            )
            lines += [here, jnp.zeros((32, 256), BF)]
        moved = dott(s5_ref[...], jnp.concatenate(lines, axis=0)).astype(BF)
        for half in range(2):
            at = pl.multiple_of((2 * n + 1 + half) * PITCH, 16)
            for u in range(6):
                c5[pl.ds(at, PITCH), u * 128 : (u + 1) * 128] = moved[
                    u * PITCH : (u + 1) * PITCH, half * 128 : (half + 1) * 128
                ]

    grouped(2, 14, GROUP5, cot_pair)

    def back_four(start, size):
        ok = take(mask, start, size)
        for q in range(4):
            z = dott(take(c5, start, size, q * 128, q * 128 + 384), r5[...])
            for p in range(2):
                at = p * 512 + q * 128
                z_p = z[:, p * 128 : (p + 1) * 128] * ok
                put(b4, start, size, z_p * slope(take(a4, start, size, at, at + 128)), at, at + 128)

    blocks(5, 24 // M4, M4, back_four)

    def back_three(start, size):
        wide = size + 32
        ok = take(mask, start, size)
        inner = slice(16, 16 + size)
        for p in range(2):
            lines = []
            for t in range(3):
                phase, by = row_of(p + t - 1)
                lines.append(take(b4, start - 16 + by, wide, phase * 512, phase * 512 + 512))
            z = dott(jnp.concatenate(lines, axis=1), r4[...])
            moved = jnp.where(low, roll(z[:, 128:256], -1), roll(z[:, 128:256], 1))
            z = (z[:, 0:128] + moved)[inner] * ok
            at = p * 128
            put(b3, start, size, z * slope(take(a3, start, size, at, at + 128)), at, at + 128)

    blocks(6, 21 // M3, M3, back_three)

    def back_narrow(src, weight, act, out):
        def work(start, size):
            wide = size + 32
            z = dott(taps(src, start - 16, wide), weight[...])
            pair = jnp.where(low, roll(z[:, 0:128], -1), z[:, 0:128])
            z = pair + lane_roll(pair, 64) + roll(z[:, 128:256], 1)
            z = z[16 : 16 + size] * take(mask, start, size)
            z = jnp.where(low, 0.0, z * slope(take(act, start, size, 0, 128)))
            put(out, start, size, z, 0, 128)

        return work

    blocks(7, 20 // M2, M2, back_narrow(b3, r3, x2, b2))
    blocks(8, 18 // M1, M1, back_narrow(b2, r2, x1, b1))

    g_ref[1344:, :] = jnp.zeros((g_ref.shape[0] - 1344, 256), F32)
    g_ref[1152:1344, 192:256] = jnp.zeros((192, 64), F32)

    back = own(b4, 0, 1024)
    sums4 = jnp.sum(back.astype(F32), axis=0, keepdims=True)
    back = back.T
    for r in range(3):
        total = None
        for p in range(2):
            phase, by = row_of(p + r - 1)
            field = own(x3, phase * 256, phase * 256 + 256, by // PITCH)
            term = dotn(back[p * 512 : (p + 1) * 512, :], field)
            total = term if total is None else total + term
        total = total[0:256, 0:192] + total[256:512, 64:256]
        g_ref[r * 192 : (r + 1) * 192, :] = total.T * scale
    sums4 = sums4[:, 0:512] + sums4[:, 512:1024]
    sums4 = sums4[:, 0:256] + sums4[:, 256:512]

    back = own(b3, 0, 256)
    sums3 = jnp.sum(back.astype(F32), axis=0, keepdims=True)
    back = back.T
    for r in range(3):
        total = dotn(back, own(x2, 0, 256, r - 1))[:, 0:192]
        g_ref[576 + r * 192 : 576 + (r + 1) * 192, :] = total.T * scale

    back = own(b2, 0, 128)
    sums2 = jnp.sum(back.astype(F32), axis=0, keepdims=True)
    back = back.T
    for r in range(3):
        total = dotn(back[64:128, :], own(x1, 0, 256, r - 1))
        g_ref[1152:1344, r * 64 : (r + 1) * 64] = total[:, 0:192].T * scale

    back = own(b1, 0, 128)
    sums1 = jnp.sum(back.astype(F32), axis=0, keepdims=True)
    back = back.T
    total = dotn(back[64:128, :], own(x0, 0, 384)).T * scale
    for s in range(3):
        g_ref[1152 + s * 48 : 1152 + (s + 1) * 48, 192:256] = total[s * 128 : s * 128 + 48, :]

    cot = own(c5, 0, 768)
    sums5 = jnp.sum(cot.astype(F32), axis=0, keepdims=True)
    cot = cot.T
    total = None
    for q in range(4):
        field = jnp.concatenate(
            [own(a4, q * 128, q * 128 + 128), own(a4, 512 + q * 128, 640 + q * 128)], axis=1
        )
        term = dotn(cot[q * 128 : q * 128 + 384, :], field)
        total = term if total is None else total + term
    total = total * scale
    for r in range(3):
        for s in range(3):
            sum_p = None
            for p in range(4):
                at = (2 - s) * 128 + (p + 2 - r) * 16
                term = total[at : at + 16, p * 64 : (p + 1) * 64]
                sum_p = term if sum_p is None else sum_p + term
            g_ref[1344 + s * 16 : 1344 + (s + 1) * 16, r * 64 : (r + 1) * 64] = sum_p

    sums5 = sums5[:, 128:256] + sums5[:, 256:384] + sums5[:, 384:512] + sums5[:, 512:640]
    five = sums5
    for t in range(1, 4):
        five = five + lane_roll(sums5, -16 * t)
    biases = [
        sums4 * scale,
        sums3 * scale,
        jnp.concatenate([sums2, sums1], axis=1) * scale,
        jnp.concatenate([five, jnp.zeros((1, 128), F32)], axis=1) * scale,
    ]
    for n, value in enumerate(biases):
        high = value.astype(BF).astype(F32)
        g_ref[1392 + 2 * n : 1393 + 2 * n, :] = high
        g_ref[1393 + 2 * n : 1394 + 2 * n, :] = value - high

    half = g_ref.shape[0] // 2
    core = pos_ref[2]
    keep_ref[...] = g_ref[pl.ds(pl.multiple_of(core * half, 16), half), :]
    send_ref[...] = g_ref[pl.ds(pl.multiple_of((1 - core) * half, 16), half), :].astype(BF)
    kept.wait()


def finish(chans, places, pos_ref, mine_ref, other_ref, turn3_ref, turn4_ref, g1, g2, g3, g4, g5, c1, c2, c3, c4, c5, full):
    half = full.shape[0] // 2
    size = half // places
    core = pos_ref[2]
    for b in range(places):
        at = pl.multiple_of(lax.bitwise_xor(pos_ref[3], b) * size, 16)
        here = pl.multiple_of(core * half + b * size, 16)
        there = pl.multiple_of((1 - core) * half + b * size, 16)
        full[pl.ds(here, size), :] = mine_ref[pl.ds(at, size), :]
        full[pl.ds(there, size), :] = other_ref[pl.ds(at, size), :]
    g4[...] = dotn(full[0:576, :], turn4_ref[...])
    g3[...] = dotn(full[576:1152, :], turn3_ref[...])
    for r in range(3):
        g2[r * 192 : (r + 1) * 192, :] = full[1152:1344, r * 64 : (r + 1) * 64].astype(F32)
        for s in range(3):
            at = 1152 + s * 48 + r * 16
            g1[r, s] = full[at : at + 16, 192:256].astype(F32)[:chans]
            at = 1344 + s * 16
            g5[r, s] = full[at : at + 16, r * 64 : (r + 1) * 64].astype(F32)[:chans]
    terms = full[1392:1408, :]
    turned4 = dotn(terms, turn4_ref[...])
    turned3 = dotn(terms, turn3_ref[...])
    terms = terms.astype(F32)
    c4[...] = turned4[0:1] + turned4[1:2]
    c3[...] = turned3[2:3] + turned3[3:4]
    sums = [None, None, terms[4:5] + terms[5:6], terms[6:7] + terms[7:8]]
    c2[...] = sums[2][:, 64:128]
    c1[...] = sums[2][:, 192:256]
    c5[...] = sums[3][:, 16 : 16 + chans]


def exchange(axis, first, last):
    count = lax.axis_size(axis)
    odd = lax.axis_index(axis) % 2 == 1
    even_swap = [(i, i ^ 1) for i in range(count)]
    odd_swap = [(i, ((i + 1) ^ 1) - 1) for i in range(1, count - 1)]
    one = lax.ppermute(jnp.where(odd, first, last), axis, even_swap)
    two = lax.ppermute(jnp.where(odd, last, first), axis, odd_swap)
    return jnp.where(odd, one, two), jnp.where(odd, two, one)


def swap(block, axis, flip):
    return lax.ppermute(block, axis, [(i, i ^ flip) for i in range(lax.axis_size(axis))])


def chip_window(coarse, beside):
    gy, at = lax.axis_size("gy"), lax.axis_index("gy")
    chans, each, ny = coarse.shape
    cols = 2 * ny // gy
    block = jnp.pad(coarse.transpose(1, 0, 2), ((0, 0), (0, 16 - chans), (HALO, HALO)))
    other = swap(block, "gy", 1)
    block = jnp.where(
        at % 2 == 0, jnp.concatenate([block, other]), jnp.concatenate([other, block])
    )
    held = jnp.stack(
        [block[:, :, cols * c : cols * (c + 1) + 2 * HALO] for c in range(gy // 2)]
    )
    flip, bits = gy // 2, 0
    while flip > 1:
        half = held.shape[0] // 2
        high = (at & flip) != 0
        mine = jnp.where(high, held[half:], held[:half])
        other = swap(jnp.where(high, held[:half], held[half:]), "gy", flip)
        held = jnp.where(
            high,
            jnp.concatenate([other, mine], axis=1),
            jnp.concatenate([mine, other], axis=1),
        )
        flip, bits = flip // 2, bits + 1
        if bits == 1:
            held, beside = lax.optimization_barrier((held, beside))
    tail = (2 * each,) + held.shape[2:]
    held = held.reshape((2,) * bits + tail)
    held = held.transpose(tuple(reversed(range(bits))) + (bits, bits + 1, bits + 2))
    return held.reshape((gy * each,) + tail[1:]), beside


def halo_pieces(coarse, cotangent):
    n = FINE_HALO
    spare = 16 - coarse.shape[0]
    edges = (cotangent[:, :, :n].transpose(2, 0, 1), cotangent[:, :, -n:].transpose(2, 0, 1))
    got, edges = chip_window(coarse, edges)
    left, right = exchange("gy", *edges)
    wide = got.shape[2]
    cot = jnp.pad(cotangent.transpose(1, 0, 2), ((0, 0), (0, spare), (0, 0)))
    rim = jnp.concatenate([left.transpose(2, 1, 0), right.transpose(2, 1, 0)], axis=2)
    rim = jnp.pad(rim, ((0, 0), (0, spare), (0, 0)))

    def edge(cot_rows, coarse_rows):
        side = jnp.pad(got[coarse_rows], ((0, n - HALO), (0, 0), (0, 128 - 2 * n - wide)))
        side = jnp.concatenate([rim[cot_rows], side], axis=2)
        return jnp.concatenate([cot[cot_rows], side])

    first = edge(slice(0, n), slice(0, HALO))
    last = edge(slice(-n, None), slice(-HALO, None))
    above, below = exchange("gx", first, last)
    got = jnp.pad(got, ((0, 0), (0, 0), (0, 128 - wide)))
    return got, above, below, cot, jnp.pad(rim, ((0, 0), (0, 0), (0, 128 - 2 * n)))


def total_over_all(keep, send, beside, chans):
    gx, gy = lax.axis_size("gx"), lax.axis_size("gy")
    at_x = lax.axis_index("gx")

    def tree(terms):
        while len(terms) > 1:
            terms = [terms[n] + terms[n + 1] for n in range(0, len(terms), 2)]
        return terms[0]

    value = keep + swap(send, "gy", 1).astype(F32)
    size = value.shape[0] // gx

    def part(place):
        return lax.dynamic_slice_in_dim(value, place * size, size, 0)

    terms = [swap(part(at_x ^ d).astype(BF), "gx", d) for d in range(1, gx)]
    terms, beside = lax.optimization_barrier((terms, beside))
    beside = beside.transpose(1, 0, 2)[:chans]
    block = tree([part(at_x)] + [term.astype(F32) for term in terms])
    flip = 2
    while flip < gy:
        block = block.astype(BF)
        other = swap(block, "gy", flip)
        flip *= 2
        if flip == gy:
            other, beside = lax.optimization_barrier((other, beside))
        block = block.astype(F32) + other.astype(F32)
    block = block.astype(BF)
    mine = jnp.concatenate([block] + [swap(block, "gx", d) for d in range(1, gx)])
    return mine, swap(mine, "gy", 1), beside


def local(
    coarse,
    weight_one,
    weight_two,
    weight_three,
    weight_four,
    weight_five,
    bias_one,
    bias_two,
    bias_three,
    bias_four,
    bias_five,
    cotangent,
):
    gx, gy = lax.axis_size("gx"), lax.axis_size("gy")
    chans = coarse.shape[0]
    tile_rows = coarse.shape[1] * gy
    tile_cols = coarse.shape[2] // gy
    assert (tile_rows, tile_cols) == (ROWS, COLS)
    at_x, at_y = lax.axis_index("gx"), lax.axis_index("gy")
    pos = jnp.stack([at_x * ROWS, at_y * COLS, at_y % 2, at_x]).astype(jnp.int32)
    extent = (ROWS * gx, COLS * gy)
    scale = float((16 * extent[0] * extent[1]) ** -0.5)

    smem = pl.BlockSpec(memory_space=pltpu.SMEM)
    vmem = pl.BlockSpec(memory_space=pltpu.VMEM)
    params = pltpu.CompilerParams(vmem_limit_bytes=LIMIT * 1024 * 1024)

    def near(value):
        return pltpu.with_memory_space_constraint(value, pltpu.VMEM)

    def buf(width, kind=BF):
        return pltpu.VMEM((CELLS, width), kind)

    window, above, below, cot, rim = halo_pieces(coarse, cotangent)
    shared = (
        buf(128, F32),
        pltpu.VMEM((6 * PITCH, 256), BF),
        pltpu.VMEM((256, 256), BF),
        pltpu.VMEM((256, 256), BF),
        pltpu.VMEM((256, 384), BF),
        pltpu.VMEM((256, 1536), BF),
        pltpu.VMEM((256, 768), BF),
        pltpu.VMEM((256, 384), BF),
        buf(384),
        buf(256),
        buf(256),
        buf(512),
        buf(256),
        buf(1024),
    )
    hbm = pl.BlockSpec(memory_space=pltpu.HBM)
    weights = (
        weight_one,
        weight_two.reshape(576, 64),
        weight_three.reshape(576, 256),
        weight_four.reshape(576, 256),
        weight_five.transpose(0, 1, 3, 2),
    )
    fields = pl.pallas_call(
        lambda *refs: forward(extent, *refs),
        out_shape=shared,
        in_specs=[smem] + [vmem] * 3 + [hbm] * 5 + [vmem] * 4,
        out_specs=(vmem,) * 14,
        scratch_shapes=[
            pltpu.VMEM((32, 512), F32),
            pltpu.VMEM((3 * PITCH, 256), BF),
            pltpu.VMEM((384, 128), BF),
            pltpu.VMEM((768, 128), BF),
            pltpu.VMEM((768, 256), BF),
            pltpu.VMEM((768, 512), BF),
        ]
        + [pltpu.VMEM(w.shape, BF) for w in weights]
        + [pltpu.VMEM((32, 16, 128), BF)]
        + [pltpu.SemaphoreType.DMA((5,))],
        compiler_params=params,
        name="forward",
    )(
        pos,
        window,
        above,
        below,
        *[pltpu.with_memory_space_constraint(w, pltpu.HBM) for w in weights],
        bias_one.reshape(1, -1),
        bias_two.reshape(1, -1),
        bias_three.reshape(1, -1),
        bias_four.reshape(1, -1),
    )
    fields = [near(f) for f in fields]
    half = -(-TERMS // (32 * gx)) * 16 * gx
    keep, send, kept = pl.pallas_call(
        lambda *refs: backward(scale, *refs),
        out_shape=(
            pltpu.VMEM((half, 256), F32),
            pltpu.VMEM((half, 256), BF),
            pltpu.HBM((NEAR_CELLS, 1024), BF),
        ),
        in_specs=[smem] + [vmem] * 16,
        out_specs=(vmem, vmem, hbm),
        scratch_shapes=[
            buf(768),
            buf(1024),
            buf(256),
            buf(128),
            buf(128),
            pltpu.VMEM((2 * half, 256), F32),
            pltpu.VMEM((98, 16, 128), BF),
            pltpu.VMEM((98, 16, 128), BF),
            pltpu.SemaphoreType.DMA,
        ],
        compiler_params=params,
        name="backward",
    )(pos, above, below, cot, rim, *fields[:2], *fields[4:])
    fine = pl.pallas_call(
        fine_field,
        out_shape=jax.ShapeDtypeStruct((4 * ROWS, 16, 4 * COLS), F32),
        in_specs=[hbm, vmem, vmem],
        out_specs=vmem,
        scratch_shapes=[
            pltpu.VMEM((512, 512), BF),
            pltpu.VMEM((256, 2048), BF),
            pltpu.VMEM((1024, 128), BF),
            buf(1024),
            pltpu.SemaphoreType.DMA,
        ],
        compiler_params=params,
        name="fine",
    )(pltpu.with_memory_space_constraint(kept, pltpu.HBM), weights[4], bias_five.reshape(1, -1))
    mine, other, fine = total_over_all(keep, send, fine, chans)

    def out(*shape):
        return jax.ShapeDtypeStruct(shape, F32)

    g1, g2, g3, g4, g5, c1, c2, c3, c4, c5 = pl.pallas_call(
        lambda *refs: finish(chans, gx, *refs),
        out_shape=(
            out(3, 3, chans, 64),
            out(576, 64),
            out(576, 256),
            out(576, 256),
            out(3, 3, chans, 64),
            out(1, 64),
            out(1, 64),
            out(1, 256),
            out(1, 256),
            out(1, chans),
        ),
        in_specs=[smem] + [vmem] * 4,
        out_specs=(vmem,) * 10,
        scratch_shapes=[pltpu.VMEM((2 * half, 256), BF)],
        compiler_params=params,
        name="finish",
    )(pos, mine, other, fields[2], fields[3])
    return (
        fine,
        g1,
        g2.reshape(3, 3, 64, 64),
        g3.reshape(3, 3, 64, 256),
        g4.reshape(3, 3, 64, 256),
        g5.transpose(0, 1, 3, 2),
        c1.reshape(64),
        c2.reshape(64),
        c3.reshape(256),
        c4.reshape(256),
        c5.reshape(chans),
    )


def solution(mesh):
    in_specs = (
        P(None, ("gx", "gy"), None),
        P(),
        P(),
        P(),
        P(),
        P(),
        P(),
        P(),
        P(),
        P(),
        P(),
        P(None, "gx", "gy"),
    )
    out_specs = (P(None, "gx", "gy"), P(), P(), P(), P(), P(), P(), P(), P(), P(), P())
    return jax.shard_map(local, mesh=mesh, in_specs=in_specs, out_specs=out_specs, check_vma=False)
```

```python
import jax
import jax.numpy as jnp
from jax import lax
from jax.experimental import pallas as pl
from jax.experimental.pallas import tpu as pltpu
from jax.sharding import PartitionSpec as P

BF = jnp.bfloat16
F32 = jnp.float32

ROWS, COLS, PITCH, CHUNKS = 16, 32, 48, 32
CELLS = PITCH * CHUNKS
OWN = PITCH * 8
NEAR = OWN - PITCH - 16
NEAR_CELLS = PITCH * (ROWS + 2) + 32
HALO = 6
FINE_HALO = 12
TERMS = 1400
GROUP0, GROUP5 = 7, 12
N1, N2, N3, N4 = 1, 1, 1, 1
M4, M3, M2, M1 = 1, 1, 1, 1
LIMIT = 12
BIG = 34


def dotn(left, right):
    return lax.dot_general(left, right, (((1,), (0,)), ((), ())), preferred_element_type=F32)


def dott(left, right):
    return lax.dot_general(left, right, (((1,), (1,)), ((), ())), preferred_element_type=F32)


def take(ref, start, count, low=0, high=None):
    high = ref.shape[1] if high is None else high
    if not isinstance(start, int):
        start = pl.multiple_of(start, 16)
    return ref[pl.ds(start, count), low:high]


def taps(ref, start, count):
    return jnp.concatenate([take(ref, start + d, count) for d in (-PITCH, 0, PITCH)], axis=1)


def own(ref, low, high, row=0):
    block = ref[OWN + PITCH * row : OWN + PITCH * (row + ROWS), low:high]
    return block.reshape(ROWS, PITCH, high - low)[:, 16:48, :].reshape(ROWS * COLS, high - low)


def roll(value, by):
    return pltpu.roll(value, by % value.shape[0], 0)


def lane_roll(value, by):
    return pltpu.roll(value, by % value.shape[1], 1)


def grouped(first, last, group, work):
    def step(n, _):
        for k in range(group):
            work(first + n * group + k)
        return 0

    lax.fori_loop(0, (last - first) // group, step, 0)


def blocks(first, chunks_each, count, work):
    size = chunks_each * PITCH
    if count == 1:
        work(first * PITCH, size)
        return

    def step(n, _):
        work(pl.multiple_of(first * PITCH + n * size, 16), size)
        return 0

    lax.fori_loop(0, count, step, 0)


def clear_margins(fields):
    for ref, first, last in fields:
        ref[0 : first * PITCH, :] = jnp.zeros((first * PITCH, ref.shape[1]), BF)
        if last < CHUNKS:
            ref[last * PITCH :, :] = jnp.zeros((CELLS - last * PITCH, ref.shape[1]), BF)


def put(ref, start, size, value, low, high):
    ref[pl.ds(start, size), low:high] = value.astype(BF)


def row_of(t):
    return t % 2, PITCH * (t // 2)


def low_half():
    return lax.broadcasted_iota(jnp.int32, (1, 128), 1) < 64


def slope(act):
    act = act.astype(F32)
    return 1.0 - act * act


def split_dot(value, perm):
    high = value.astype(BF)
    rest = value - high.astype(F32)
    middle = rest.astype(BF)
    low = (rest - middle.astype(F32)).astype(BF)
    return (dotn(low, perm) + dotn(middle, perm)) + dotn(high, perm)


def grid(rows, cols):
    return tuple(lax.broadcasted_iota(jnp.int32, (rows, cols), n) for n in (0, 1))


def one_hot(chosen):
    return jnp.where(chosen, 1.0, 0.0).astype(BF)


def select(core, s0_ref, s5_ref, turn3_ref, turn4_ref):
    m, lane = grid(PITCH, 256)
    for s in range(3):
        after = m + 31 + s + HALO + core * COLS
        here = m - 17 + s + HALO + core * COLS
        wanted = jnp.where(m < 8, after, jnp.where(here >= 0, here + 128, -1))
        s0_ref[s * PITCH : (s + 1) * PITCH, :] = one_hot(lane == wanted)
    for u in range(6):
        col = 4 * jnp.where(m < 8, m + 32, m - 16) + u - 1
        beyond = jnp.where(col - 128 < FINE_HALO, col + 64, -1)
        beyond = jnp.where(col == 127, 204, beyond)
        here = jnp.where(col < 0, col + 140, jnp.where(col < 128, col, col + 12))
        here = jnp.where(col < -FINE_HALO, -1, here)
        s5_ref[u * PITCH : (u + 1) * PITCH, :] = one_hot(lane == jnp.where(m < 8, beyond, here))
    new, old = grid(256, 256)
    turn3_ref[...] = one_hot(old == 4 * (new & 63) + 2 * (new >> 7) + 1 - ((new >> 6) & 1))
    turn4_ref[...] = one_hot(old == 4 * (new & 63) + 2 * ((new >> 6) & 1) + (new >> 7))


def small_terms(perms, small, bias_ref):
    b1_ref, b2_ref, b3_ref, b4_ref = small
    perm3, perm4 = perms

    def wide(value):
        return jnp.broadcast_to(value, (8, value.shape[1]))

    bias_ref[0:8, 0:128] = wide(jnp.concatenate([b1_ref[...]] * 2, axis=1))
    bias_ref[8:16, 0:128] = wide(jnp.concatenate([b2_ref[...]] * 2, axis=1))
    bias_ref[16:24, 0:256] = split_dot(wide(b3_ref[...]), perm3)
    four = split_dot(wide(b4_ref[...]), perm4)
    bias_ref[24:32, :] = jnp.concatenate([four, four], axis=1)


def arrange(perms, weights, there, back):
    w1_ref, w2_ref, w3_ref, w4_ref, w5_ref = weights
    k1, k2, k3, k4 = there
    r5, r4, r3, r2 = back
    perm3, perm4 = perms
    chans = w1_ref.shape[2]
    w3p = dotn(w3_ref[...], perm3).astype(BF)
    w4p = dotn(w4_ref[...], perm4).astype(BF)
    for ref in (k1, k2, k3, k4, r4, r3, r2):
        ref[...] = jnp.zeros(ref.shape, BF)
    for r in range(3):
        for s in range(3):
            at = s * 128 + r * 16
            k1[at : at + chans, :] = jnp.concatenate([w1_ref[r, s]] * 2, axis=1)
        part = w2_ref[r * 192 : (r + 1) * 192, :]
        k2[r * 256 : r * 256 + 192, :] = jnp.concatenate([part, part], axis=1)
        k3[r * 256 : r * 256 + 192, :] = w3p[r * 192 : (r + 1) * 192, :]
        for q in range(2):
            k4[r * 256 + q * 64 : r * 256 + q * 64 + 192, q * 256 : (q + 1) * 256] = w4p[
                r * 192 : (r + 1) * 192, :
            ]
        for s in range(3):
            t = 2 - r
            tap = (3 * r + s) * 64
            block = w3p[tap : tap + 64, :]
            r3[s * 64 : (s + 1) * 64, t * 256 : (t + 1) * 256] = block
            small = w2_ref[tap : tap + 64, :]
            r2[s * 64 : (s + 1) * 64, t * 128 + 64 : t * 128 + 128] = small
            if s == 2:
                r3[192:256, t * 256 : (t + 1) * 256] = block
                r2[192:256, t * 128 + 64 : t * 128 + 128] = small
            block = w4p[tap : tap + 64, :]
            for q in range(2):
                for q_src in range(2):
                    at = t * 512 + q_src * 256
                    if q - q_src + 1 == s:
                        r4[(1 - q) * 64 : (2 - q) * 64, at : at + 256] = block
                    if q_src == 1 - q and s == 2 - 2 * q:
                        r4[128 + (1 - q) * 64 : 128 + (2 - q) * 64, at : at + 256] = block
    columns = output_columns(w5_ref)
    for p in range(4):
        for v in range(3):
            r5[p * 64 : (p + 1) * 64, v * 128 : (v + 1) * 128] = lane_roll(
                columns[2 - v].T, 16 * p
            ).astype(BF)


def output_columns(w5_ref):
    gap_rows = jnp.zeros((16 - w5_ref.shape[2], 64), F32)
    columns = []
    for s in range(3):
        column = []
        for r in (2, 1, 0):
            column += [w5_ref[r, s].astype(F32), gap_rows]
        columns.append(jnp.concatenate(column + [jnp.zeros((80, 64), F32)], axis=0))
    return columns


def fine_field(kept_hbm, w5_ref, b5_ref, fine_ref, e_ref, k5, k5s, a4, sem):
    copy = pltpu.make_async_copy(kept_hbm, a4.at[pl.ds(NEAR, NEAR_CELLS)], sem)
    copy.start()
    low = low_half()
    cell, lane = grid(512, 512)
    e_ref[...] = one_hot(lane == ((cell >> 5) & 3) * 128 + (cell & 31) * 4 + (cell >> 7))
    k5[...] = jnp.zeros(k5.shape, BF)
    k5s[...] = jnp.zeros(k5s.shape, BF)
    columns = output_columns(w5_ref)
    w5 = [value.T for value in columns]
    columns = [value.astype(BF) for value in columns]
    empty = jnp.zeros((64, 64), BF)
    for t in range(6):
        at = 64 if t == 0 else (1536 if t == 5 else 512 + ((t - 1) // 2) * 512 + ((t - 1) % 2) * 64)
        side = 64 if t == 0 else (384 if t == 5 else 128 + ((t - 1) // 2) * 128 + ((t - 1) % 2) * 64)
        for b in range(3):
            p = t - 2 + b
            if not 0 <= p < 4:
                continue
            for src in range(4):
                for q in range(max(src - 1, 0), min(src + 1, 3) + 1):
                    k5[q * 64 + p * 16 : q * 64 + p * 16 + 16, at + src * 128 : at + src * 128 + 64] = (
                        columns[src - q + 1][b * 16 : b * 16 + 16, :]
                    )
        rows = [lane_roll(w5[s], 16 * (t - 2)).astype(BF)[:, :64] for s in (0, 2)]
        k5s[side : side + 64, :] = jnp.concatenate([rows[0], empty], axis=1)
        k5s[512 + side : 512 + side + 64, :] = jnp.concatenate([empty, rows[1]], axis=1)
    chans = b5_ref.shape[1]
    five = jnp.concatenate([b5_ref[...], jnp.zeros((1, 128 - chans), F32)], axis=1)
    five = sum(lane_roll(five, 16 * n) for n in range(8))
    five = jnp.concatenate([jnp.broadcast_to(five, (128, 128)).T] * 2, axis=0)
    copy.wait()
    size = ROWS * PITCH
    wide = size + 32
    at = OWN - 16
    side = []
    for low_lane in (384, 0):
        side.append(take(a4, at - PITCH, wide, 512 + low_lane, 640 + low_lane))
        side.append(take(a4, at, wide, low_lane, low_lane + 128))
        side.append(take(a4, at, wide, 512 + low_lane, 640 + low_lane))
        side.append(take(a4, at + PITCH, wide, low_lane, low_lane + 128))
    side = dotn(jnp.concatenate(side, axis=1), k5s[...])
    side = jnp.where(low, roll(side, 1), roll(side, -1))[16 : 16 + size]
    side = side.reshape(ROWS, PITCH, 128)[:, 16:48, :].reshape(ROWS * COLS, 128).T
    field = jnp.concatenate(
        [own(a4, 512, 1024, -1), own(a4, 0, 1024), own(a4, 0, 512, 1)], axis=1
    )
    z = dott(k5[...], field) + five[:, 0:1]
    z = [z[0:64] + side[0:64], z[64:128], z[128:192], z[192:256] + side[64:128]]
    z = jnp.concatenate(
        [jnp.concatenate([z[q][:, g * 128 : (g + 1) * 128] for q in range(4)], axis=1) for g in range(4)],
        axis=0,
    )
    high = z.astype(BF)
    rest = (z - high.astype(F32)).astype(BF)
    z = dotn(jnp.concatenate([rest, high], axis=0), e_ref[...])
    z = z[0:256] + z[256:512]
    for g in range(4):
        for n in range(4):
            for p in range(4):
                fine_ref[16 * g + 4 * n + p] = z[
                    g * 64 + p * 16 : g * 64 + p * 16 + 16, n * 128 : (n + 1) * 128
                ]


def in_plane(extent, pos_ref, mask):
    row0 = pos_ref[0]
    col0 = pos_ref[1]
    m = lax.broadcasted_iota(jnp.int32, (PITCH, 128), 0)
    col = col0 + jnp.where(m < 8, m + 32, m - 16)
    col_ok = jnp.logical_and(col >= 0, col < extent[1])
    for k in range(CHUNKS):
        row = row0 + jnp.where(m < 8, k - 9, k - 8)
        ok = jnp.logical_and(col_ok, jnp.logical_and(row >= 0, row < extent[0]))
        mask[k * PITCH : (k + 1) * PITCH, :] = jnp.where(ok, 1.0, 0.0)


def forward(
    extent,
    pos_ref,
    window_ref,
    above_ref,
    below_ref,
    w1_hbm,
    w2_hbm,
    w3_hbm,
    w4_hbm,
    w5_hbm,
    b1_ref,
    b2_ref,
    b3_ref,
    b4_ref,
    mask,
    s5_ref,
    turn3_ref,
    turn4_ref,
    r5,
    r4,
    r3,
    r2,
    x0,
    x1,
    x2,
    x3,
    a3,
    a4,
    bias_ref,
    s0_ref,
    k1,
    k2,
    k3,
    k4,
    w1_ref,
    w2_ref,
    w3_ref,
    w4_ref,
    w5_ref,
    dx_ref,
    sems,
):
    copies = [
        pltpu.make_async_copy(src, dst, sems.at[n])
        for n, (src, dst) in enumerate(
            (
                (w1_hbm, w1_ref),
                (w2_hbm, w2_ref),
                (w3_hbm, w3_ref),
                (w4_hbm, w4_ref),
                (w5_hbm, w5_ref),
            )
        )
    ]
    for copy in copies:
        copy.start()
    small = (b1_ref, b2_ref, b3_ref, b4_ref)
    select(pos_ref[2], s0_ref, s5_ref, turn3_ref, turn4_ref)
    in_plane(extent, pos_ref, mask)
    low = low_half()
    clear_margins(((x0, 2, 30), (x1, 3, 30), (x2, 4, 29), (x3, 5, 29), (a4, 5, 29)))

    lane = lax.broadcasted_iota(jnp.int32, (1, 128), 1)
    dx_ref[0:2] = jnp.zeros((2, 16, 128), BF)
    dx_ref[8:24] = window_ref[...]
    dx_ref[30:32] = jnp.zeros((2, 16, 128), BF)
    for ref, at in ((above_ref, 2), (below_ref, 24)):
        sent = ref[FINE_HALO : FINE_HALO + HALO].reshape(HALO * 16, 128).astype(F32)
        sent = jnp.where(lane < 2 * COLS + 2 * HALO, lane_roll(sent, -2 * FINE_HALO), 0.0)
        dx_ref[at : at + HALO] = sent.astype(BF).reshape(HALO, 16, 128)

    def coarse_pair(n):
        lines = []
        for k in (2 * n, 2 * n + 1):
            before = dx_ref[pl.ds(k - 2, 3)].reshape(48, 128)
            here = dx_ref[pl.ds(k - 1, 3)].reshape(48, 128)
            lines += [jnp.concatenate([before, here], axis=1), jnp.zeros((80, 256), BF)]
        moved = dott(s0_ref[...], jnp.concatenate(lines, axis=0)).astype(BF)
        for half in range(2):
            at = pl.multiple_of((2 * n + half) * PITCH, 16)
            for s in range(3):
                x0[pl.ds(at, PITCH), s * 128 : (s + 1) * 128] = moved[
                    s * PITCH : (s + 1) * PITCH, half * 128 : (half + 1) * 128
                ]

    grouped(1, 15, GROUP0, coarse_pair)
    for copy in copies:
        copy.wait()
    perms = (turn3_ref[...].T, turn4_ref[...].T)
    small_terms(perms, small, bias_ref)
    arrange(
        perms,
        (w1_ref, w2_ref, w3_ref, w4_ref, w5_ref),
        (k1, k2, k3, k4),
        (r5, r4, r3, r2),
    )

    def narrow(read, weight, bias_at, variants):
        def work(start, size):
            wide = size + 32
            z = dotn(read(start - 16, wide), weight[...])
            z = jnp.tanh(z + bias_ref[8 * bias_at : 8 * bias_at + 1, 0:128])
            z = z * take(mask, start - 16, wide)
            inner = slice(16, 16 + size)
            left = jnp.where(low, roll(z, 1), z)
            put(variants, start, size, left[inner], 0, 128)
            put(variants, start, size, roll(z, -1)[inner], 128, 256)

        return work

    blocks(3, 27 // N1, N1, narrow(lambda at, n: take(x0, at, n), k1, 0, x1))
    blocks(4, 25 // N2, N2, narrow(lambda at, n: taps(x1, at, n), k2, 1, x2))

    def conv_three(start, size):
        wide = size + 32
        z = dotn(taps(x2, start - 16, wide), k3[...])
        z = jnp.tanh(z + bias_ref[16:17, 0:256])
        ok = take(mask, start - 16, wide)
        inner = slice(16, 16 + size)
        for p in range(2):
            half = z[:, p * 128 : (p + 1) * 128] * ok
            left = jnp.where(low, roll(half, 1), half)
            right = jnp.where(low, half, roll(half, -1))
            put(x3, start, size, left[inner], p * 256, p * 256 + 128)
            put(x3, start, size, right[inner], p * 256 + 128, p * 256 + 256)
            put(a3, start, size, half[inner], p * 128, p * 128 + 128)

    blocks(5, 24 // N3, N3, conv_three)

    def conv_four(start, size):
        ok = take(mask, start, size)
        for p in range(2):
            lines = []
            for r in range(3):
                phase, by = row_of(p + r - 1)
                lines.append(take(x3, start + by, size, phase * 256, phase * 256 + 256))
            z = dotn(jnp.concatenate(lines, axis=1), k4[...])
            z = jnp.tanh(z + bias_ref[24:25, 0:512])
            for q in range(4):
                at = p * 512 + q * 128
                put(a4, start, size, z[:, q * 128 : (q + 1) * 128] * ok, at, at + 128)

    blocks(5, 24 // N4, N4, conv_four)


def backward(
    scale,
    pos_ref,
    above_ref,
    below_ref,
    cot_ref,
    sides_ref,
    mask,
    s5_ref,
    r5,
    r4,
    r3,
    r2,
    x0,
    x1,
    x2,
    x3,
    a3,
    a4,
    keep_ref,
    send_ref,
    kept_hbm,
    c5,
    b4,
    b3,
    b2,
    b1,
    g_ref,
    center_ref,
    rim_ref,
    sem,
):
    kept = pltpu.make_async_copy(a4.at[pl.ds(NEAR, NEAR_CELLS)], kept_hbm, sem)
    kept.start()
    low = low_half()
    clear_margins(((c5, 5, 29), (b4, 5, 29), (b3, 6, 27), (b2, 7, 27)))

    n = FINE_HALO
    rows = 4 * ROWS
    lane = lax.broadcasted_iota(jnp.int32, (1, 128), 1)
    for ref, inside, parts in (
        (center_ref, cot_ref, slice(0, n)),
        (rim_ref, sides_ref, slice(n, 2 * n)),
    ):
        ref[0] = jnp.zeros((16, 128), BF)
        ref[1 : n + 1] = above_ref[parts]
        ref[n + 1 : n + 1 + rows] = inside[...]
        ref[n + 1 + rows : 2 * n + 1 + rows] = below_ref[parts]
        ref[2 * n + 1 + rows :] = jnp.zeros((9, 16, 128), BF)
    count = (2 * n + 10 + rows) * 16
    sides = rim_ref[...].reshape(count, 128).astype(F32)
    before = lane_roll(sides[: count - 64], 64 - n)
    corner = lane_roll(center_ref[...].reshape(count, 128).astype(F32)[: count - 64], 77)
    before = jnp.where(lane < 64 + n, before, corner)
    before = jnp.concatenate([jnp.zeros((64, 128), F32), before], axis=0)
    sides = jnp.where(lane < 2 * n, sides, jnp.where(lane < 64, 0.0, before))
    sides = jnp.where(lane < 65 + n, sides, 0.0)
    rim_ref[...] = sides.astype(BF).reshape(count // 16, 16, 128)

    def cot_pair(n):
        lines = []
        for k in (2 * n + 1, 2 * n + 2):
            at = pl.ds(4 * (k - 5), 6)
            here = jnp.concatenate(
                [center_ref[at].reshape(96, 128), rim_ref[at].reshape(96, 128)], axis=1
            )
            lines += [here, jnp.zeros((32, 256), BF)]
        moved = dott(s5_ref[...], jnp.concatenate(lines, axis=0)).astype(BF)
        for half in range(2):
            at = pl.multiple_of((2 * n + 1 + half) * PITCH, 16)
            for u in range(6):
                c5[pl.ds(at, PITCH), u * 128 : (u + 1) * 128] = moved[
                    u * PITCH : (u + 1) * PITCH, half * 128 : (half + 1) * 128
                ]

    grouped(2, 14, GROUP5, cot_pair)

    def back_four(start, size):
        ok = take(mask, start, size)
        for q in range(4):
            z = dott(take(c5, start, size, q * 128, q * 128 + 384), r5[...])
            for p in range(2):
                at = p * 512 + q * 128
                z_p = z[:, p * 128 : (p + 1) * 128] * ok
                put(b4, start, size, z_p * slope(take(a4, start, size, at, at + 128)), at, at + 128)

    blocks(5, 24 // M4, M4, back_four)

    def back_three(start, size):
        wide = size + 32
        ok = take(mask, start, size)
        inner = slice(16, 16 + size)
        for p in range(2):
            lines = []
            for t in range(3):
                phase, by = row_of(p + t - 1)
                lines.append(take(b4, start - 16 + by, wide, phase * 512, phase * 512 + 512))
            z = dott(jnp.concatenate(lines, axis=1), r4[...])
            moved = jnp.where(low, roll(z[:, 128:256], -1), roll(z[:, 128:256], 1))
            z = (z[:, 0:128] + moved)[inner] * ok
            at = p * 128
            put(b3, start, size, z * slope(take(a3, start, size, at, at + 128)), at, at + 128)

    blocks(6, 21 // M3, M3, back_three)

    def back_narrow(src, weight, act, out):
        def work(start, size):
            wide = size + 32
            z = dott(taps(src, start - 16, wide), weight[...])
            pair = jnp.where(low, roll(z[:, 0:128], -1), z[:, 0:128])
            z = pair + lane_roll(pair, 64) + roll(z[:, 128:256], 1)
            z = z[16 : 16 + size] * take(mask, start, size)
            z = jnp.where(low, 0.0, z * slope(take(act, start, size, 0, 128)))
            put(out, start, size, z, 0, 128)

        return work

    blocks(7, 20 // M2, M2, back_narrow(b3, r3, x2, b2))
    blocks(8, 18 // M1, M1, back_narrow(b2, r2, x1, b1))

    g_ref[1344:, :] = jnp.zeros((g_ref.shape[0] - 1344, 256), F32)
    g_ref[1152:1344, 192:256] = jnp.zeros((192, 64), F32)

    back = own(b4, 0, 1024)
    sums4 = jnp.sum(back.astype(F32), axis=0, keepdims=True)
    back = back.T
    for r in range(3):
        total = None
        for p in range(2):
            phase, by = row_of(p + r - 1)
            field = own(x3, phase * 256, phase * 256 + 256, by // PITCH)
            term = dotn(back[p * 512 : (p + 1) * 512, :], field)
            total = term if total is None else total + term
        total = total[0:256, 0:192] + total[256:512, 64:256]
        g_ref[r * 192 : (r + 1) * 192, :] = total.T * scale
    sums4 = sums4[:, 0:512] + sums4[:, 512:1024]
    sums4 = sums4[:, 0:256] + sums4[:, 256:512]

    back = own(b3, 0, 256)
    sums3 = jnp.sum(back.astype(F32), axis=0, keepdims=True)
    back = back.T
    for r in range(3):
        total = dotn(back, own(x2, 0, 256, r - 1))[:, 0:192]
        g_ref[576 + r * 192 : 576 + (r + 1) * 192, :] = total.T * scale

    back = own(b2, 0, 128)
    sums2 = jnp.sum(back.astype(F32), axis=0, keepdims=True)
    back = back.T
    for r in range(3):
        total = dotn(back[64:128, :], own(x1, 0, 256, r - 1))
        g_ref[1152:1344, r * 64 : (r + 1) * 64] = total[:, 0:192].T * scale

    back = own(b1, 0, 128)
    sums1 = jnp.sum(back.astype(F32), axis=0, keepdims=True)
    back = back.T
    total = dotn(back[64:128, :], own(x0, 0, 384)).T * scale
    for s in range(3):
        g_ref[1152 + s * 48 : 1152 + (s + 1) * 48, 192:256] = total[s * 128 : s * 128 + 48, :]

    cot = own(c5, 0, 768)
    sums5 = jnp.sum(cot.astype(F32), axis=0, keepdims=True)
    cot = cot.T
    total = None
    for q in range(4):
        field = jnp.concatenate(
            [own(a4, q * 128, q * 128 + 128), own(a4, 512 + q * 128, 640 + q * 128)], axis=1
        )
        term = dotn(cot[q * 128 : q * 128 + 384, :], field)
        total = term if total is None else total + term
    total = total * scale
    for r in range(3):
        for s in range(3):
            sum_p = None
            for p in range(4):
                at = (2 - s) * 128 + (p + 2 - r) * 16
                term = total[at : at + 16, p * 64 : (p + 1) * 64]
                sum_p = term if sum_p is None else sum_p + term
            g_ref[1344 + s * 16 : 1344 + (s + 1) * 16, r * 64 : (r + 1) * 64] = sum_p

    sums5 = sums5[:, 128:256] + sums5[:, 256:384] + sums5[:, 384:512] + sums5[:, 512:640]
    five = sums5
    for t in range(1, 4):
        five = five + lane_roll(sums5, -16 * t)
    biases = [
        sums4 * scale,
        sums3 * scale,
        jnp.concatenate([sums2, sums1], axis=1) * scale,
        jnp.concatenate([five, jnp.zeros((1, 128), F32)], axis=1) * scale,
    ]
    for n, value in enumerate(biases):
        high = value.astype(BF).astype(F32)
        g_ref[1392 + 2 * n : 1393 + 2 * n, :] = high
        g_ref[1393 + 2 * n : 1394 + 2 * n, :] = value - high

    half = g_ref.shape[0] // 2
    core = pos_ref[2]
    keep_ref[...] = g_ref[pl.ds(pl.multiple_of(core * half, 16), half), :]
    send_ref[...] = g_ref[pl.ds(pl.multiple_of((1 - core) * half, 16), half), :].astype(BF)
    kept.wait()


def finish(chans, places, pos_ref, mine_ref, other_ref, turn3_ref, turn4_ref, g1, g2, g3, g4, g5, c1, c2, c3, c4, c5, full):
    half = full.shape[0] // 2
    size = half // places
    core = pos_ref[2]
    for b in range(places):
        at = pl.multiple_of(lax.bitwise_xor(pos_ref[3], b) * size, 16)
        here = pl.multiple_of(core * half + b * size, 16)
        there = pl.multiple_of((1 - core) * half + b * size, 16)
        full[pl.ds(here, size), :] = mine_ref[pl.ds(at, size), :]
        full[pl.ds(there, size), :] = other_ref[pl.ds(at, size), :]
    g4[...] = dotn(full[0:576, :], turn4_ref[...])
    g3[...] = dotn(full[576:1152, :], turn3_ref[...])
    for r in range(3):
        g2[r * 192 : (r + 1) * 192, :] = full[1152:1344, r * 64 : (r + 1) * 64].astype(F32)
        for s in range(3):
            at = 1152 + s * 48 + r * 16
            g1[r, s] = full[at : at + 16, 192:256].astype(F32)[:chans]
            at = 1344 + s * 16
            g5[r, s] = full[at : at + 16, r * 64 : (r + 1) * 64].astype(F32)[:chans]
    terms = full[1392:1408, :]
    turned4 = dotn(terms, turn4_ref[...])
    turned3 = dotn(terms, turn3_ref[...])
    terms = terms.astype(F32)
    c4[...] = turned4[0:1] + turned4[1:2]
    c3[...] = turned3[2:3] + turned3[3:4]
    sums = [None, None, terms[4:5] + terms[5:6], terms[6:7] + terms[7:8]]
    c2[...] = sums[2][:, 64:128]
    c1[...] = sums[2][:, 192:256]
    c5[...] = sums[3][:, 16 : 16 + chans]


def exchange(axis, first, last):
    count = lax.axis_size(axis)
    odd = lax.axis_index(axis) % 2 == 1
    even_swap = [(i, i ^ 1) for i in range(count)]
    odd_swap = [(i, ((i + 1) ^ 1) - 1) for i in range(1, count - 1)]
    one = lax.ppermute(jnp.where(odd, first, last), axis, even_swap)
    two = lax.ppermute(jnp.where(odd, last, first), axis, odd_swap)
    return jnp.where(odd, one, two), jnp.where(odd, two, one)


def swap(block, axis, flip):
    return lax.ppermute(block, axis, [(i, i ^ flip) for i in range(lax.axis_size(axis))])


def chip_window(coarse, beside):
    gy, at = lax.axis_size("gy"), lax.axis_index("gy")
    chans, each, ny = coarse.shape
    cols = 2 * ny // gy
    block = jnp.pad(coarse.transpose(1, 0, 2), ((0, 0), (0, 16 - chans), (HALO, HALO)))
    other = swap(block, "gy", 1)
    block = jnp.where(
        at % 2 == 0, jnp.concatenate([block, other]), jnp.concatenate([other, block])
    )
    held = jnp.stack(
        [block[:, :, cols * c : cols * (c + 1) + 2 * HALO] for c in range(gy // 2)]
    )
    flip, bits = gy // 2, 0
    while flip > 1:
        half = held.shape[0] // 2
        high = (at & flip) != 0
        mine = jnp.where(high, held[half:], held[:half])
        other = swap(jnp.where(high, held[:half], held[half:]), "gy", flip)
        held = jnp.where(
            high,
            jnp.concatenate([other, mine], axis=1),
            jnp.concatenate([mine, other], axis=1),
        )
        flip, bits = flip // 2, bits + 1
        if bits == 1:
            held, beside = lax.optimization_barrier((held, beside))
    tail = (2 * each,) + held.shape[2:]
    held = held.reshape((2,) * bits + tail)
    held = held.transpose(tuple(reversed(range(bits))) + (bits, bits + 1, bits + 2))
    return held.reshape((gy * each,) + tail[1:]), beside


def halo_pieces(coarse, cotangent):
    n = FINE_HALO
    spare = 16 - coarse.shape[0]
    edges = (cotangent[:, :, :n].transpose(2, 0, 1), cotangent[:, :, -n:].transpose(2, 0, 1))
    got, edges = chip_window(coarse, edges)
    left, right = exchange("gy", *edges)
    wide = got.shape[2]
    cot = jnp.pad(cotangent.transpose(1, 0, 2), ((0, 0), (0, spare), (0, 0)))
    rim = jnp.concatenate([left.transpose(2, 1, 0), right.transpose(2, 1, 0)], axis=2)
    rim = jnp.pad(rim, ((0, 0), (0, spare), (0, 0)))

    def edge(cot_rows, coarse_rows):
        side = jnp.pad(got[coarse_rows], ((0, n - HALO), (0, 0), (0, 128 - 2 * n - wide)))
        side = jnp.concatenate([rim[cot_rows], side], axis=2)
        return jnp.concatenate([cot[cot_rows], side])

    first = edge(slice(0, n), slice(0, HALO))
    last = edge(slice(-n, None), slice(-HALO, None))
    above, below = exchange("gx", first, last)
    got = jnp.pad(got, ((0, 0), (0, 0), (0, 128 - wide)))
    return got, above, below, cot, jnp.pad(rim, ((0, 0), (0, 0), (0, 128 - 2 * n)))


def total_over_all(keep, send, beside, chans):
    gx, gy = lax.axis_size("gx"), lax.axis_size("gy")
    at_x = lax.axis_index("gx")

    def tree(terms):
        while len(terms) > 1:
            terms = [terms[n] + terms[n + 1] for n in range(0, len(terms), 2)]
        return terms[0]

    value = keep + swap(send, "gy", 1).astype(F32)
    size = value.shape[0] // gx

    def part(place):
        return lax.dynamic_slice_in_dim(value, place * size, size, 0)

    terms = [swap(part(at_x ^ d).astype(BF), "gx", d) for d in range(1, gx)]
    terms, beside = lax.optimization_barrier((terms, beside))
    beside = beside.transpose(1, 0, 2)[:chans]
    block = tree([part(at_x)] + [term.astype(F32) for term in terms])
    flip = 2
    while flip < gy:
        block = block.astype(BF)
        other = swap(block, "gy", flip)
        flip *= 2
        if flip == gy:
            other, beside = lax.optimization_barrier((other, beside))
        block = block.astype(F32) + other.astype(F32)
    block = block.astype(BF)
    mine = jnp.concatenate([block] + [swap(block, "gx", d) for d in range(1, gx)])
    return mine, swap(mine, "gy", 1), beside


def local(
    coarse,
    weight_one,
    weight_two,
    weight_three,
    weight_four,
    weight_five,
    bias_one,
    bias_two,
    bias_three,
    bias_four,
    bias_five,
    cotangent,
):
    gx, gy = lax.axis_size("gx"), lax.axis_size("gy")
    chans = coarse.shape[0]
    tile_rows = coarse.shape[1] * gy
    tile_cols = coarse.shape[2] // gy
    assert (tile_rows, tile_cols) == (ROWS, COLS)
    at_x, at_y = lax.axis_index("gx"), lax.axis_index("gy")
    pos = jnp.stack([at_x * ROWS, at_y * COLS, at_y % 2, at_x]).astype(jnp.int32)
    extent = (ROWS * gx, COLS * gy)
    scale = float((16 * extent[0] * extent[1]) ** -0.5)

    smem = pl.BlockSpec(memory_space=pltpu.SMEM)
    vmem = pl.BlockSpec(memory_space=pltpu.VMEM)
    params = pltpu.CompilerParams(vmem_limit_bytes=LIMIT * 1024 * 1024)

    def near(value):
        return pltpu.with_memory_space_constraint(value, pltpu.VMEM)

    def buf(width, kind=BF):
        return pltpu.VMEM((CELLS, width), kind)

    window, above, below, cot, rim = halo_pieces(coarse, cotangent)
    shared = (
        buf(128, F32),
        pltpu.VMEM((6 * PITCH, 256), BF),
        pltpu.VMEM((256, 256), BF),
        pltpu.VMEM((256, 256), BF),
        pltpu.VMEM((256, 384), BF),
        pltpu.VMEM((256, 1536), BF),
        pltpu.VMEM((256, 768), BF),
        pltpu.VMEM((256, 384), BF),
        buf(384),
        buf(256),
        buf(256),
        buf(512),
        buf(256),
        buf(1024),
    )
    hbm = pl.BlockSpec(memory_space=pltpu.HBM)
    weights = (
        weight_one,
        weight_two.reshape(576, 64),
        weight_three.reshape(576, 256),
        weight_four.reshape(576, 256),
        weight_five.transpose(0, 1, 3, 2),
    )
    half = -(-TERMS // (32 * gx)) * 16 * gx
    first_scratch = (
        [
            pltpu.VMEM((32, 512), F32),
            pltpu.VMEM((3 * PITCH, 256), BF),
            pltpu.VMEM((384, 128), BF),
            pltpu.VMEM((768, 128), BF),
            pltpu.VMEM((768, 256), BF),
            pltpu.VMEM((768, 512), BF),
        ]
        + [pltpu.VMEM(w.shape, BF) for w in weights]
        + [pltpu.VMEM((32, 16, 128), BF)]
        + [pltpu.SemaphoreType.DMA((5,))]
    )
    second_scratch = [
            buf(768),
            buf(1024),
            buf(256),
            buf(128),
            buf(128),
            pltpu.VMEM((2 * half, 256), F32),
            pltpu.VMEM((98, 16, 128), BF),
            pltpu.VMEM((98, 16, 128), BF),
            pltpu.SemaphoreType.DMA,
        ]

    def gradients(*refs):
        place, sent, weight_refs, tile = refs[:1], refs[1:4], refs[4:13], refs[13:15]
        results, turns = refs[15:18], refs[18:20]
        rest = refs[20:]
        fields = rest[:2] + turns + rest[2:12]
        first = rest[12 : 12 + len(first_scratch)]
        second = rest[12 + len(first_scratch) :]
        forward(extent, *place, *sent, *weight_refs, *fields, *first)
        backward(scale, *place, *sent[1:], *tile, *fields[:2], *fields[4:], *results, *second)

    keep, send, kept, turn3, turn4 = pl.pallas_call(
        gradients,
        out_shape=(
            pltpu.VMEM((half, 256), F32),
            pltpu.VMEM((half, 256), BF),
            pltpu.HBM((NEAR_CELLS, 1024), BF),
            shared[2],
            shared[3],
        ),
        in_specs=[smem] + [vmem] * 3 + [hbm] * 5 + [vmem] * 6,
        out_specs=(vmem, vmem, hbm, vmem, vmem),
        scratch_shapes=list(shared[:2] + shared[4:]) + first_scratch + second_scratch,
        compiler_params=pltpu.CompilerParams(vmem_limit_bytes=BIG * 1024 * 1024),
        name="gradients",
    )(
        pos,
        window,
        above,
        below,
        *[pltpu.with_memory_space_constraint(w, pltpu.HBM) for w in weights],
        bias_one.reshape(1, -1),
        bias_two.reshape(1, -1),
        bias_three.reshape(1, -1),
        bias_four.reshape(1, -1),
        cot,
        rim,
    )
    fine = pl.pallas_call(
        fine_field,
        out_shape=jax.ShapeDtypeStruct((4 * ROWS, 16, 4 * COLS), F32),
        in_specs=[hbm, vmem, vmem],
        out_specs=vmem,
        scratch_shapes=[
            pltpu.VMEM((512, 512), BF),
            pltpu.VMEM((256, 2048), BF),
            pltpu.VMEM((1024, 128), BF),
            buf(1024),
            pltpu.SemaphoreType.DMA,
        ],
        compiler_params=params,
        name="fine",
    )(pltpu.with_memory_space_constraint(kept, pltpu.HBM), weights[4], bias_five.reshape(1, -1))
    mine, other, fine = total_over_all(keep, send, fine, chans)

    def out(*shape):
        return jax.ShapeDtypeStruct(shape, F32)

    g1, g2, g3, g4, g5, c1, c2, c3, c4, c5 = pl.pallas_call(
        lambda *refs: finish(chans, gx, *refs),
        out_shape=(
            out(3, 3, chans, 64),
            out(576, 64),
            out(576, 256),
            out(576, 256),
            out(3, 3, chans, 64),
            out(1, 64),
            out(1, 64),
            out(1, 256),
            out(1, 256),
            out(1, chans),
        ),
        in_specs=[smem] + [vmem] * 4,
        out_specs=(vmem,) * 10,
        scratch_shapes=[pltpu.VMEM((2 * half, 256), BF)],
        compiler_params=params,
        name="finish",
    )(pos, mine, other, near(turn3), near(turn4))
    return (
        fine,
        g1,
        g2.reshape(3, 3, 64, 64),
        g3.reshape(3, 3, 64, 256),
        g4.reshape(3, 3, 64, 256),
        g5.transpose(0, 1, 3, 2),
        c1.reshape(64),
        c2.reshape(64),
        c3.reshape(256),
        c4.reshape(256),
        c5.reshape(chans),
    )


def solution(mesh):
    in_specs = (
        P(None, ("gx", "gy"), None),
        P(),
        P(),
        P(),
        P(),
        P(),
        P(),
        P(),
        P(),
        P(),
        P(),
        P(None, "gx", "gy"),
    )
    out_specs = (P(None, "gx", "gy"), P(), P(), P(), P(), P(), P(), P(), P(), P(), P())
    return jax.shard_map(local, mesh=mesh, in_specs=in_specs, out_specs=out_specs, check_vma=False)
```

```python
import jax
import jax.numpy as jnp
from jax import lax
from jax.experimental import pallas as pl
from jax.experimental.pallas import tpu as pltpu
from jax.sharding import PartitionSpec as P

BF = jnp.bfloat16
F32 = jnp.float32

ROWS, COLS, PITCH, CHUNKS = 16, 32, 48, 32
CELLS = PITCH * CHUNKS
OWN = PITCH * 8
NEAR = OWN - PITCH - 16
NEAR_CELLS = PITCH * (ROWS + 2) + 32
HALO = 6
FINE_HALO = 12
TERMS = 1400
GROUP0, GROUP5 = 7, 12
N1, N2, N3, N4 = 1, 1, 1, 1
M4, M3, M2, M1 = 1, 1, 1, 1
LIMIT = 12
BIG = 34


def dotn(left, right):
    return lax.dot_general(left, right, (((1,), (0,)), ((), ())), preferred_element_type=F32)


def dott(left, right):
    return lax.dot_general(left, right, (((1,), (1,)), ((), ())), preferred_element_type=F32)


def take(ref, start, count, low=0, high=None):
    high = ref.shape[1] if high is None else high
    if not isinstance(start, int):
        start = pl.multiple_of(start, 16)
    return ref[pl.ds(start, count), low:high]


def taps(ref, start, count):
    return jnp.concatenate([take(ref, start + d, count) for d in (-PITCH, 0, PITCH)], axis=1)


def own(ref, low, high, row=0):
    block = ref[OWN + PITCH * row : OWN + PITCH * (row + ROWS), low:high]
    return block.reshape(ROWS, PITCH, high - low)[:, 16:48, :].reshape(ROWS * COLS, high - low)


def roll(value, by):
    return pltpu.roll(value, by % value.shape[0], 0)


def lane_roll(value, by):
    return pltpu.roll(value, by % value.shape[1], 1)


def grouped(first, last, group, work):
    def step(n, _):
        for k in range(group):
            work(first + n * group + k)
        return 0

    lax.fori_loop(0, (last - first) // group, step, 0)


def blocks(first, chunks_each, count, work):
    size = chunks_each * PITCH
    if count == 1:
        work(first * PITCH, size)
        return

    def step(n, _):
        work(pl.multiple_of(first * PITCH + n * size, 16), size)
        return 0

    lax.fori_loop(0, count, step, 0)


def clear_margins(fields):
    for ref, first, last in fields:
        ref[0 : first * PITCH, :] = jnp.zeros((first * PITCH, ref.shape[1]), BF)
        if last < CHUNKS:
            ref[last * PITCH :, :] = jnp.zeros((CELLS - last * PITCH, ref.shape[1]), BF)


def put(ref, start, size, value, low, high):
    ref[pl.ds(start, size), low:high] = value.astype(BF)


def row_of(t):
    return t % 2, PITCH * (t // 2)


def low_half():
    return lax.broadcasted_iota(jnp.int32, (1, 128), 1) < 64


def slope(act):
    act = act.astype(F32)
    return 1.0 - act * act


def split_dot(value, perm):
    high = value.astype(BF)
    rest = value - high.astype(F32)
    middle = rest.astype(BF)
    low = (rest - middle.astype(F32)).astype(BF)
    return (dotn(low, perm) + dotn(middle, perm)) + dotn(high, perm)


def grid(rows, cols):
    return tuple(lax.broadcasted_iota(jnp.int32, (rows, cols), n) for n in (0, 1))


def one_hot(chosen):
    return jnp.where(chosen, 1.0, 0.0).astype(BF)


def select(core, s0_ref, s5_ref, turn3_ref, turn4_ref):
    m, lane = grid(PITCH, 256)
    for s in range(3):
        after = m + 31 + s + HALO + core * COLS
        here = m - 17 + s + HALO + core * COLS
        wanted = jnp.where(m < 8, after, jnp.where(here >= 0, here + 128, -1))
        s0_ref[s * PITCH : (s + 1) * PITCH, :] = one_hot(lane == wanted)
    for u in range(6):
        col = 4 * jnp.where(m < 8, m + 32, m - 16) + u - 1
        beyond = jnp.where(col - 128 < FINE_HALO, col + 64, -1)
        beyond = jnp.where(col == 127, 204, beyond)
        here = jnp.where(col < 0, col + 140, jnp.where(col < 128, col, col + 12))
        here = jnp.where(col < -FINE_HALO, -1, here)
        s5_ref[u * PITCH : (u + 1) * PITCH, :] = one_hot(lane == jnp.where(m < 8, beyond, here))
    new, old = grid(256, 256)
    turn3_ref[...] = one_hot(old == 4 * (new & 63) + 2 * (new >> 7) + 1 - ((new >> 6) & 1))
    turn4_ref[...] = one_hot(old == 4 * (new & 63) + 2 * ((new >> 6) & 1) + (new >> 7))


def small_terms(perms, small, bias_ref):
    b1_ref, b2_ref, b3_ref, b4_ref = small
    perm3, perm4 = perms

    def wide(value):
        return jnp.broadcast_to(value, (8, value.shape[1]))

    bias_ref[0:8, 0:128] = wide(jnp.concatenate([b1_ref[...]] * 2, axis=1))
    bias_ref[8:16, 0:128] = wide(jnp.concatenate([b2_ref[...]] * 2, axis=1))
    bias_ref[16:24, 0:256] = split_dot(wide(b3_ref[...]), perm3)
    four = split_dot(wide(b4_ref[...]), perm4)
    bias_ref[24:32, :] = jnp.concatenate([four, four], axis=1)


def arrange(perms, weights, there, back):
    w1_ref, w2_ref, w3_ref, w4_ref, w5_ref = weights
    k1, k2, k3, k4 = there
    r5, r4, r3, r2 = back
    perm3, perm4 = perms
    chans = w1_ref.shape[2]
    w3p = dotn(w3_ref[...], perm3).astype(BF)
    w4p = dotn(w4_ref[...], perm4).astype(BF)
    for ref in (k1, k2, k3, k4, r4, r3, r2):
        ref[...] = jnp.zeros(ref.shape, BF)
    for r in range(3):
        for s in range(3):
            at = s * 128 + r * 16
            k1[at : at + chans, :] = jnp.concatenate([w1_ref[r, s]] * 2, axis=1)
        part = w2_ref[r * 192 : (r + 1) * 192, :]
        k2[r * 256 : r * 256 + 192, :] = jnp.concatenate([part, part], axis=1)
        k3[r * 256 : r * 256 + 192, :] = w3p[r * 192 : (r + 1) * 192, :]
        for q in range(2):
            k4[r * 256 + q * 64 : r * 256 + q * 64 + 192, q * 256 : (q + 1) * 256] = w4p[
                r * 192 : (r + 1) * 192, :
            ]
        for s in range(3):
            t = 2 - r
            tap = (3 * r + s) * 64
            block = w3p[tap : tap + 64, :]
            r3[s * 64 : (s + 1) * 64, t * 256 : (t + 1) * 256] = block
            small = w2_ref[tap : tap + 64, :]
            r2[s * 64 : (s + 1) * 64, t * 128 + 64 : t * 128 + 128] = small
            if s == 2:
                r3[192:256, t * 256 : (t + 1) * 256] = block
                r2[192:256, t * 128 + 64 : t * 128 + 128] = small
            block = w4p[tap : tap + 64, :]
            for q in range(2):
                for q_src in range(2):
                    at = t * 512 + q_src * 256
                    if q - q_src + 1 == s:
                        r4[(1 - q) * 64 : (2 - q) * 64, at : at + 256] = block
                    if q_src == 1 - q and s == 2 - 2 * q:
                        r4[128 + (1 - q) * 64 : 128 + (2 - q) * 64, at : at + 256] = block
    columns = output_columns(w5_ref)
    for p in range(4):
        for v in range(3):
            r5[p * 64 : (p + 1) * 64, v * 128 : (v + 1) * 128] = lane_roll(
                columns[2 - v].T, 16 * p
            ).astype(BF)


def output_columns(w5_ref):
    gap_rows = jnp.zeros((16 - w5_ref.shape[2], 64), F32)
    columns = []
    for s in range(3):
        column = []
        for r in (2, 1, 0):
            column += [w5_ref[r, s].astype(F32), gap_rows]
        columns.append(jnp.concatenate(column + [jnp.zeros((80, 64), F32)], axis=0))
    return columns


def fine_field(kept_hbm, w5_ref, b5_ref, fine_ref, e_ref, k5, k5s, a4, sem):
    copy = pltpu.make_async_copy(kept_hbm, a4.at[pl.ds(NEAR, NEAR_CELLS)], sem)
    copy.start()
    low = low_half()
    cell, lane = grid(512, 512)
    e_ref[...] = one_hot(lane == ((cell >> 5) & 3) * 128 + (cell & 31) * 4 + (cell >> 7))
    k5[...] = jnp.zeros(k5.shape, BF)
    k5s[...] = jnp.zeros(k5s.shape, BF)
    columns = output_columns(w5_ref)
    w5 = [value.T for value in columns]
    columns = [value.astype(BF) for value in columns]
    empty = jnp.zeros((64, 64), BF)
    for t in range(6):
        at = 64 if t == 0 else (1536 if t == 5 else 512 + ((t - 1) // 2) * 512 + ((t - 1) % 2) * 64)
        side = 64 if t == 0 else (384 if t == 5 else 128 + ((t - 1) // 2) * 128 + ((t - 1) % 2) * 64)
        for b in range(3):
            p = t - 2 + b
            if not 0 <= p < 4:
                continue
            for src in range(4):
                for q in range(max(src - 1, 0), min(src + 1, 3) + 1):
                    k5[q * 64 + p * 16 : q * 64 + p * 16 + 16, at + src * 128 : at + src * 128 + 64] = (
                        columns[src - q + 1][b * 16 : b * 16 + 16, :]
                    )
        rows = [lane_roll(w5[s], 16 * (t - 2)).astype(BF)[:, :64] for s in (0, 2)]
        k5s[side : side + 64, :] = jnp.concatenate([rows[0], empty], axis=1)
        k5s[512 + side : 512 + side + 64, :] = jnp.concatenate([empty, rows[1]], axis=1)
    chans = b5_ref.shape[1]
    five = jnp.concatenate([b5_ref[...], jnp.zeros((1, 128 - chans), F32)], axis=1)
    five = sum(lane_roll(five, 16 * n) for n in range(8))
    five = jnp.concatenate([jnp.broadcast_to(five, (128, 128)).T] * 2, axis=0)
    copy.wait()
    size = ROWS * PITCH
    wide = size + 32
    at = OWN - 16
    side = []
    for low_lane in (384, 0):
        side.append(take(a4, at - PITCH, wide, 512 + low_lane, 640 + low_lane))
        side.append(take(a4, at, wide, low_lane, low_lane + 128))
        side.append(take(a4, at, wide, 512 + low_lane, 640 + low_lane))
        side.append(take(a4, at + PITCH, wide, low_lane, low_lane + 128))
    side = dotn(jnp.concatenate(side, axis=1), k5s[...])
    side = jnp.where(low, roll(side, 1), roll(side, -1))[16 : 16 + size]
    side = side.reshape(ROWS, PITCH, 128)[:, 16:48, :].reshape(ROWS * COLS, 128).T
    field = jnp.concatenate(
        [own(a4, 512, 1024, -1), own(a4, 0, 1024), own(a4, 0, 512, 1)], axis=1
    )
    z = dott(k5[...], field) + five[:, 0:1]
    z = [z[0:64] + side[0:64], z[64:128], z[128:192], z[192:256] + side[64:128]]
    z = jnp.concatenate(
        [jnp.concatenate([z[q][:, g * 128 : (g + 1) * 128] for q in range(4)], axis=1) for g in range(4)],
        axis=0,
    )
    high = z.astype(BF)
    rest = (z - high.astype(F32)).astype(BF)
    z = dotn(jnp.concatenate([rest, high], axis=0), e_ref[...])
    z = z[0:256] + z[256:512]
    for g in range(4):
        for n in range(4):
            for p in range(4):
                fine_ref[16 * g + 4 * n + p] = z[
                    g * 64 + p * 16 : g * 64 + p * 16 + 16, n * 128 : (n + 1) * 128
                ]


def in_plane(extent, pos_ref, mask):
    row0 = pos_ref[0]
    col0 = pos_ref[1]
    m = lax.broadcasted_iota(jnp.int32, (PITCH, 128), 0)
    col = col0 + jnp.where(m < 8, m + 32, m - 16)
    col_ok = jnp.logical_and(col >= 0, col < extent[1])
    for k in range(CHUNKS):
        row = row0 + jnp.where(m < 8, k - 9, k - 8)
        ok = jnp.logical_and(col_ok, jnp.logical_and(row >= 0, row < extent[0]))
        mask[k * PITCH : (k + 1) * PITCH, :] = jnp.where(ok, 1.0, 0.0)


def forward(
    extent,
    pos_ref,
    window_ref,
    above_ref,
    below_ref,
    w1_hbm,
    w2_hbm,
    w3_hbm,
    w4_hbm,
    w5_hbm,
    b1_ref,
    b2_ref,
    b3_ref,
    b4_ref,
    mask,
    s5_ref,
    turn3_ref,
    turn4_ref,
    r5,
    r4,
    r3,
    r2,
    x0,
    x1,
    x2,
    x3,
    a3,
    a4,
    bias_ref,
    s0_ref,
    k1,
    k2,
    k3,
    k4,
    w1_ref,
    w2_ref,
    w3_ref,
    w4_ref,
    w5_ref,
    dx_ref,
    sems,
):
    copies = [
        pltpu.make_async_copy(src, dst, sems.at[n])
        for n, (src, dst) in enumerate(
            (
                (w1_hbm, w1_ref),
                (w2_hbm, w2_ref),
                (w3_hbm, w3_ref),
                (w4_hbm, w4_ref),
                (w5_hbm, w5_ref),
            )
        )
    ]
    for copy in copies:
        copy.start()
    small = (b1_ref, b2_ref, b3_ref, b4_ref)
    select(pos_ref[2], s0_ref, s5_ref, turn3_ref, turn4_ref)
    in_plane(extent, pos_ref, mask)
    low = low_half()
    clear_margins(((x0, 2, 30), (x1, 3, 30), (x2, 4, 29), (x3, 5, 29), (a4, 5, 29)))

    lane = lax.broadcasted_iota(jnp.int32, (1, 128), 1)
    dx_ref[0:2] = jnp.zeros((2, 16, 128), BF)
    dx_ref[8:24] = window_ref[...]
    dx_ref[30:32] = jnp.zeros((2, 16, 128), BF)
    for ref, at in ((above_ref, 2), (below_ref, 24)):
        sent = ref[FINE_HALO : FINE_HALO + HALO].reshape(HALO * 16, 128).astype(F32)
        sent = jnp.where(lane < 2 * COLS + 2 * HALO, lane_roll(sent, -2 * FINE_HALO), 0.0)
        dx_ref[at : at + HALO] = sent.astype(BF).reshape(HALO, 16, 128)

    def coarse_pair(n):
        lines = []
        for k in (2 * n, 2 * n + 1):
            before = dx_ref[pl.ds(k - 2, 3)].reshape(48, 128)
            here = dx_ref[pl.ds(k - 1, 3)].reshape(48, 128)
            lines += [jnp.concatenate([before, here], axis=1), jnp.zeros((80, 256), BF)]
        moved = dott(s0_ref[...], jnp.concatenate(lines, axis=0)).astype(BF)
        for half in range(2):
            at = pl.multiple_of((2 * n + half) * PITCH, 16)
            for s in range(3):
                x0[pl.ds(at, PITCH), s * 128 : (s + 1) * 128] = moved[
                    s * PITCH : (s + 1) * PITCH, half * 128 : (half + 1) * 128
                ]

    grouped(1, 15, GROUP0, coarse_pair)
    for copy in copies:
        copy.wait()
    perms = (turn3_ref[...].T, turn4_ref[...].T)
    small_terms(perms, small, bias_ref)
    arrange(
        perms,
        (w1_ref, w2_ref, w3_ref, w4_ref, w5_ref),
        (k1, k2, k3, k4),
        (r5, r4, r3, r2),
    )

    def narrow(read, weight, bias_at, variants):
        def work(start, size):
            wide = size + 32
            z = dotn(read(start - 16, wide), weight[...])
            z = jnp.tanh(z + bias_ref[8 * bias_at : 8 * bias_at + 1, 0:128])
            z = z * take(mask, start - 16, wide)
            inner = slice(16, 16 + size)
            left = jnp.where(low, roll(z, 1), z)
            put(variants, start, size, left[inner], 0, 128)
            put(variants, start, size, roll(z, -1)[inner], 128, 256)

        return work

    blocks(3, 27 // N1, N1, narrow(lambda at, n: take(x0, at, n), k1, 0, x1))
    blocks(4, 25 // N2, N2, narrow(lambda at, n: taps(x1, at, n), k2, 1, x2))

    def conv_three(start, size):
        wide = size + 32
        z = dotn(taps(x2, start - 16, wide), k3[...])
        z = jnp.tanh(z + bias_ref[16:17, 0:256])
        ok = take(mask, start - 16, wide)
        inner = slice(16, 16 + size)
        for p in range(2):
            half = z[:, p * 128 : (p + 1) * 128] * ok
            left = jnp.where(low, roll(half, 1), half)
            right = jnp.where(low, half, roll(half, -1))
            put(x3, start, size, left[inner], p * 256, p * 256 + 128)
            put(x3, start, size, right[inner], p * 256 + 128, p * 256 + 256)
            put(a3, start, size, half[inner], p * 128, p * 128 + 128)

    blocks(5, 24 // N3, N3, conv_three)

    def conv_four(start, size):
        ok = take(mask, start, size)
        for p in range(2):
            lines = []
            for r in range(3):
                phase, by = row_of(p + r - 1)
                lines.append(take(x3, start + by, size, phase * 256, phase * 256 + 256))
            z = dotn(jnp.concatenate(lines, axis=1), k4[...])
            z = jnp.tanh(z + bias_ref[24:25, 0:512])
            for q in range(4):
                at = p * 512 + q * 128
                put(a4, start, size, z[:, q * 128 : (q + 1) * 128] * ok, at, at + 128)

    blocks(5, 24 // N4, N4, conv_four)


def backward(
    scale,
    pos_ref,
    above_ref,
    below_ref,
    cot_ref,
    sides_ref,
    mask,
    s5_ref,
    r5,
    r4,
    r3,
    r2,
    x0,
    x1,
    x2,
    x3,
    a3,
    a4,
    keep_ref,
    send_ref,
    kept_hbm,
    c5,
    b4,
    b3,
    b2,
    b1,
    g_ref,
    center_ref,
    rim_ref,
    sem,
):
    kept = pltpu.make_async_copy(a4.at[pl.ds(NEAR, NEAR_CELLS)], kept_hbm, sem)
    kept.start()
    low = low_half()
    clear_margins(((c5, 5, 29), (b4, 5, 29), (b3, 6, 27), (b2, 7, 27)))

    n = FINE_HALO
    rows = 4 * ROWS
    lane = lax.broadcasted_iota(jnp.int32, (1, 128), 1)
    for ref, inside, parts in (
        (center_ref, cot_ref, slice(0, n)),
        (rim_ref, sides_ref, slice(n, 2 * n)),
    ):
        ref[0] = jnp.zeros((16, 128), BF)
        ref[1 : n + 1] = above_ref[parts]
        ref[n + 1 : n + 1 + rows] = inside[...]
        ref[n + 1 + rows : 2 * n + 1 + rows] = below_ref[parts]
        ref[2 * n + 1 + rows :] = jnp.zeros((9, 16, 128), BF)
    count = (2 * n + 10 + rows) * 16
    sides = rim_ref[...].reshape(count, 128).astype(F32)
    before = lane_roll(sides[: count - 64], 64 - n)
    corner = lane_roll(center_ref[...].reshape(count, 128).astype(F32)[: count - 64], 77)
    before = jnp.where(lane < 64 + n, before, corner)
    before = jnp.concatenate([jnp.zeros((64, 128), F32), before], axis=0)
    sides = jnp.where(lane < 2 * n, sides, jnp.where(lane < 64, 0.0, before))
    sides = jnp.where(lane < 65 + n, sides, 0.0)
    rim_ref[...] = sides.astype(BF).reshape(count // 16, 16, 128)

    def cot_pair(n):
        lines = []
        for k in (2 * n + 1, 2 * n + 2):
            at = pl.ds(4 * (k - 5), 6)
            here = jnp.concatenate(
                [center_ref[at].reshape(96, 128), rim_ref[at].reshape(96, 128)], axis=1
            )
            lines += [here, jnp.zeros((32, 256), BF)]
        moved = dott(s5_ref[...], jnp.concatenate(lines, axis=0)).astype(BF)
        for half in range(2):
            at = pl.multiple_of((2 * n + 1 + half) * PITCH, 16)
            for u in range(6):
                c5[pl.ds(at, PITCH), u * 128 : (u + 1) * 128] = moved[
                    u * PITCH : (u + 1) * PITCH, half * 128 : (half + 1) * 128
                ]

    grouped(2, 14, GROUP5, cot_pair)

    def back_four(start, size):
        ok = take(mask, start, size)
        for q in range(4):
            z = dott(take(c5, start, size, q * 128, q * 128 + 384), r5[...])
            for p in range(2):
                at = p * 512 + q * 128
                z_p = z[:, p * 128 : (p + 1) * 128] * ok
                put(b4, start, size, z_p * slope(take(a4, start, size, at, at + 128)), at, at + 128)

    blocks(5, 24 // M4, M4, back_four)

    def back_three(start, size):
        wide = size + 32
        ok = take(mask, start, size)
        inner = slice(16, 16 + size)
        for p in range(2):
            lines = []
            for t in range(3):
                phase, by = row_of(p + t - 1)
                lines.append(take(b4, start - 16 + by, wide, phase * 512, phase * 512 + 512))
            z = dott(jnp.concatenate(lines, axis=1), r4[...])
            moved = jnp.where(low, roll(z[:, 128:256], -1), roll(z[:, 128:256], 1))
            z = (z[:, 0:128] + moved)[inner] * ok
            at = p * 128
            put(b3, start, size, z * slope(take(a3, start, size, at, at + 128)), at, at + 128)

    blocks(6, 21 // M3, M3, back_three)

    def back_narrow(src, weight, act, out):
        def work(start, size):
            wide = size + 32
            z = dott(taps(src, start - 16, wide), weight[...])
            pair = jnp.where(low, roll(z[:, 0:128], -1), z[:, 0:128])
            z = pair + lane_roll(pair, 64) + roll(z[:, 128:256], 1)
            z = z[16 : 16 + size] * take(mask, start, size)
            z = jnp.where(low, 0.0, z * slope(take(act, start, size, 0, 128)))
            put(out, start, size, z, 0, 128)

        return work

    blocks(7, 20 // M2, M2, back_narrow(b3, r3, x2, b2))
    blocks(8, 18 // M1, M1, back_narrow(b2, r2, x1, b1))

    g_ref[1344:, :] = jnp.zeros((g_ref.shape[0] - 1344, 256), F32)
    g_ref[1152:1344, 192:256] = jnp.zeros((192, 64), F32)

    back = own(b4, 0, 1024)
    sums4 = jnp.sum(back.astype(F32), axis=0, keepdims=True)
    back = back.T
    for r in range(3):
        total = None
        for p in range(2):
            phase, by = row_of(p + r - 1)
            field = own(x3, phase * 256, phase * 256 + 256, by // PITCH)
            term = dotn(back[p * 512 : (p + 1) * 512, :], field)
            total = term if total is None else total + term
        total = total[0:256, 0:192] + total[256:512, 64:256]
        g_ref[r * 192 : (r + 1) * 192, :] = total.T * scale
    sums4 = sums4[:, 0:512] + sums4[:, 512:1024]
    sums4 = sums4[:, 0:256] + sums4[:, 256:512]

    back = own(b3, 0, 256)
    sums3 = jnp.sum(back.astype(F32), axis=0, keepdims=True)
    back = back.T
    for r in range(3):
        total = dotn(back, own(x2, 0, 256, r - 1))[:, 0:192]
        g_ref[576 + r * 192 : 576 + (r + 1) * 192, :] = total.T * scale

    back = own(b2, 0, 128)
    sums2 = jnp.sum(back.astype(F32), axis=0, keepdims=True)
    back = back.T
    for r in range(3):
        total = dotn(back[64:128, :], own(x1, 0, 256, r - 1))
        g_ref[1152:1344, r * 64 : (r + 1) * 64] = total[:, 0:192].T * scale

    back = own(b1, 0, 128)
    sums1 = jnp.sum(back.astype(F32), axis=0, keepdims=True)
    back = back.T
    total = dotn(back[64:128, :], own(x0, 0, 384)).T * scale
    for s in range(3):
        g_ref[1152 + s * 48 : 1152 + (s + 1) * 48, 192:256] = total[s * 128 : s * 128 + 48, :]

    cot = own(c5, 0, 768)
    sums5 = jnp.sum(cot.astype(F32), axis=0, keepdims=True)
    cot = cot.T
    total = None
    for q in range(4):
        field = jnp.concatenate(
            [own(a4, q * 128, q * 128 + 128), own(a4, 512 + q * 128, 640 + q * 128)], axis=1
        )
        term = dotn(cot[q * 128 : q * 128 + 384, :], field)
        total = term if total is None else total + term
    total = total * scale
    for r in range(3):
        for s in range(3):
            sum_p = None
            for p in range(4):
                at = (2 - s) * 128 + (p + 2 - r) * 16
                term = total[at : at + 16, p * 64 : (p + 1) * 64]
                sum_p = term if sum_p is None else sum_p + term
            g_ref[1344 + s * 16 : 1344 + (s + 1) * 16, r * 64 : (r + 1) * 64] = sum_p

    sums5 = sums5[:, 128:256] + sums5[:, 256:384] + sums5[:, 384:512] + sums5[:, 512:640]
    five = sums5
    for t in range(1, 4):
        five = five + lane_roll(sums5, -16 * t)
    biases = [
        sums4 * scale,
        sums3 * scale,
        jnp.concatenate([sums2, sums1], axis=1) * scale,
        jnp.concatenate([five, jnp.zeros((1, 128), F32)], axis=1) * scale,
    ]
    for n, value in enumerate(biases):
        high = value.astype(BF).astype(F32)
        g_ref[1392 + 2 * n : 1393 + 2 * n, :] = high
        g_ref[1393 + 2 * n : 1394 + 2 * n, :] = value - high

    half = g_ref.shape[0] // 2
    core = pos_ref[2]
    keep_ref[...] = g_ref[pl.ds(pl.multiple_of(core * half, 16), half), :]
    send_ref[...] = g_ref[pl.ds(pl.multiple_of((1 - core) * half, 16), half), :].astype(BF)
    kept.wait()


def finish(chans, places, pos_ref, mine_ref, other_ref, turn3_ref, turn4_ref, g1, g2, g3, g4, g5, c1, c2, c3, c4, c5, full):
    half = full.shape[0] // 2
    size = half // places
    core = pos_ref[2]
    for b in range(places):
        at = pl.multiple_of(lax.bitwise_xor(pos_ref[3], b) * size, 16)
        here = pl.multiple_of(core * half + b * size, 16)
        there = pl.multiple_of((1 - core) * half + b * size, 16)
        full[pl.ds(here, size), :] = mine_ref[pl.ds(at, size), :]
        full[pl.ds(there, size), :] = other_ref[pl.ds(at, size), :]
    g4[...] = dotn(full[0:576, :], turn4_ref[...])
    g3[...] = dotn(full[576:1152, :], turn3_ref[...])
    for r in range(3):
        g2[r * 192 : (r + 1) * 192, :] = full[1152:1344, r * 64 : (r + 1) * 64].astype(F32)
        for s in range(3):
            at = 1152 + s * 48 + r * 16
            g1[r, s] = full[at : at + 16, 192:256].astype(F32)[:chans]
            at = 1344 + s * 16
            g5[r, s] = full[at : at + 16, r * 64 : (r + 1) * 64].astype(F32)[:chans]
    terms = full[1392:1408, :]
    turned4 = dotn(terms, turn4_ref[...])
    turned3 = dotn(terms, turn3_ref[...])
    terms = terms.astype(F32)
    c4[...] = turned4[0:1] + turned4[1:2]
    c3[...] = turned3[2:3] + turned3[3:4]
    sums = [None, None, terms[4:5] + terms[5:6], terms[6:7] + terms[7:8]]
    c2[...] = sums[2][:, 64:128]
    c1[...] = sums[2][:, 192:256]
    c5[...] = sums[3][:, 16 : 16 + chans]


def exchange(axis, first, last):
    count = lax.axis_size(axis)
    odd = lax.axis_index(axis) % 2 == 1
    even_swap = [(i, i ^ 1) for i in range(count)]
    odd_swap = [(i, ((i + 1) ^ 1) - 1) for i in range(1, count - 1)]
    one = lax.ppermute(jnp.where(odd, first, last), axis, even_swap)
    two = lax.ppermute(jnp.where(odd, last, first), axis, odd_swap)
    return jnp.where(odd, one, two), jnp.where(odd, two, one)


def swap(block, axis, flip):
    return lax.ppermute(block, axis, [(i, i ^ flip) for i in range(lax.axis_size(axis))])


def chip_window(coarse, beside):
    gy, at = lax.axis_size("gy"), lax.axis_index("gy")
    chans, each, ny = coarse.shape
    cols = 2 * ny // gy
    block = jnp.pad(coarse.transpose(1, 0, 2), ((0, 0), (0, 16 - chans), (HALO, HALO)))
    other = swap(block, "gy", 1)
    block = jnp.where(
        at % 2 == 0, jnp.concatenate([block, other]), jnp.concatenate([other, block])
    )
    held = jnp.stack(
        [block[:, :, cols * c : cols * (c + 1) + 2 * HALO] for c in range(gy // 2)]
    )
    flip, bits = gy // 2, 0
    while flip > 1:
        half = held.shape[0] // 2
        high = (at & flip) != 0
        mine = jnp.where(high, held[half:], held[:half])
        other = swap(jnp.where(high, held[:half], held[half:]), "gy", flip)
        held = jnp.where(
            high,
            jnp.concatenate([other, mine], axis=1),
            jnp.concatenate([mine, other], axis=1),
        )
        flip, bits = flip // 2, bits + 1
        if bits == 1:
            held, beside = lax.optimization_barrier((held, beside))
    tail = (2 * each,) + held.shape[2:]
    held = held.reshape((2,) * bits + tail)
    held = held.transpose(tuple(reversed(range(bits))) + (bits, bits + 1, bits + 2))
    return held.reshape((gy * each,) + tail[1:]), beside


def halo_pieces(coarse, cotangent):
    n = FINE_HALO
    spare = 16 - coarse.shape[0]
    edges = (cotangent[:, :, :n].transpose(2, 0, 1), cotangent[:, :, -n:].transpose(2, 0, 1))
    got, edges = chip_window(coarse, edges)
    left, right = exchange("gy", *edges)
    wide = got.shape[2]
    cot = jnp.pad(cotangent.transpose(1, 0, 2), ((0, 0), (0, spare), (0, 0)))
    rim = jnp.concatenate([left.transpose(2, 1, 0), right.transpose(2, 1, 0)], axis=2)
    rim = jnp.pad(rim, ((0, 0), (0, spare), (0, 0)))

    def edge(cot_rows, coarse_rows):
        side = jnp.pad(got[coarse_rows], ((0, n - HALO), (0, 0), (0, 128 - 2 * n - wide)))
        side = jnp.concatenate([rim[cot_rows], side], axis=2)
        return jnp.concatenate([cot[cot_rows], side])

    first = edge(slice(0, n), slice(0, HALO))
    last = edge(slice(-n, None), slice(-HALO, None))
    above, below = exchange("gx", first, last)
    got = jnp.pad(got, ((0, 0), (0, 0), (0, 128 - wide)))
    return got, above, below, cot, jnp.pad(rim, ((0, 0), (0, 0), (0, 128 - 2 * n)))


def total_over_all(keep, send, beside, chans):
    gx, gy = lax.axis_size("gx"), lax.axis_size("gy")
    at_x = lax.axis_index("gx")

    def tree(terms):
        while len(terms) > 1:
            terms = [terms[n] + terms[n + 1] for n in range(0, len(terms), 2)]
        return terms[0]

    value = keep + swap(send, "gy", 1).astype(F32)
    size = value.shape[0] // gx

    def part(place):
        return lax.dynamic_slice_in_dim(value, place * size, size, 0)

    terms = [swap(part(at_x ^ d).astype(BF), "gx", d) for d in range(gx - 1, 0, -1)][::-1]
    terms, beside = lax.optimization_barrier((terms, beside))
    beside = beside.transpose(1, 0, 2)[:chans]
    block = tree([part(at_x)] + [term.astype(F32) for term in terms])
    flip = 2
    while flip < gy:
        block = block.astype(BF)
        other = swap(block, "gy", flip)
        flip *= 2
        if flip == gy:
            other, beside = lax.optimization_barrier((other, beside))
        block = block.astype(F32) + other.astype(F32)
    block = block.astype(BF)
    mine = jnp.concatenate([block] + [swap(block, "gx", d) for d in range(1, gx)])
    return mine, swap(mine, "gy", 1), beside


def local(
    coarse,
    weight_one,
    weight_two,
    weight_three,
    weight_four,
    weight_five,
    bias_one,
    bias_two,
    bias_three,
    bias_four,
    bias_five,
    cotangent,
):
    gx, gy = lax.axis_size("gx"), lax.axis_size("gy")
    chans = coarse.shape[0]
    tile_rows = coarse.shape[1] * gy
    tile_cols = coarse.shape[2] // gy
    assert (tile_rows, tile_cols) == (ROWS, COLS)
    at_x, at_y = lax.axis_index("gx"), lax.axis_index("gy")
    pos = jnp.stack([at_x * ROWS, at_y * COLS, at_y % 2, at_x]).astype(jnp.int32)
    extent = (ROWS * gx, COLS * gy)
    scale = float((16 * extent[0] * extent[1]) ** -0.5)

    smem = pl.BlockSpec(memory_space=pltpu.SMEM)
    vmem = pl.BlockSpec(memory_space=pltpu.VMEM)
    params = pltpu.CompilerParams(vmem_limit_bytes=LIMIT * 1024 * 1024)

    def near(value):
        return pltpu.with_memory_space_constraint(value, pltpu.VMEM)

    def buf(width, kind=BF):
        return pltpu.VMEM((CELLS, width), kind)

    window, above, below, cot, rim = halo_pieces(coarse, cotangent)
    shared = (
        buf(128, F32),
        pltpu.VMEM((6 * PITCH, 256), BF),
        pltpu.VMEM((256, 256), BF),
        pltpu.VMEM((256, 256), BF),
        pltpu.VMEM((256, 384), BF),
        pltpu.VMEM((256, 1536), BF),
        pltpu.VMEM((256, 768), BF),
        pltpu.VMEM((256, 384), BF),
        buf(384),
        buf(256),
        buf(256),
        buf(512),
        buf(256),
        buf(1024),
    )
    hbm = pl.BlockSpec(memory_space=pltpu.HBM)
    weights = (
        weight_one,
        weight_two.reshape(576, 64),
        weight_three.reshape(576, 256),
        weight_four.reshape(576, 256),
        weight_five.transpose(0, 1, 3, 2),
    )
    half = -(-TERMS // (32 * gx)) * 16 * gx
    first_scratch = (
        [
            pltpu.VMEM((32, 512), F32),
            pltpu.VMEM((3 * PITCH, 256), BF),
            pltpu.VMEM((384, 128), BF),
            pltpu.VMEM((768, 128), BF),
            pltpu.VMEM((768, 256), BF),
            pltpu.VMEM((768, 512), BF),
        ]
        + [pltpu.VMEM(w.shape, BF) for w in weights]
        + [pltpu.VMEM((32, 16, 128), BF)]
        + [pltpu.SemaphoreType.DMA((5,))]
    )
    second_scratch = [
            buf(768),
            buf(1024),
            buf(256),
            buf(128),
            buf(128),
            pltpu.VMEM((2 * half, 256), F32),
            pltpu.VMEM((98, 16, 128), BF),
            pltpu.VMEM((98, 16, 128), BF),
            pltpu.SemaphoreType.DMA,
        ]

    def gradients(*refs):
        place, sent, weight_refs, tile = refs[:1], refs[1:4], refs[4:13], refs[13:15]
        results, turns = refs[15:18], refs[18:20]
        rest = refs[20:]
        fields = rest[:2] + turns + rest[2:12]
        first = rest[12 : 12 + len(first_scratch)]
        second = rest[12 + len(first_scratch) :]
        forward(extent, *place, *sent, *weight_refs, *fields, *first)
        backward(scale, *place, *sent[1:], *tile, *fields[:2], *fields[4:], *results, *second)

    keep, send, kept, turn3, turn4 = pl.pallas_call(
        gradients,
        out_shape=(
            pltpu.VMEM((half, 256), F32),
            pltpu.VMEM((half, 256), BF),
            pltpu.HBM((NEAR_CELLS, 1024), BF),
            shared[2],
            shared[3],
        ),
        in_specs=[smem] + [vmem] * 3 + [hbm] * 5 + [vmem] * 6,
        out_specs=(vmem, vmem, hbm, vmem, vmem),
        scratch_shapes=list(shared[:2] + shared[4:]) + first_scratch + second_scratch,
        compiler_params=pltpu.CompilerParams(vmem_limit_bytes=BIG * 1024 * 1024),
        name="gradients",
    )(
        pos,
        window,
        above,
        below,
        *[pltpu.with_memory_space_constraint(w, pltpu.HBM) for w in weights],
        bias_one.reshape(1, -1),
        bias_two.reshape(1, -1),
        bias_three.reshape(1, -1),
        bias_four.reshape(1, -1),
        cot,
        rim,
    )
    fine = pl.pallas_call(
        fine_field,
        out_shape=jax.ShapeDtypeStruct((4 * ROWS, 16, 4 * COLS), F32),
        in_specs=[hbm, vmem, vmem],
        out_specs=vmem,
        scratch_shapes=[
            pltpu.VMEM((512, 512), BF),
            pltpu.VMEM((256, 2048), BF),
            pltpu.VMEM((1024, 128), BF),
            buf(1024),
            pltpu.SemaphoreType.DMA,
        ],
        compiler_params=params,
        name="fine",
    )(pltpu.with_memory_space_constraint(kept, pltpu.HBM), weights[4], bias_five.reshape(1, -1))
    mine, other, fine = total_over_all(keep, send, fine, chans)

    def out(*shape):
        return jax.ShapeDtypeStruct(shape, F32)

    g1, g2, g3, g4, g5, c1, c2, c3, c4, c5 = pl.pallas_call(
        lambda *refs: finish(chans, gx, *refs),
        out_shape=(
            out(3, 3, chans, 64),
            out(576, 64),
            out(576, 256),
            out(576, 256),
            out(3, 3, chans, 64),
            out(1, 64),
            out(1, 64),
            out(1, 256),
            out(1, 256),
            out(1, chans),
        ),
        in_specs=[smem] + [vmem] * 4,
        out_specs=(vmem,) * 10,
        scratch_shapes=[pltpu.VMEM((2 * half, 256), BF)],
        compiler_params=params,
        name="finish",
    )(pos, mine, other, near(turn3), near(turn4))
    return (
        fine,
        g1,
        g2.reshape(3, 3, 64, 64),
        g3.reshape(3, 3, 64, 256),
        g4.reshape(3, 3, 64, 256),
        g5.transpose(0, 1, 3, 2),
        c1.reshape(64),
        c2.reshape(64),
        c3.reshape(256),
        c4.reshape(256),
        c5.reshape(chans),
    )


def solution(mesh):
    in_specs = (
        P(None, ("gx", "gy"), None),
        P(),
        P(),
        P(),
        P(),
        P(),
        P(),
        P(),
        P(),
        P(),
        P(),
        P(None, "gx", "gy"),
    )
    out_specs = (P(None, "gx", "gy"), P(), P(), P(), P(), P(), P(), P(), P(), P(), P())
    return jax.shard_map(local, mesh=mesh, in_specs=in_specs, out_specs=out_specs, check_vma=False)
```
